32 devices in a mesh: group: 2 (over x), dom: 16 (over z, y, core).
Axes of the slice: x: 2, y: 2, z: 4, core: 2. Of those that a mesh axis runs over, the one named last changes fastest.
Arguments:
- fields: float32 [6, 35, 32768], P(None, None, ('group', 'dom')), may hold values from -6 to 6
- metric: float32 [9, 32768], P(None, ('group', 'dom')), may hold values from -3 to 3
- face_scale: float32 [4, 32768], P(None, ('group', 'dom')), may hold values from 0.5 to 10
- face_angles: float32 [2, 4, 32768], P(None, None, ('group', 'dom')), may hold values from -3.140625 to 3.140625
- neighbours: int32 [4, 32768], P(None, ('group', 'dom')), may hold values from -1 to 4479, as said below
- send_dom: int32 [2, 4096], P(None, ('group', 'dom')), may hold values from 0 to 4095, as said below
- send_partner: int32 [4096], P(('group', 'dom')), may hold values from 0 to 4095, as said below
- element_kind: int32 [32768], P(('group', 'dom')), may hold values from 0 to 6, as said below
- derivative: float32 [3, 35, 35], replicated, may hold values from -1 to 1
- lifting: float32 [35, 60], replicated, may hold values from -0.75 to 0.75
- block_inverse: bfloat16 [6, 210, 210], replicated
Outputs:
- advanced: float32 [6, 35, 32768], P(None, None, ('group', 'dom'))
The draws below stay inside these ranges and needn't reach their ends.
Inputs may be any that keep to these rules, and one draw needn't show every extreme that they name: `send_dom`: values are local face ids f * 1024 + e. Row 0 lists exactly the faces of the device whose neighbours slots are 4096 + i for i < 128, in the order of i; row 1 those with 4224 + i, in the order of i. `send_partner`: values are local face ids; exactly the faces of the device whose neighbours slot is 4352 + i, in the order of i. `neighbours`: on each device: every slot from 4096 up is read by exactly one face; 128 faces hold -1; every other face holds the id of another face of the same device, and that face holds its id. `element_kind`: elements of kind 1 or more (the fine region) lie exactly on the devices with group index 1 and dom index at least half of the dom axis; all elements of those devices have kind 1 or more, all others kind 0.
All inputs are finite; a program needn't handle non-finite values.
Results may differ from the reference program's by a relative error of at most 0.0003.
Values sent between devices are 32-bit elements; how exact they have to be, the bound alone decides.
A program may use at most 64 MiB of HBM per device.

```python
import jax
import jax.numpy as jnp
import numpy as np
from jax import lax

NC = 6
NP = 35
NFP = 15
KTYPES = 6
SWEEPS = 4
EL = 1024
NB = 128
NG = 128
NWALL = 128
TOTAL = 32768
N_GROUP = 2
N_DOM = 16


def face_plan(key):
    devices = N_GROUP * N_DOM
    face_total = 4 * EL

    def one_device(device_key):
        shuffled = jax.random.permutation(device_key, face_total).astype(jnp.int32)
        halo_faces = shuffled[:2 * NB]
        group_faces = shuffled[2 * NB:2 * NB + NG]
        wall_faces = shuffled[2 * NB + NG:2 * NB + NG + NWALL]
        paired = shuffled[2 * NB + NG + NWALL:].reshape(-1, 2)
        listed = jnp.zeros((face_total,), jnp.int32)
        listed = listed.at[halo_faces].set(face_total + jnp.arange(2 * NB, dtype=jnp.int32))
        listed = listed.at[group_faces].set(face_total + 2 * NB + jnp.arange(NG, dtype=jnp.int32))
        listed = listed.at[wall_faces].set(-1)
        listed = listed.at[paired[:, 0]].set(paired[:, 1])
        listed = listed.at[paired[:, 1]].set(paired[:, 0])
        return (listed, halo_faces.reshape(2, NB), group_faces)
    device_keys = jax.random.split(key, devices)
    return jax.vmap(one_device)(device_keys)


def draw_neighbours(key, part):
    listed = face_plan(jax.random.fold_in(key, 11))[0]
    devices = listed.shape[0]
    return jnp.transpose(listed.reshape(devices, 4, EL), (1, 0, 2)).reshape(4, devices * EL).astype(jnp.int32)


def draw_send_dom(key, part):
    halo_lists = face_plan(jax.random.fold_in(key, 11))[1]
    return jnp.transpose(halo_lists, (1, 0, 2)).reshape(2, -1).astype(jnp.int32)


def draw_send_partner(key, part):
    group_lists = face_plan(jax.random.fold_in(key, 11))[2]
    return group_lists.reshape(-1).astype(jnp.int32)


def draw_element_kind(key, part):
    devices = N_GROUP * N_DOM
    owner = jnp.arange(devices * EL, dtype=jnp.int32) // EL
    fine_region = (owner >= N_DOM) & (owner % N_DOM >= N_DOM // 2)
    shapes = jax.random.randint(key, (devices * EL,), 1, KTYPES + 1, dtype=jnp.int32)
    return jnp.where(fine_region, shapes, 0).astype(jnp.int32)


def draw_face_scale(key, part):
    devices = N_GROUP * N_DOM
    owner = jnp.arange(devices * EL, dtype=jnp.int32) // EL
    fine_region = (owner >= N_DOM) & (owner % N_DOM >= N_DOM // 2)
    low_end = jnp.where(fine_region, 2.5, 0.5).astype(jnp.float32)[None, :]
    unit = jax.random.uniform(jax.random.fold_in(key, 23), (4, devices * EL), jnp.float32, 0.0, 1.0)
    values = low_end * jnp.exp(unit * jnp.log(4.0))
    return jnp.clip(values, 0.5, 10.0).astype(jnp.float32)


def draw_block_inverse(key, part):
    order_n = NC * NP
    diag_key, off_key = jax.random.split(key)
    diagonal = jax.random.uniform(diag_key, (KTYPES, order_n), jnp.float32, 0.6, 1.0)
    spread = jax.random.normal(off_key, (KTYPES, order_n, order_n), jnp.float32) * 0.02
    identity = jnp.eye(order_n, dtype=jnp.float32)
    return (spread * (1.0 - identity) + identity * diagonal[:, :, None]).astype(jnp.bfloat16)


def block_scale(own_key, extent, shards, low, top_value):
    factor_of = 1.0
    for dim, blocks in shards:
        draws = jax.random.uniform(jax.random.fold_in(jax.random.fold_in(own_key, 6), dim), (blocks,), jnp.float32, low / len(shards), top_value / len(shards))
        factor_of = factor_of * jnp.repeat(jnp.exp(draws), extent[dim] // blocks).reshape((-1,) + (1,) * (len(extent) - 1 - dim))
    return factor_of


def bell_draw(own_key, dims, width, reach, shards=(), held_as=jnp.bfloat16):
    values = width * jax.random.normal(own_key, dims, jnp.float32)
    if shards:
        values = values * block_scale(own_key, dims, shards, -0.22, 0.18)
    return jnp.clip(values, -reach, reach).astype(held_as)


def setup_inputs(seed: int = 0) -> dict:
    keys = jax.random.split(jax.random.key(seed), 12)
    fields = bell_draw(keys[0], (NC, NP, TOTAL), 1.0, 6.0, ((2, 32),), jnp.float32)
    metric = bell_draw(keys[1], (9, TOTAL), 0.5, 3.0, ((1, 32),), jnp.float32)
    face_scale = draw_face_scale(jax.random.fold_in(keys[11], 71), 0)
    face_angles = jnp.clip(jax.random.uniform(keys[3], (2, 4, TOTAL), jnp.float32, -3.140625, 3.140625), -3.140625, 3.140625)
    neighbours = draw_neighbours(jax.random.fold_in(keys[11], 71), 0)
    send_dom = draw_send_dom(jax.random.fold_in(keys[11], 71), 0)
    send_partner = draw_send_partner(jax.random.fold_in(keys[11], 71), 0)
    element_kind = draw_element_kind(jax.random.fold_in(keys[11], 71), 0)
    derivative = bell_draw(keys[8], (3, NP, NP), NP ** -0.5, 1.0, (), jnp.float32)
    lifting = bell_draw(keys[9], (NP, 4 * NFP), (4 * NFP) ** -0.5, 0.75, (), jnp.float32)
    block_inverse = draw_block_inverse(jax.random.fold_in(keys[11], 71), 0)
    return {"fields": fields, "metric": metric, "face_scale": face_scale, "face_angles": face_angles, "neighbours": neighbours, "send_dom": send_dom, "send_partner": send_partner, "element_kind": element_kind, "derivative": derivative, "lifting": lifting, "block_inverse": block_inverse}


step_size = 0.2
highest = lax.Precision.HIGHEST


def face_nodes():
    lattice = []
    for along_r in range(5):
        for along_s in range(5 - along_r):
            for along_t in range(5 - along_r - along_s):
                lattice.append((along_r, along_s, along_t))
    checks = [lambda point: point[2] == 0, lambda point: point[1] == 0, lambda point: point[0] == 0, lambda point: point[0] + point[1] + point[2] == 4]
    chosen = []
    for check_of in checks:
        chosen.extend([position for position, point in enumerate(lattice) if check_of(point)])
    return np.array(chosen, dtype=np.int32)


def normals_of(face_angles):
    polar = face_angles[0]
    azimuth = face_angles[1]
    return jnp.stack([jnp.sin(polar) * jnp.cos(azimuth), jnp.sin(polar) * jnp.sin(azimuth), jnp.cos(polar)])


def trace_block(state_now):
    picked = state_now[:, face_nodes(), :]
    return picked.reshape(state_now.shape[0], 4, -1, state_now.shape[2])


def pool_of(traces):
    return jnp.transpose(traces, (0, 2, 1, 3)).reshape(traces.shape[0] * traces.shape[2], -1)


def exterior(trace_pool, neighbours, traces):
    flat_list = neighbours.reshape(-1)
    gathered = jnp.take(trace_pool, jnp.maximum(flat_list, 0), axis=1)
    gathered = gathered.reshape(traces.shape[0], traces.shape[2], traces.shape[1], traces.shape[3])
    gathered = jnp.transpose(gathered, (0, 2, 1, 3))
    mirror_sign = jnp.array([-1.0, -1.0, -1.0, 1.0, 1.0, 1.0], jnp.float32)
    mirrored = traces * mirror_sign[:, None, None, None]
    walled = (neighbours < 0)[None, :, None, :]
    return jnp.where(walled, mirrored, gathered)


def cross_product(left_vec, right_vec):
    return jnp.stack([left_vec[1] * right_vec[2] - left_vec[2] * right_vec[1],
                      left_vec[2] * right_vec[0] - left_vec[0] * right_vec[2],
                      left_vec[0] * right_vec[1] - left_vec[1] * right_vec[0]])


def surface(traces, normals, face_scale, lifting):
    electric = traces[:3]
    magnetic = traces[3:]
    normal_b = normals[:, :, None, :]
    along_e = jnp.sum(normal_b * electric, axis=0)
    along_h = jnp.sum(normal_b * magnetic, axis=0)
    flux_e = -cross_product(normal_b, magnetic) + along_e * normal_b - electric
    flux_h = cross_product(normal_b, electric) + along_h * normal_b - magnetic
    fluxes = jnp.concatenate([flux_e, flux_h]) * (0.5 * face_scale)[None, :, None, :]
    fluxes = fluxes.reshape(fluxes.shape[0], -1, fluxes.shape[3])
    return jnp.einsum("ij,cje->cie", lifting, fluxes, precision=highest, preferred_element_type=jnp.float32)


def volume(state_now, metric, derivative):
    grads = jnp.einsum("bij,cje->bcie", derivative, state_now, precision=highest, preferred_element_type=jnp.float32)

    def along(component, axis_no):
        return (metric[3 * axis_no] * grads[0, component] + metric[3 * axis_no + 1] * grads[1, component]
                + metric[3 * axis_no + 2] * grads[2, component])

    curl_h = jnp.stack([along(5, 1) - along(4, 2), along(3, 2) - along(5, 0), along(4, 0) - along(3, 1)])
    curl_e = jnp.stack([along(2, 1) - along(1, 2), along(0, 2) - along(2, 0), along(1, 0) - along(0, 1)])
    return jnp.concatenate([curl_h, -curl_e])


def apply_inverse(right_side, kinds, block_inverse):
    flattened = right_side.reshape(-1, right_side.shape[2])
    summed = jnp.zeros_like(flattened)
    for shape_no in range(block_inverse.shape[0]):
        matrix = block_inverse[shape_no].astype(jnp.float32)
        product = jnp.dot(matrix, flattened, precision=highest, preferred_element_type=jnp.float32)
        summed = summed + jnp.where(kinds == shape_no + 1, product, 0.0)
    return summed.reshape(right_side.shape)


def reference(fields, metric, face_scale, face_angles, neighbours, send_dom, send_partner, element_kind, derivative, lifting, block_inverse):
    devices = N_GROUP * N_DOM
    trace_rows = NC * NFP

    def blocks(array):
        leading = array.shape[:-1]
        return jnp.moveaxis(array.reshape(leading + (devices, EL)), -2, 0)

    field_b = blocks(fields)
    metric_b = blocks(metric)
    scale_b = blocks(face_scale)
    angle_b = blocks(face_angles)
    nbr_b = blocks(neighbours)
    kind_b = blocks(element_kind)
    dom_b = jnp.moveaxis(send_dom.reshape(2, devices, NB), 1, 0)
    part_b = send_partner.reshape(devices, NG)

    def outgoing(inputs):
        state_now, dom_list, part_list = inputs
        trace_pool = pool_of(trace_block(state_now))
        return jnp.take(trace_pool, dom_list.reshape(-1), axis=1), jnp.take(trace_pool, part_list, axis=1)

    def arrivals(current):
        dom_out, part_out = lax.map(outgoing, (current, dom_b, part_b))
        dom_out = dom_out.reshape(N_GROUP, N_DOM, trace_rows, 2 * NB)
        empty = jnp.zeros((N_GROUP, 1, trace_rows, NB), dom_out.dtype)
        from_prev = jnp.concatenate([empty, dom_out[:, :-1, :, NB:]], axis=1)
        from_next = jnp.concatenate([dom_out[:, 1:, :, :NB], empty], axis=1)
        partner = jnp.flip(part_out.reshape(N_GROUP, N_DOM, trace_rows, NG), axis=0)
        joined = jnp.concatenate([from_prev, from_next, partner], axis=3)
        return joined.reshape(devices, trace_rows, 2 * NB + NG)

    def explicit_step(inputs):
        state_now, arrived, metric_d, scale_d, angle_d, nbr_d = inputs
        normals = normals_of(angle_d)
        traces = trace_block(state_now)
        whole_pool = jnp.concatenate([pool_of(traces), arrived], axis=1)
        outside = exterior(whole_pool, nbr_d, traces)
        return state_now + step_size * (volume(state_now, metric_d, derivative) + surface(traces, normals, scale_d, lifting)
                                        - surface(outside, normals, scale_d, lifting))

    def sweep_step(inputs):
        state_now, current, arrived, scale_d, angle_d, nbr_d, kind_d = inputs
        normals = normals_of(angle_d)
        traces = trace_block(current)
        whole_pool = jnp.concatenate([pool_of(traces), arrived], axis=1)
        outside = exterior(whole_pool, nbr_d, traces)
        right_side = state_now - step_size * surface(outside, normals, scale_d, lifting)

        def solve_branch(operands):
            return apply_inverse(operands[0], operands[1], block_inverse)

        def empty_branch(operands):
            return jnp.zeros_like(operands[0])

        solved = lax.cond(jnp.any(kind_d > 0), solve_branch, empty_branch, (right_side, kind_d))
        return jnp.where(kind_d > 0, solved, state_now)

    arrived = arrivals(field_b)
    explicit = lax.map(explicit_step, (field_b, arrived, metric_b, scale_b, angle_b, nbr_b))
    current = field_b
    for sweep_no in range(SWEEPS):
        if sweep_no > 0:
            arrived = arrivals(current)
        current = lax.map(sweep_step, (field_b, current, arrived, scale_b, angle_b, nbr_b, kind_b))
    final = jnp.where(kind_b[:, None, None, :] > 0, current, explicit)
    return jnp.moveaxis(final, 0, -2).reshape(NC, NP, devices * EL)
```

```python
import functools

import jax
import jax.numpy as jnp
import numpy as np
from jax import lax
from jax.experimental import pallas as pl
from jax.experimental.pallas import tpu as pltpu
from jax.sharding import PartitionSpec as P

SWEEPS = 4
STEP = 0.2
NC, NP, NFP = 6, 35, 15
RP = 40
HB = NC * RP
KB = 256
FP = 16
TR = NC * 4 * FP
TILE = 256
SUB = 128
MSG = NC * FP + 8
f32, bf16, i32 = jnp.float32, jnp.bfloat16, jnp.int32


def face_nodes():
    lattice = [(r, s, t) for r in range(5) for s in range(5 - r) for t in range(5 - r - s)]
    tests = [
        lambda p: p[2] == 0,
        lambda p: p[1] == 0,
        lambda p: p[0] == 0,
        lambda p: sum(p) == 4,
    ]
    return [[i for i, p in enumerate(lattice) if test(p)] for test in tests]


def constants(el, kinds):
    trace = np.zeros((4 * FP, NP), np.float32)
    for f, nodes in enumerate(face_nodes()):
        for n, node in enumerate(nodes):
            trace[f * FP + n, node] = 1
    eye6 = np.eye(NC, dtype=np.float32)
    pad = np.eye(RP, NP, dtype=np.float32)
    trace6 = np.kron(eye6, trace)
    rows6 = np.kron(eye6, pad)
    cols6 = np.zeros((NC * NP, KB), np.float32)
    cols6[:, :HB] = rows6.T
    tracep = np.tile(trace6 @ cols6, (1, 2))
    spread = np.zeros((2, NP, 3 * RP), np.float32)
    for i in range(NP):
        spread[0, i, i] = spread[0, i, RP + i] = spread[1, i, 2 * RP + i] = 1
    lift_spread = np.zeros((4, 4 * NFP, 16 * FP), np.float32)
    for f in range(4):
        for n in range(NFP):
            row, col = f * NFP + n, f * FP + n
            for i in range(2):
                lift_spread[2 * i, row, 8 * FP * i + col] = 1
                lift_spread[2 * i, row, 8 * FP * i + 4 * FP + col] = 1
                lift_spread[2 * i + 1, row, 8 * FP * i + col] = 1
    upper = np.concatenate([np.triu(np.ones((SUB, SUB)), 1), np.ones((SUB, SUB))], axis=1)
    lines = (kinds + 1) * (el // SUB)
    lower = np.tril(np.ones((lines, lines)), -1)
    small = [jnp.asarray(a, bf16) for a in (upper, lower, spread, lift_spread)]
    large = [jnp.asarray(a, bf16) for a in (tracep, trace6, rows6, cols6)]
    return small, large


def split(x):
    hi = x.astype(bf16)
    return hi, (x - hi.astype(f32)).astype(bf16)


def dot(a, b):
    return jnp.dot(a, b, preferred_element_type=f32)


def stacked(x):
    hi, lo = split(x)
    gap = jnp.zeros((KB - HB, x.shape[1]), bf16)
    return jnp.concatenate([hi, gap, lo, gap], axis=0)


def project(at, n):
    sa, ca, sb, cb = n
    e_t = ca * (cb * at[0] + sb * at[1]) - sa * at[2]
    e_p = cb * at[1] - sb * at[0]
    h_t = ca * (cb * at[3] + sb * at[4]) - sa * at[5]
    h_p = cb * at[4] - sb * at[3]
    return jnp.concatenate([h_p - e_t, -h_t - e_p], axis=0)


def lanes(x, index):
    return jnp.take_along_axis(x, jnp.broadcast_to(index, x.shape), axis=1)


def kernel(
    el, kinds, scale, angles, nb, send_dom, send_part, kind, deriv, lift,
    upper, lower, spread, lift_spread,
    fields_h, metric_h, binv_h, tracep_h, trace6_h, rows6_h, cols6_h,
    out,
    fraw, metric, binv, tracep, trace6, rows6, cols6,
    fpad, own, xs, ohs, lnorm, slots, sgn, kindrow, offs, lsl, pm, sel, pooln, pool, recvn, coef,
    d3, l2, trs, ext, base, rem, remn, wt, wf, rhs, zs, pq0, grads,
    send0, recv0, sendk, recvk, off, walk,
    in_sem, ssem0, rsem0, ssemk, rsemk,
):
    grp, dom = lax.axis_index("group"), lax.axis_index("dom")
    count = lax.axis_size("dom")
    half = count // 2
    fine = jnp.logical_and(grp == 1, dom >= half)
    coarse = jnp.logical_not(fine)
    nt = el // TILE
    shift = el.bit_length() - 1
    lines = el // SUB
    steps = nt - 1 + kinds - 1
    has_prev, has_next = dom > 0, dom < count - 1
    fine_prev = jnp.logical_and(fine, dom > half)
    fine_next = jnp.logical_and(fine, has_next)

    loads = [
        pltpu.make_async_copy(a, b, in_sem.at[i])
        for i, (a, b) in enumerate((
            (fields_h, fraw), (tracep_h, tracep), (cols6_h, cols6), (binv_h, binv),
            (trace6_h, trace6), (rows6_h, rows6), (metric_h, metric),
        ))
    ]
    for load in loads:
        load.start()

    barrier = pltpu.get_barrier_semaphore()

    @pl.when(has_prev)
    def _():
        pl.semaphore_signal(barrier, inc=1, device_id={"dom": dom - 1})

    @pl.when(has_next)
    def _():
        pl.semaphore_signal(barrier, inc=1, device_id={"dom": dom + 1})

    pl.semaphore_signal(barrier, inc=1, device_id={"group": 1 - grp})

    targets = ({"dom": dom - 1}, {"dom": dom + 1}, {"group": 1 - grp})
    lands = (1, 0, 2)
    first = [
        pltpu.make_async_remote_copy(
            src_ref=send0.at[i], dst_ref=recv0.at[lands[i]],
            send_sem=ssem0.at[i], recv_sem=rsem0.at[lands[i]], device_id=targets[i],
        )
        for i in range(3)
    ]

    def later(no):
        return [
            pltpu.make_async_remote_copy(
                src_ref=sendk.at[no - 1, i], dst_ref=recvk.at[no - 1, lands[i]],
                send_sem=ssemk.at[no - 1, i], recv_sem=rsemk.at[no - 1, lands[i]],
                device_id=targets[i],
            )
            for i in range(2)
        ]

    polar, azimuth = angles[0], angles[1]
    parts = (jnp.sin(polar), jnp.cos(polar), jnp.sin(azimuth), jnp.cos(azimuth))
    own[...] = jnp.zeros_like(own)
    for f in range(4):
        for i in range(4):
            own[f * 8 + i : f * 8 + i + 1, :] = parts[i][f : f + 1, :]
        own[f * 8 + 4 : f * 8 + 5, :] = 0.5 * scale[f : f + 1, :]
    lists = jnp.concatenate([send_dom[0:1, :], send_dom[1:2, :], send_part[...]], axis=1)
    down = lax.broadcasted_iota(i32, (el, 3 * SUB), 0)
    ohs[...] = jnp.where(down == (lists & (el - 1)), 1.0, 0.0).astype(bf16)
    xs[2 * HB : 2 * HB + 32, :], xs[2 * HB + 32 : 2 * HB + 64, :] = split(own[...])

    loads[0].wait()
    for c in range(NC):
        fpad[c * RP + 32 : (c + 1) * RP, :] = jnp.zeros((8, el), f32)
        fpad[c * RP : c * RP + NP, :] = fraw[c]
    xs[0:HB, :], xs[HB : 2 * HB, :] = split(fpad[...])
    loads[1].wait()
    y = dot(xs[...], ohs[...])
    at_list = y[2 * HB : 2 * HB + 32] + y[2 * HB + 32 : 2 * HB + 64]
    face = lists >> shift
    mine = at_list[0:8]
    for f in range(1, 4):
        mine = jnp.where(face == f, at_list[f * 8 : (f + 1) * 8], mine)
    lnorm[...] = mine
    t = dot(tracep[...], stacked(y[0:HB] + y[HB : 2 * HB]))
    for c in range(NC):
        v = t[c * 4 * FP : c * 4 * FP + FP]
        for f in range(1, 4):
            v = jnp.where(face == f, t[(c * 4 + f) * FP : (c * 4 + f + 1) * FP], v)
        for i in range(3):
            send0[i, c * FP : (c + 1) * FP, :] = v[:, i * SUB : (i + 1) * SUB]
    for i in range(3):
        send0[i, NC * FP : MSG, :] = mine[:, i * SUB : (i + 1) * SUB]

    pl.semaphore_wait(barrier, 1 + has_prev.astype(i32) + has_next.astype(i32))

    @pl.when(has_prev)
    def _():
        first[0].start()

    @pl.when(has_next)
    def _():
        first[1].start()

    first[2].start()

    @pl.when(coarse)
    def _():
        for f in range(4):
            row = nb[f : f + 1, :]
            lane = lax.broadcasted_iota(i32, (1, el), 1)
            slots[f : f + 1, :] = jnp.where(row < 0, lane + f * el, row)
            sgn[f : f + 1, :] = jnp.where(row < 0, -1.0, 1.0)

    @pl.when(fine)
    def _():
        def square(row):
            return jnp.concatenate([row[:, i * SUB : (i + 1) * SUB] for i in range(lines)], axis=0)

        def line(sq):
            return jnp.concatenate([sq[i : i + 1] for i in range(lines)], axis=1)

        faces = [square(nb[f : f + 1, :]) for f in range(4)]
        which = square(kind[...])
        edge = functools.reduce(
            jnp.logical_or,
            [jnp.logical_and(n >= 4 * el, n < 4 * el + 2 * SUB) for n in faces],
        )
        group = jnp.where(edge, 0, which)
        masks = jnp.concatenate(
            [jnp.where(group == k, 1.0, 0.0) for k in range(kinds + 1)], axis=0
        )
        pre = dot(masks.astype(bf16), upper[...])
        before = dot(lower[...], pre[:, SUB:].astype(bf16))
        ranks = masks * (pre[:, :SUB] + before)
        pos = sum(ranks[k * lines : (k + 1) * lines] for k in range(kinds + 1))
        offs[...] = before.astype(i32)
        for k in range(kinds):
            off[k] = offs[(k + 1) * lines, 0]
        off[kinds] = jnp.int32(el)
        t, k = jnp.int32(1), jnp.int32(1)
        seen = [jnp.int32(-1)] * nt
        for s in range(steps):
            lo, hi = off[k - 1], off[k]
            walk[0, s] = t
            walk[1, s] = k - 1
            walk[2, s] = lo - t * TILE
            walk[3, s] = hi - t * TILE
            seen = [n + jnp.where(t <= i, 1, 0) for i, n in enumerate(seen)]
            stay = jnp.logical_and(hi <= (t + 1) * TILE, k < kinds)
            k, t = jnp.where(stay, k + 1, k), jnp.where(stay, t, jnp.minimum(t + 1, nt - 1))
        for i in range(nt):
            walk[4, i] = jnp.clip(seen[i], 0, steps - 1)

        def lookup(e):
            lane, row = e & (SUB - 1), e >> (SUB.bit_length() - 1)
            res = jnp.zeros((lines, SUB), f32)
            for r in range(lines):
                table = jnp.broadcast_to(pos[r : r + 1], (lines, SUB))
                res = jnp.where(row == r, jnp.take_along_axis(table, lane, axis=1), res)
            return res.astype(i32)

        place = pos.astype(i32)
        for f in range(4):
            n = faces[f]
            inner = (n >> shift) * el + lookup(n & (el - 1))
            m = jnp.where(n < 0, f * el + place, jnp.where(n >= 4 * el, n, inner))
            flag = 2 * which + jnp.where(n < 0, 1, 0)
            for i, v in enumerate((m >> 6, m & 63, flag)):
                own[f * 8 + 5 + i : f * 8 + 6 + i, :] = line(v.astype(f32))
        mine = jnp.concatenate([send_dom[...]] * (lines // 2), axis=0)
        lsl[...] = (mine >> shift) * TILE + lookup(mine & (el - 1))

        row = line(place)
        for i in range(nt):
            down = lax.broadcasted_iota(i32, (TILE, el), 0) + i * TILE
            pm[i * TILE : (i + 1) * TILE, :] = jnp.where(down == row, 1.0, 0.0).astype(bf16)
        xs[2 * HB : 2 * HB + 32, :], xs[2 * HB + 32 : 2 * HB + 64, :] = split(own[...])
        y = lax.dot_general(
            xs[...], pm[...], (((1,), (1,)), ((), ())), preferred_element_type=f32
        )
        fpad[...] = y[0:HB] + y[HB : 2 * HB]
        own[...] = y[2 * HB : 2 * HB + 32] + y[2 * HB + 32 : 2 * HB + 64]
        for f in range(4):
            at = f * 8 + 5
            slots[f : f + 1, :] = (own[at : at + 1, :] * 64 + own[at + 1 : at + 2, :]).astype(i32)
            flag = own[at + 2 : at + 3, :].astype(i32)
            sgn[f : f + 1, :] = jnp.where((flag & 1) == 1, -1.0, 1.0)
            if f == 0:
                kindrow[...] = flag >> 1

    def pick(y, f, rows, total):
        which = slots[f : f + 1, :] >> (TILE.bit_length() - 1)
        for h in range(4 * nt):
            total = jnp.where(which == h, y[h * rows : (h + 1) * rows], total)
        return total

    def gather(source, rows, dest, under=None):
        for f in range(4):
            s = sel[:, f * el : (f + 1) * el]
            y = dot(source[...], jnp.concatenate([s, s], axis=0))
            dest[f] = pick(y, f, rows, jnp.zeros((rows, el), f32) if under is None else under[f])

    def place_at(dest, source, f, j, sources):
        s = slots[f : f + 1, j * SUB : (j + 1) * SUB]
        v = dest[f, :, j * SUB : (j + 1) * SUB]
        for i in sources:
            here = (s >> (SUB.bit_length() - 1)) == 4 * el // SUB + i
            v = jnp.where(here, lanes(source[i], s & (SUB - 1)), v)
        dest[f, :, j * SUB : (j + 1) * SUB] = v

    def fill(t, at_rows):
        cols = slice(t * TILE, (t + 1) * TILE)
        for f in range(4):
            at = [at_rows(c * 4 * FP + f * FP) for c in range(NC)]
            sign = sgn[f : f + 1, cols]
            at[:3] = [sign * e for e in at[:3]]
            pq = project(at, [recvn[f, i : i + 1, cols] for i in range(4)])
            hi, lo = split(pq)
            h = f * nt + t
            pool[h * 2 * FP : (h + 1) * 2 * FP, 0:TILE] = hi
            pool[h * 2 * FP : (h + 1) * 2 * FP, TILE : 2 * TILE] = lo
            if t == 0:
                pq0[f] = pq

    down = lax.broadcasted_iota(i32, (TILE, el), 0)
    for f in range(4):
        low = slots[f : f + 1, :] & (TILE - 1)
        sel[:, f * el : (f + 1) * el] = jnp.where(down == low, 1.0, 0.0).astype(bf16)
    for f in range(4):
        for t in range(0, nt, 2):
            both = [own[f * 8 : f * 8 + 8, (t + i) * TILE : (t + i + 1) * TILE] for i in range(2)]
            h = (f * nt + t) * 8
            pooln[h : h + 16, 0:TILE], pooln[h : h + 16, TILE : 2 * TILE] = split(
                jnp.concatenate(both, axis=0)
            )
        sa, ca, sb, cb, w = (own[f * 8 + i : f * 8 + i + 1, :] for i in range(5))
        for i, row in enumerate((w * ca * cb, w * ca * sb, -w * sa, -w * sb, w * cb)):
            coef[f, i : i + 1, :] = row
    gather(pooln, 8, recvn)
    for t in range(nt):
        z = dot(tracep[...], stacked(fpad[:, t * TILE : (t + 1) * TILE]))
        trs[t] = z
        fill(t, lambda r: z[r : r + FP])
    gather(pool, 2 * FP, ext)

    l2[...] = jnp.zeros_like(l2)
    hi, lo = split(lift[...])
    for i in range(4):
        l2[i * RP : i * RP + NP, :] = dot(lo if i % 2 else hi, lift_spread[i])
    for load in loads[2:]:
        load.wait()

    @pl.when(fine)
    def _():
        for k in range(kinds):
            b2 = dot(binv[k], cols6[...]).astype(bf16)
            a = dot(trace6[...], b2).astype(bf16)
            b = dot(rows6[...], b2).astype(bf16)
            for i in range(2):
                wt[k, :, i * KB : (i + 1) * KB] = a
                wf[k, :, i * KB : (i + 1) * KB] = b

    @pl.when(coarse)
    def _():
        d3[...] = jnp.zeros_like(d3)
        for b in range(3):
            hi, lo = split(deriv[b])
            d3[b * RP : b * RP + NP, :] = dot(hi, spread[0]) + dot(lo, spread[1])
        db = d3[...].astype(bf16)
        for c in range(NC):
            x = fpad[c * RP : (c + 1) * RP, :]
            hi = x.astype(bf16).astype(f32)
            grads[c] = dot(db, jnp.concatenate([hi, x - hi, hi], axis=0).astype(bf16))

    def arrive(i):
        at = [recv0[i, c * FP : (c + 1) * FP, :] for c in range(NC)]
        rem[i] = project(at, [lnorm[r : r + 1, i * SUB : (i + 1) * SUB] for r in range(4)])
        remn[i] = recv0[i, NC * FP : MSG, :]

    rem[...] = jnp.zeros_like(rem)
    remn[...] = jnp.zeros_like(remn)

    @pl.when(has_prev)
    def _():
        first[0].wait_send()
        first[1].wait_recv()
        arrive(0)

    @pl.when(has_next)
    def _():
        first[1].wait_send()
        first[0].wait_recv()
        arrive(1)

    first[2].wait()
    arrive(2)

    def lifted(t, pq):
        cols = slice(t * TILE, (t + 1) * TILE)
        for pair in range(NC // 2):
            pieces = []
            for c in (2 * pair, 2 * pair + 1):
                rows = []
                k = c % 3
                for f in range(4):
                    p, q = pq[f][:FP], pq[f][FP:]
                    a, b = (p, q) if c < 3 else (q, -p)
                    row = coef[f, k : k + 1, cols] * a
                    if k < 2:
                        row = row + coef[f, 3 + k : 4 + k, cols] * b
                    rows.append(row)
                pieces.extend(split(jnp.concatenate(rows, axis=0)))
            y = dot(l2[...].astype(bf16), jnp.concatenate(pieces, axis=0))
            for i in range(2):
                at = 2 * i * RP
                yield 2 * pair + i, y[at : at + RP] + y[at + RP : at + 2 * RP]

    @pl.when(coarse)
    def _():
        for f in range(4):
            for j in range(lines):
                place_at(ext, rem, f, j, range(3))
        for t in range(nt):
            cols = slice(t * TILE, (t + 1) * TILE)

            def along(c, axis):
                return sum(
                    metric[3 * axis + b : 3 * axis + b + 1, cols]
                    * grads[c, b * RP : (b + 1) * RP, cols]
                    for b in range(3)
                )

            pq = []
            for f in range(4):
                at = [trs[t, (c * 4 + f) * FP : (c * 4 + f + 1) * FP, :] for c in range(NC)]
                n = [own[f * 8 + i : f * 8 + i + 1, cols] for i in range(4)]
                pq.append(project(at, n) - ext[f, :, cols])
            for c, s in lifted(t, pq):
                k, other = c % 3, 3 - 3 * (c // 3)
                one, two = (k + 1) % 3, (k + 2) % 3
                curl = along(other + two, one) - along(other + one, two)
                vol = curl if c < 3 else -curl
                value = fpad[c * RP : (c + 1) * RP, cols] + STEP * (vol + s)
                out[c, :, cols] = value[:NP]

    @pl.when(fine)
    def _():
        for f in range(4):
            for j in range(lines):
                edge = j < TILE // SUB
                place_at(ext, rem, f, j, range(3) if edge else (2,))
                if edge:
                    place_at(recvn, remn, f, j, range(2))
            base[f] = jnp.where(slots[f : f + 1, :] >= 4 * el, ext[f], 0.0)

        def right_side(t):
            cols = slice(t * TILE, (t + 1) * TILE)
            terms = [
                fpad[c * RP : (c + 1) * RP, cols] - STEP * s
                for c, s in lifted(t, [ext[f, :, cols] for f in range(4)])
            ]
            rhs[t] = stacked(jnp.concatenate(terms, axis=0))

        def edge_blocks(weights, rows):
            z = dot(weights[0], rhs[0])
            for k in range(1, kinds):
                z = jnp.where(kindrow[:, 0:TILE] == k + 1, dot(weights[k], rhs[0]), z)
            zs[0, 0:rows, :] = z

        def inside(row, at, size):
            return jnp.clip(walk[row, at], 0, size - 1)

        def inner_blocks(weights, rows):
            lane = lax.broadcasted_iota(i32, (1, TILE), 1)
            for s in range(steps):
                y = dot(weights[inside(1, s, kinds)], rhs[inside(0, s, nt)])
                if s:
                    here = jnp.logical_and(lane >= walk[2, s], lane < walk[3, s])
                    y = jnp.where(here, y, zs[s, 0:rows, :])
                zs[1 + s, 0:rows, :] = y

        def sweep(no, carry):
            right_side(0)
            edge_blocks(wt, TR)
            fill(0, lambda r: zs[0, r : r + FP, :])
            for i in range(2):
                at = lsl[i : i + 1, :]
                v = jnp.zeros((2 * FP, SUB), f32)
                for h in range(4 * TILE // SUB):
                    f, j = h // (TILE // SUB), h % (TILE // SUB)
                    x = lanes(pq0[f, :, j * SUB : (j + 1) * SUB], at & (SUB - 1))
                    v = jnp.where((at >> (SUB.bit_length() - 1)) == h, x, v)
                sendk[no - 1, i] = v
            copies = later(no)

            @pl.when(fine_prev)
            def _():
                copies[0].start()

            @pl.when(fine_next)
            def _():
                copies[1].start()

            for t in range(1, nt):
                right_side(t)
            inner_blocks(wt, TR)
            for t in range(1, nt):
                last = inside(4, t, steps)
                fill(t, lambda r: zs[1 + last, r : r + FP, :])
            gather(pool, 2 * FP, ext, base)

            @pl.when(fine_prev)
            def _():
                copies[0].wait_send()
                copies[1].wait_recv()
                rem[0] = recvk[no - 1, 0]

            @pl.when(fine_next)
            def _():
                copies[1].wait_send()
                copies[0].wait_recv()
                rem[1] = recvk[no - 1, 1]

            for f in range(4):
                for j in range(TILE // SUB):
                    place_at(ext, rem, f, j, range(2))
            return carry

        lax.fori_loop(1, SWEEPS, sweep, 0)
        for t in range(nt):
            right_side(t)
        edge_blocks(wf, HB)
        inner_blocks(wf, HB)
        for t in range(nt):
            at = 1 + inside(4, t, steps) if t else 0
            cols = slice(t * TILE, (t + 1) * TILE)
            xs[0:HB, cols], xs[HB : 2 * HB, cols] = split(zs[at, 0:HB, :])
        y = dot(xs[0 : 2 * HB, :], pm[...])
        for c in range(NC):
            at = c * RP
            out[c] = y[at : at + NP] + y[HB + at : HB + at + NP]


def shards(*args):
    (fields, metric, scale, angles, nb, send_dom, send_part, kind, deriv, lift, binv) = args
    el = fields.shape[2]
    kinds = binv.shape[0]
    nt, lines = el // TILE, el // SUB
    steps = nt - 1 + kinds - 1
    small, large = constants(el, kinds)
    near = [
        scale, angles, nb, send_dom, send_part.reshape(1, -1), kind.reshape(1, -1), deriv, lift,
        *small,
    ]
    far = [fields, metric, binv, *large]
    vmem, dma = pltpu.VMEM, pltpu.SemaphoreType.DMA
    return pl.pallas_call(
        functools.partial(kernel, el, kinds),
        out_shape=jax.ShapeDtypeStruct(fields.shape, f32),
        in_specs=[pl.BlockSpec(memory_space=vmem)] * len(near)
        + [pl.BlockSpec(memory_space=pl.ANY)] * len(far),
        out_specs=pl.BlockSpec(memory_space=vmem),
        scratch_shapes=[
            *[vmem(a.shape, a.dtype) for a in far],
            vmem((HB, el), f32),
            vmem((32, el), f32),
            vmem((2 * HB + 64, el), bf16),
            vmem((el, 3 * SUB), bf16),
            vmem((8, 3 * SUB), f32),
            vmem((4, el), i32),
            vmem((4, el), f32),
            vmem((1, el), i32),
            vmem(((kinds + 1) * lines, SUB), i32),
            vmem((lines, SUB), i32),
            vmem((el, el), bf16),
            vmem((TILE, 4 * el), bf16),
            vmem((4 * nt * 8, 2 * TILE), bf16),
            vmem((4 * nt * 2 * FP, 2 * TILE), bf16),
            vmem((4, 8, el), f32),
            vmem((4, 8, el), f32),
            vmem((3 * RP, 3 * RP), f32),
            vmem((4 * RP, 16 * FP), f32),
            vmem((nt, TR, TILE), f32),
            vmem((4, 2 * FP, el), f32),
            vmem((4, 2 * FP, el), f32),
            vmem((3, 2 * FP, SUB), f32),
            vmem((3, 8, SUB), f32),
            vmem((kinds, TR, 2 * KB), bf16),
            vmem((kinds, HB, 2 * KB), bf16),
            vmem((nt, 2 * KB, TILE), bf16),
            vmem((1 + steps, TR, TILE), f32),
            vmem((4, 2 * FP, TILE), f32),
            vmem((NC, 3 * RP, el), f32),
            vmem((3, MSG, SUB), f32),
            vmem((3, MSG, SUB), f32),
            vmem((SWEEPS - 1, 2, 2 * FP, SUB), f32),
            vmem((SWEEPS - 1, 2, 2 * FP, SUB), f32),
            pltpu.SMEM((kinds + 1,), i32),
            pltpu.SMEM((5, max(steps, nt)), i32),
            dma((len(far),)), dma((3,)), dma((3,)), dma((SWEEPS - 1, 2)), dma((SWEEPS - 1, 2)),
        ],
        compiler_params=pltpu.CompilerParams(
            collective_id=0, has_side_effects=True, vmem_limit_bytes=56 * 2**20
        ),
    )(*near, *far)


def solution(mesh):
    both = ("group", "dom")
    in_specs = (
        P(None, None, both), P(None, both), P(None, both), P(None, None, both), P(None, both),
        P(None, both), P(both), P(both), P(), P(), P(),
    )
    return jax.shard_map(
        shards, mesh=mesh, in_specs=in_specs, out_specs=P(None, None, both), check_vma=False
    )
```

```python
import functools

import jax
import jax.numpy as jnp
import numpy as np
from jax import lax
from jax.experimental import pallas as pl
from jax.experimental.pallas import tpu as pltpu
from jax.sharding import PartitionSpec as P

SWEEPS = 4
STEP = 0.2
NC, NP, NFP = 6, 35, 15
RP = 40
HB = NC * RP
KB = 256
FP = 16
TR = NC * 4 * FP
TILE = 256
SUB = 128
MSG = NC * FP + 8
f32, bf16, i32 = jnp.float32, jnp.bfloat16, jnp.int32


def face_nodes():
    lattice = [(r, s, t) for r in range(5) for s in range(5 - r) for t in range(5 - r - s)]
    tests = [
        lambda p: p[2] == 0,
        lambda p: p[1] == 0,
        lambda p: p[0] == 0,
        lambda p: sum(p) == 4,
    ]
    return [[i for i, p in enumerate(lattice) if test(p)] for test in tests]


def constants(el, kinds):
    trace = np.zeros((4 * FP, NP), np.float32)
    for f, nodes in enumerate(face_nodes()):
        for n, node in enumerate(nodes):
            trace[f * FP + n, node] = 1
    eye6 = np.eye(NC, dtype=np.float32)
    pad = np.eye(RP, NP, dtype=np.float32)
    trace6 = np.kron(eye6, trace)
    rows6 = np.kron(eye6, pad)
    cols6 = np.zeros((NC * NP, KB), np.float32)
    cols6[:, :HB] = rows6.T
    tracep = np.tile(trace6 @ cols6, (1, 2))
    spread = np.zeros((2, NP, 3 * RP), np.float32)
    for i in range(NP):
        spread[0, i, i] = spread[0, i, RP + i] = spread[1, i, 2 * RP + i] = 1
    lift_spread = np.zeros((4, 4 * NFP, 16 * FP), np.float32)
    for f in range(4):
        for n in range(NFP):
            row, col = f * NFP + n, f * FP + n
            for i in range(2):
                lift_spread[2 * i, row, 8 * FP * i + col] = 1
                lift_spread[2 * i, row, 8 * FP * i + 4 * FP + col] = 1
                lift_spread[2 * i + 1, row, 8 * FP * i + col] = 1
    upper = np.concatenate([np.triu(np.ones((SUB, SUB)), 1), np.ones((SUB, SUB))], axis=1)
    lines = (kinds + 1) * (el // SUB)
    lower = np.tril(np.ones((lines, lines)), -1)
    small = [jnp.asarray(a, bf16) for a in (upper, lower, spread, lift_spread)]
    large = [jnp.asarray(a, bf16) for a in (tracep, trace6, rows6, cols6)]
    return small, large


def split(x):
    hi = x.astype(bf16)
    return hi, (x - hi.astype(f32)).astype(bf16)


def dot(a, b):
    return jnp.dot(a, b, preferred_element_type=f32)


def stacked(x):
    hi, lo = split(x)
    gap = jnp.zeros((KB - HB, x.shape[1]), bf16)
    return jnp.concatenate([hi, gap, lo, gap], axis=0)


def project(at, n):
    sa, ca, sb, cb = n
    e_t = ca * (cb * at[0] + sb * at[1]) - sa * at[2]
    e_p = cb * at[1] - sb * at[0]
    h_t = ca * (cb * at[3] + sb * at[4]) - sa * at[5]
    h_p = cb * at[4] - sb * at[3]
    return jnp.concatenate([h_p - e_t, -h_t - e_p], axis=0)


def lanes(x, index):
    return jnp.take_along_axis(x, jnp.broadcast_to(index, x.shape), axis=1)


def kernel(
    el, kinds, scale, angles, nb, send_dom, send_part, kind, deriv, lift,
    upper, lower, spread, lift_spread,
    fields_h, metric_h, binv_h, tracep_h, trace6_h, rows6_h, cols6_h,
    out,
    fraw, metric, binv, tracep, trace6, rows6, cols6,
    fpad, own, xs, ohs, lnorm, slots, sgn, kindrow, offs, lsl, pm, sel, pooln, pool, recvn, coef,
    d3, l2, trs, ext, base, rem, remn, wt, wf, rhs, zs, pq0, grads,
    send0, recv0, sendk, recvk, off, walk,
    in_sem, ssem0, rsem0, ssemk, rsemk,
):
    grp, dom = lax.axis_index("group"), lax.axis_index("dom")
    count = lax.axis_size("dom")
    half = count // 2
    fine = jnp.logical_and(grp == 1, dom >= half)
    coarse = jnp.logical_not(fine)
    nt = el // TILE
    shift = el.bit_length() - 1
    lines = el // SUB
    steps = nt - 1 + kinds - 1
    has_prev, has_next = dom > 0, dom < count - 1
    fine_prev = jnp.logical_and(fine, dom > half)
    fine_next = jnp.logical_and(fine, has_next)

    loads = [
        pltpu.make_async_copy(a, b, in_sem.at[i])
        for i, (a, b) in enumerate((
            (fields_h, fraw), (tracep_h, tracep), (cols6_h, cols6), (binv_h, binv),
            (trace6_h, trace6), (rows6_h, rows6), (metric_h, metric),
        ))
    ]
    for load in loads:
        load.start()

    barrier = pltpu.get_barrier_semaphore()

    @pl.when(has_prev)
    def _():
        pl.semaphore_signal(barrier, inc=1, device_id={"dom": dom - 1})

    @pl.when(has_next)
    def _():
        pl.semaphore_signal(barrier, inc=1, device_id={"dom": dom + 1})

    pl.semaphore_signal(barrier, inc=1, device_id={"group": 1 - grp})

    targets = ({"dom": dom - 1}, {"dom": dom + 1}, {"group": 1 - grp})
    lands = (1, 0, 2)
    first = [
        pltpu.make_async_remote_copy(
            src_ref=send0.at[i], dst_ref=recv0.at[lands[i]],
            send_sem=ssem0.at[i], recv_sem=rsem0.at[lands[i]], device_id=targets[i],
        )
        for i in range(3)
    ]

    def later(no):
        return [
            pltpu.make_async_remote_copy(
                src_ref=sendk.at[no - 1, i], dst_ref=recvk.at[no - 1, lands[i]],
                send_sem=ssemk.at[no - 1, i], recv_sem=rsemk.at[no - 1, lands[i]],
                device_id=targets[i],
            )
            for i in range(2)
        ]

    polar, azimuth = angles[0], angles[1]
    parts = (jnp.sin(polar), jnp.cos(polar), jnp.sin(azimuth), jnp.cos(azimuth))
    own[...] = jnp.zeros_like(own)
    for f in range(4):
        for i in range(4):
            own[f * 8 + i : f * 8 + i + 1, :] = parts[i][f : f + 1, :]
        own[f * 8 + 4 : f * 8 + 5, :] = 0.5 * scale[f : f + 1, :]
    lists = jnp.concatenate([send_dom[0:1, :], send_dom[1:2, :], send_part[...]], axis=1)
    down = lax.broadcasted_iota(i32, (el, 3 * SUB), 0)
    ohs[...] = jnp.where(down == (lists & (el - 1)), 1.0, 0.0).astype(bf16)
    xs[2 * HB : 2 * HB + 32, :], xs[2 * HB + 32 : 2 * HB + 64, :] = split(own[...])

    loads[0].wait()
    for c in range(NC):
        fpad[c * RP + 32 : (c + 1) * RP, :] = jnp.zeros((8, el), f32)
        fpad[c * RP : c * RP + NP, :] = fraw[c]
    xs[0:HB, :], xs[HB : 2 * HB, :] = split(fpad[...])
    loads[1].wait()
    y = dot(xs[...], ohs[...])
    at_list = y[2 * HB : 2 * HB + 32] + y[2 * HB + 32 : 2 * HB + 64]
    face = lists >> shift
    mine = at_list[0:8]
    for f in range(1, 4):
        mine = jnp.where(face == f, at_list[f * 8 : (f + 1) * 8], mine)
    lnorm[...] = mine
    t = dot(tracep[...], stacked(y[0:HB] + y[HB : 2 * HB]))
    for c in range(NC):
        v = t[c * 4 * FP : c * 4 * FP + FP]
        for f in range(1, 4):
            v = jnp.where(face == f, t[(c * 4 + f) * FP : (c * 4 + f + 1) * FP], v)
        for i in range(3):
            send0[i, c * FP : (c + 1) * FP, :] = v[:, i * SUB : (i + 1) * SUB]
    for i in range(3):
        send0[i, NC * FP : MSG, :] = mine[:, i * SUB : (i + 1) * SUB]

    pl.semaphore_wait(barrier, 1 + has_prev.astype(i32) + has_next.astype(i32))

    @pl.when(has_prev)
    def _():
        first[0].start()

    @pl.when(has_next)
    def _():
        first[1].start()

    first[2].start()

    @pl.when(coarse)
    def _():
        for f in range(4):
            row = nb[f : f + 1, :]
            lane = lax.broadcasted_iota(i32, (1, el), 1)
            slots[f : f + 1, :] = jnp.where(row < 0, lane + f * el, row)
            sgn[f : f + 1, :] = jnp.where(row < 0, -1.0, 1.0)

    @pl.when(fine)
    def _():
        def square(row):
            return jnp.concatenate([row[:, i * SUB : (i + 1) * SUB] for i in range(lines)], axis=0)

        def line(sq):
            return jnp.concatenate([sq[i : i + 1] for i in range(lines)], axis=1)

        faces = [square(nb[f : f + 1, :]) for f in range(4)]
        which = square(kind[...])
        edge = functools.reduce(
            jnp.logical_or,
            [jnp.logical_and(n >= 4 * el, n < 4 * el + 2 * SUB) for n in faces],
        )
        group = jnp.where(edge, 0, which)
        masks = jnp.concatenate(
            [jnp.where(group == k, 1.0, 0.0) for k in range(kinds + 1)], axis=0
        )
        pre = dot(masks.astype(bf16), upper[...])
        before = dot(lower[...], pre[:, SUB:].astype(bf16))
        ranks = masks * (pre[:, :SUB] + before)
        pos = sum(ranks[k * lines : (k + 1) * lines] for k in range(kinds + 1))
        offs[...] = before.astype(i32)
        for k in range(kinds):
            off[k] = offs[(k + 1) * lines, 0]
        off[kinds] = jnp.int32(el)
        t, k = jnp.int32(1), jnp.int32(1)
        seen = [jnp.int32(-1)] * nt
        for s in range(steps):
            lo, hi = off[k - 1], off[k]
            walk[0, s] = t
            walk[1, s] = k - 1
            walk[2, s] = lo - t * TILE
            walk[3, s] = hi - t * TILE
            seen = [n + jnp.where(t <= i, 1, 0) for i, n in enumerate(seen)]
            stay = jnp.logical_and(hi <= (t + 1) * TILE, k < kinds)
            k, t = jnp.where(stay, k + 1, k), jnp.where(stay, t, jnp.minimum(t + 1, nt - 1))
        for i in range(nt):
            walk[4, i] = jnp.clip(seen[i], 0, steps - 1)

        def lookup(e):
            lane, row = e & (SUB - 1), e >> (SUB.bit_length() - 1)
            res = jnp.zeros((lines, SUB), f32)
            for r in range(lines):
                table = jnp.broadcast_to(pos[r : r + 1], (lines, SUB))
                res = jnp.where(row == r, jnp.take_along_axis(table, lane, axis=1), res)
            return res.astype(i32)

        place = pos.astype(i32)
        for f in range(4):
            n = faces[f]
            inner = (n >> shift) * el + lookup(n & (el - 1))
            m = jnp.where(n < 0, f * el + place, jnp.where(n >= 4 * el, n, inner))
            flag = 2 * which + jnp.where(n < 0, 1, 0)
            for i, v in enumerate((m >> 6, m & 63, flag)):
                own[f * 8 + 5 + i : f * 8 + 6 + i, :] = line(v.astype(f32))
        mine = jnp.concatenate([send_dom[...]] * (lines // 2), axis=0)
        lsl[...] = (mine >> shift) * TILE + lookup(mine & (el - 1))

        row = line(place)
        for i in range(nt):
            down = lax.broadcasted_iota(i32, (TILE, el), 0) + i * TILE
            pm[i * TILE : (i + 1) * TILE, :] = jnp.where(down == row, 1.0, 0.0).astype(bf16)
        xs[2 * HB : 2 * HB + 32, :], xs[2 * HB + 32 : 2 * HB + 64, :] = split(own[...])
        y = lax.dot_general(
            xs[...], pm[...], (((1,), (1,)), ((), ())), preferred_element_type=f32
        )
        fpad[...] = y[0:HB] + y[HB : 2 * HB]
        own[...] = y[2 * HB : 2 * HB + 32] + y[2 * HB + 32 : 2 * HB + 64]
        for f in range(4):
            at = f * 8 + 5
            slots[f : f + 1, :] = (own[at : at + 1, :] * 64 + own[at + 1 : at + 2, :]).astype(i32)
            flag = own[at + 2 : at + 3, :].astype(i32)
            sgn[f : f + 1, :] = jnp.where((flag & 1) == 1, -1.0, 1.0)
            if f == 0:
                kindrow[...] = flag >> 1

    def pick(y, f, rows, total):
        which = slots[f : f + 1, :] >> (TILE.bit_length() - 1)
        for h in range(4 * nt):
            total = jnp.where(which == h, y[h * rows : (h + 1) * rows], total)
        return total

    def gather(source, rows, dest, under=None):
        for f in range(4):
            s = sel[:, f * el : (f + 1) * el]
            y = dot(source[...], jnp.concatenate([s, s], axis=0))
            dest[f] = pick(y, f, rows, jnp.zeros((rows, el), f32) if under is None else under[f])

    def place_at(dest, source, f, j, sources):
        s = slots[f : f + 1, j * SUB : (j + 1) * SUB]
        v = dest[f, :, j * SUB : (j + 1) * SUB]
        for i in sources:
            here = (s >> (SUB.bit_length() - 1)) == 4 * el // SUB + i
            v = jnp.where(here, lanes(source[i], s & (SUB - 1)), v)
        dest[f, :, j * SUB : (j + 1) * SUB] = v

    def fill(t, at_rows):
        cols = slice(t * TILE, (t + 1) * TILE)
        for f in range(4):
            at = [at_rows(c * 4 * FP + f * FP) for c in range(NC)]
            sign = sgn[f : f + 1, cols]
            at[:3] = [sign * e for e in at[:3]]
            pq = project(at, [recvn[f, i : i + 1, cols] for i in range(4)])
            hi, lo = split(pq)
            h = f * nt + t
            pool[h * 2 * FP : (h + 1) * 2 * FP, 0:TILE] = hi
            pool[h * 2 * FP : (h + 1) * 2 * FP, TILE : 2 * TILE] = lo
            if t == 0:
                pq0[f] = pq

    down = lax.broadcasted_iota(i32, (TILE, el), 0)
    for f in range(4):
        low = slots[f : f + 1, :] & (TILE - 1)
        sel[:, f * el : (f + 1) * el] = jnp.where(down == low, 1.0, 0.0).astype(bf16)
    for f in range(4):
        for t in range(0, nt, 2):
            both = [own[f * 8 : f * 8 + 8, (t + i) * TILE : (t + i + 1) * TILE] for i in range(2)]
            h = (f * nt + t) * 8
            pooln[h : h + 16, 0:TILE], pooln[h : h + 16, TILE : 2 * TILE] = split(
                jnp.concatenate(both, axis=0)
            )
        sa, ca, sb, cb, w = (own[f * 8 + i : f * 8 + i + 1, :] for i in range(5))
        for i, row in enumerate((w * ca * cb, w * ca * sb, -w * sa, -w * sb, w * cb)):
            coef[f, i : i + 1, :] = row
    gather(pooln, 8, recvn)
    for t in range(nt):
        z = dot(tracep[...], stacked(fpad[:, t * TILE : (t + 1) * TILE]))
        trs[t] = z
        fill(t, lambda r: z[r : r + FP])
    gather(pool, 2 * FP, ext)

    l2[...] = jnp.zeros_like(l2)
    hi, lo = split(lift[...])
    for i in range(4):
        l2[i * RP : i * RP + NP, :] = dot(lo if i % 2 else hi, lift_spread[i])
    for load in loads[2:]:
        load.wait()

    @pl.when(fine)
    def _():
        for k in range(kinds):
            b2 = dot(binv[k], cols6[...]).astype(bf16)
            a = dot(trace6[...], b2).astype(bf16)
            b = dot(rows6[...], b2).astype(bf16)
            for i in range(2):
                wt[k, :, i * KB : (i + 1) * KB] = a
                wf[k, :, i * KB : (i + 1) * KB] = b

    @pl.when(coarse)
    def _():
        d3[...] = jnp.zeros_like(d3)
        for b in range(3):
            hi, lo = split(deriv[b])
            d3[b * RP : b * RP + NP, :] = dot(hi, spread[0]) + dot(lo, spread[1])
        db = d3[...].astype(bf16)
        for c in range(NC):
            x = fpad[c * RP : (c + 1) * RP, :]
            hi = x.astype(bf16).astype(f32)
            grads[c] = dot(db, jnp.concatenate([hi, x - hi, hi], axis=0).astype(bf16))

    def arrive(i):
        at = [recv0[i, c * FP : (c + 1) * FP, :] for c in range(NC)]
        rem[i] = project(at, [lnorm[r : r + 1, i * SUB : (i + 1) * SUB] for r in range(4)])
        remn[i] = recv0[i, NC * FP : MSG, :]

    rem[...] = jnp.zeros_like(rem)
    remn[...] = jnp.zeros_like(remn)

    @pl.when(has_prev)
    def _():
        first[0].wait_send()
        first[1].wait_recv()
        arrive(0)

    @pl.when(has_next)
    def _():
        first[1].wait_send()
        first[0].wait_recv()
        arrive(1)

    first[2].wait()
    arrive(2)

    def lifted(t, pq):
        cols = slice(t * TILE, (t + 1) * TILE)
        for pair in range(NC // 2):
            pieces = []
            for c in (2 * pair, 2 * pair + 1):
                rows = []
                k = c % 3
                for f in range(4):
                    p, q = pq[f][:FP], pq[f][FP:]
                    a, b = (p, q) if c < 3 else (q, -p)
                    row = coef[f, k : k + 1, cols] * a
                    if k < 2:
                        row = row + coef[f, 3 + k : 4 + k, cols] * b
                    rows.append(row)
                pieces.extend(split(jnp.concatenate(rows, axis=0)))
            y = dot(l2[...].astype(bf16), jnp.concatenate(pieces, axis=0))
            for i in range(2):
                at = 2 * i * RP
                yield 2 * pair + i, y[at : at + RP] + y[at + RP : at + 2 * RP]

    @pl.when(coarse)
    def _():
        for f in range(4):
            for j in range(lines):
                place_at(ext, rem, f, j, range(3))
        for t in range(nt):
            cols = slice(t * TILE, (t + 1) * TILE)

            def along(c, axis):
                return sum(
                    metric[3 * axis + b : 3 * axis + b + 1, cols]
                    * grads[c, b * RP : (b + 1) * RP, cols]
                    for b in range(3)
                )

            pq = []
            for f in range(4):
                at = [trs[t, (c * 4 + f) * FP : (c * 4 + f + 1) * FP, :] for c in range(NC)]
                n = [own[f * 8 + i : f * 8 + i + 1, cols] for i in range(4)]
                pq.append(project(at, n) - ext[f, :, cols])
            for c, s in lifted(t, pq):
                k, other = c % 3, 3 - 3 * (c // 3)
                one, two = (k + 1) % 3, (k + 2) % 3
                curl = along(other + two, one) - along(other + one, two)
                vol = curl if c < 3 else -curl
                value = fpad[c * RP : (c + 1) * RP, cols] + STEP * (vol + s)
                out[c, :, cols] = value[:NP]

    @pl.when(fine)
    def _():
        for f in range(4):
            for j in range(lines):
                edge = j < TILE // SUB
                place_at(ext, rem, f, j, range(3) if edge else (2,))
                if edge:
                    place_at(recvn, remn, f, j, range(2))
            base[f] = jnp.where(slots[f : f + 1, :] >= 4 * el, ext[f], 0.0)

        def right_side(t):
            cols = slice(t * TILE, (t + 1) * TILE)
            terms = [
                fpad[c * RP : (c + 1) * RP, cols] - STEP * s
                for c, s in lifted(t, [ext[f, :, cols] for f in range(4)])
            ]
            rhs[t] = stacked(jnp.concatenate(terms, axis=0))

        def edge_blocks(weights, rows):
            z = dot(weights[0], rhs[0])
            for k in range(1, kinds):
                z = jnp.where(kindrow[:, 0:TILE] == k + 1, dot(weights[k], rhs[0]), z)
            zs[0, 0:rows, :] = z

        def inside(row, at, size):
            return jnp.clip(walk[row, at], 0, size - 1)

        def inner_blocks(weights, rows):
            lane = lax.broadcasted_iota(i32, (1, TILE), 1)
            for s in range(steps):
                y = dot(weights[inside(1, s, kinds)], rhs[inside(0, s, nt)])
                if s:
                    here = jnp.logical_and(lane >= walk[2, s], lane < walk[3, s])
                    y = jnp.where(here, y, zs[s, 0:rows, :])
                zs[1 + s, 0:rows, :] = y

        def sweep(no, carry):
            right_side(0)
            edge_blocks(wt, TR)
            fill(0, lambda r: zs[0, r : r + FP, :])
            for i in range(2):
                at = lsl[i : i + 1, :]
                v = jnp.zeros((2 * FP, SUB), f32)
                for h in range(4 * TILE // SUB):
                    f, j = h // (TILE // SUB), h % (TILE // SUB)
                    x = lanes(pq0[f, :, j * SUB : (j + 1) * SUB], at & (SUB - 1))
                    v = jnp.where((at >> (SUB.bit_length() - 1)) == h, x, v)
                sendk[no - 1, i] = v
            copies = later(no)

            @pl.when(fine_prev)
            def _():
                copies[0].start()

            @pl.when(fine_next)
            def _():
                copies[1].start()

            for t in range(1, nt):
                right_side(t)
            inner_blocks(wt, TR)
            for t in range(1, nt):
                last = inside(4, t, steps)
                fill(t, lambda r: zs[1 + last, r : r + FP, :])
            gather(pool, 2 * FP, ext, base)

            @pl.when(fine_prev)
            def _():
                copies[0].wait_send()
                copies[1].wait_recv()
                rem[0] = recvk[no - 1, 0]

            @pl.when(fine_next)
            def _():
                copies[1].wait_send()
                copies[0].wait_recv()
                rem[1] = recvk[no - 1, 1]

            for f in range(4):
                for j in range(TILE // SUB):
                    place_at(ext, rem, f, j, range(2))
            return carry

        lax.fori_loop(1, SWEEPS, sweep, 0)
        for t in range(nt):
            right_side(t)
        edge_blocks(wf, HB)
        inner_blocks(wf, HB)
        for t in range(nt):
            at = 1 + inside(4, t, steps) if t else 0
            cols = slice(t * TILE, (t + 1) * TILE)
            xs[0:HB, cols], xs[HB : 2 * HB, cols] = split(zs[at, 0:HB, :])
        y = dot(xs[0 : 2 * HB, :], pm[...])
        for c in range(NC):
            at = c * RP
            out[c] = y[at : at + NP] + y[HB + at : HB + at + NP]


def shards(*args):
    (fields, metric, scale, angles, nb, send_dom, send_part, kind, deriv, lift, binv) = args
    el = fields.shape[2]
    kinds = binv.shape[0]
    nt, lines = el // TILE, el // SUB
    steps = nt - 1 + kinds - 1
    small, large = constants(el, kinds)
    near = [
        scale, angles, nb, send_dom, send_part.reshape(1, -1), kind.reshape(1, -1), deriv, lift,
        *small,
    ]
    far = [fields, metric, binv, *large]
    vmem, dma = pltpu.VMEM, pltpu.SemaphoreType.DMA
    return pl.pallas_call(
        functools.partial(kernel, el, kinds),
        out_shape=pltpu.VMEM(fields.shape, f32),
        in_specs=[pl.BlockSpec(memory_space=vmem)] * len(near)
        + [pl.BlockSpec(memory_space=pl.ANY)] * len(far),
        out_specs=pl.BlockSpec(memory_space=vmem),
        scratch_shapes=[
            *[vmem(a.shape, a.dtype) for a in far],
            vmem((HB, el), f32),
            vmem((32, el), f32),
            vmem((2 * HB + 64, el), bf16),
            vmem((el, 3 * SUB), bf16),
            vmem((8, 3 * SUB), f32),
            vmem((4, el), i32),
            vmem((4, el), f32),
            vmem((1, el), i32),
            vmem(((kinds + 1) * lines, SUB), i32),
            vmem((lines, SUB), i32),
            vmem((el, el), bf16),
            vmem((TILE, 4 * el), bf16),
            vmem((4 * nt * 8, 2 * TILE), bf16),
            vmem((4 * nt * 2 * FP, 2 * TILE), bf16),
            vmem((4, 8, el), f32),
            vmem((4, 8, el), f32),
            vmem((3 * RP, 3 * RP), f32),
            vmem((4 * RP, 16 * FP), f32),
            vmem((nt, TR, TILE), f32),
            vmem((4, 2 * FP, el), f32),
            vmem((4, 2 * FP, el), f32),
            vmem((3, 2 * FP, SUB), f32),
            vmem((3, 8, SUB), f32),
            vmem((kinds, TR, 2 * KB), bf16),
            vmem((kinds, HB, 2 * KB), bf16),
            vmem((nt, 2 * KB, TILE), bf16),
            vmem((1 + steps, TR, TILE), f32),
            vmem((4, 2 * FP, TILE), f32),
            vmem((NC, 3 * RP, el), f32),
            vmem((3, MSG, SUB), f32),
            vmem((3, MSG, SUB), f32),
            vmem((SWEEPS - 1, 2, 2 * FP, SUB), f32),
            vmem((SWEEPS - 1, 2, 2 * FP, SUB), f32),
            pltpu.SMEM((kinds + 1,), i32),
            pltpu.SMEM((5, max(steps, nt)), i32),
            dma((len(far),)), dma((3,)), dma((3,)), dma((SWEEPS - 1, 2)), dma((SWEEPS - 1, 2)),
        ],
        compiler_params=pltpu.CompilerParams(
            collective_id=0, has_side_effects=True, vmem_limit_bytes=56 * 2**20
        ),
    )(*near, *far)


def solution(mesh):
    both = ("group", "dom")
    in_specs = (
        P(None, None, both), P(None, both), P(None, both), P(None, None, both), P(None, both),
        P(None, both), P(both), P(both), P(), P(), P(),
    )
    return jax.shard_map(
        shards, mesh=mesh, in_specs=in_specs, out_specs=P(None, None, both), check_vma=False
    )
```

```python
import functools

import jax
import jax.numpy as jnp
import numpy as np
from jax import lax
from jax.experimental import pallas as pl
from jax.experimental.pallas import tpu as pltpu
from jax.sharding import PartitionSpec as P

SWEEPS = 4
STEP = 0.2
NC, NP, NFP = 6, 35, 15
RP = 40
HB = NC * RP
KB = 256
FP = 16
TR = NC * 4 * FP
TILE = 256
SUB = 128
DIRECT = 1
MSG = NC * FP + 8
f32, bf16, i32 = jnp.float32, jnp.bfloat16, jnp.int32


def face_nodes():
    lattice = [(r, s, t) for r in range(5) for s in range(5 - r) for t in range(5 - r - s)]
    tests = [
        lambda p: p[2] == 0,
        lambda p: p[1] == 0,
        lambda p: p[0] == 0,
        lambda p: sum(p) == 4,
    ]
    return [[i for i, p in enumerate(lattice) if test(p)] for test in tests]


def constants(el, kinds):
    trace = np.zeros((4 * FP, NP), np.float32)
    for f, nodes in enumerate(face_nodes()):
        for n, node in enumerate(nodes):
            trace[f * FP + n, node] = 1
    eye6 = np.eye(NC, dtype=np.float32)
    pad = np.eye(RP, NP, dtype=np.float32)
    trace6 = np.kron(eye6, trace)
    rows6 = np.kron(eye6, pad)
    cols6 = np.zeros((NC * NP, KB), np.float32)
    cols6[:, :HB] = rows6.T
    tracep = np.tile(trace6 @ cols6, (1, 2))
    spread = np.zeros((2, NP, 3 * RP), np.float32)
    for i in range(NP):
        spread[0, i, i] = spread[0, i, RP + i] = spread[1, i, 2 * RP + i] = 1
    lift_spread = np.zeros((4, 4 * NFP, 16 * FP), np.float32)
    for f in range(4):
        for n in range(NFP):
            row, col = f * NFP + n, f * FP + n
            for i in range(2):
                lift_spread[2 * i, row, 8 * FP * i + col] = 1
                lift_spread[2 * i, row, 8 * FP * i + 4 * FP + col] = 1
                lift_spread[2 * i + 1, row, 8 * FP * i + col] = 1
    upper = np.concatenate([np.triu(np.ones((SUB, SUB)), 1), np.ones((SUB, SUB))], axis=1)
    lines = (kinds + 1) * (el // SUB)
    lower = np.tril(np.ones((lines, lines)), -1)
    small = [jnp.asarray(a, bf16) for a in (upper, lower, spread, lift_spread)]
    large = [jnp.asarray(a, bf16) for a in (tracep, trace6, rows6, cols6)]
    return small, large


def split(x):
    hi = x.astype(bf16)
    return hi, (x - hi.astype(f32)).astype(bf16)


def dot(a, b):
    return jnp.dot(a, b, preferred_element_type=f32)


def stacked(x):
    hi, lo = split(x)
    gap = jnp.zeros((KB - HB, x.shape[1]), bf16)
    return jnp.concatenate([hi, gap, lo, gap], axis=0)


def project(at, n):
    sa, ca, sb, cb = n
    e_t = ca * (cb * at[0] + sb * at[1]) - sa * at[2]
    e_p = cb * at[1] - sb * at[0]
    h_t = ca * (cb * at[3] + sb * at[4]) - sa * at[5]
    h_p = cb * at[4] - sb * at[3]
    return jnp.concatenate([h_p - e_t, -h_t - e_p], axis=0)


def lanes(x, index):
    return jnp.take_along_axis(x, jnp.broadcast_to(index, x.shape), axis=1)


def kernel(
    el, kinds, scale, angles, nb, send_dom, send_part, kind, deriv, lift,
    upper, lower, spread, lift_spread,
    fields_h, metric_h, binv_h, tracep_h, trace6_h, rows6_h, cols6_h,
    out,
    fraw, metric, binv, tracep, trace6, rows6, cols6,
    fpad, own, xs, ohs, lnorm, slots, sgn, kindrow, offs, lsl, pm, sel, pooln, pool, recvn, coef,
    d3, l2, trs, ext, base, rem, remn, wt, wf, rhs, zs, pqs, acc, grads,
    send0, recv0, sendk, recvk, off, walk,
    in_sem, ssem0, rsem0, ssemk, rsemk,
):
    grp, dom = lax.axis_index("group"), lax.axis_index("dom")
    count = lax.axis_size("dom")
    half = count // 2
    fine = jnp.logical_and(grp == 1, dom >= half)
    coarse = jnp.logical_not(fine)
    nt = el // TILE
    shift = el.bit_length() - 1
    lines = el // SUB
    steps = nt - 1 + kinds - 1
    has_prev, has_next = dom > 0, dom < count - 1
    fine_prev = jnp.logical_and(fine, dom > half)
    fine_next = jnp.logical_and(fine, has_next)

    loads = [
        pltpu.make_async_copy(a, b, in_sem.at[i])
        for i, (a, b) in enumerate((
            (fields_h, fraw), (tracep_h, tracep), (cols6_h, cols6), (binv_h, binv),
            (trace6_h, trace6), (rows6_h, rows6), (metric_h, metric),
        ))
    ]
    for load in loads:
        load.start()

    barrier = pltpu.get_barrier_semaphore()

    @pl.when(has_prev)
    def _():
        pl.semaphore_signal(barrier, inc=1, device_id={"dom": dom - 1})

    @pl.when(has_next)
    def _():
        pl.semaphore_signal(barrier, inc=1, device_id={"dom": dom + 1})

    pl.semaphore_signal(barrier, inc=1, device_id={"group": 1 - grp})

    targets = ({"dom": dom - 1}, {"dom": dom + 1}, {"group": 1 - grp})
    lands = (1, 0, 2)
    first = [
        pltpu.make_async_remote_copy(
            src_ref=send0.at[i], dst_ref=recv0.at[lands[i]],
            send_sem=ssem0.at[i], recv_sem=rsem0.at[lands[i]], device_id=targets[i],
        )
        for i in range(3)
    ]

    def later(no):
        return [
            pltpu.make_async_remote_copy(
                src_ref=sendk.at[no - 1, i], dst_ref=recvk.at[no - 1, lands[i]],
                send_sem=ssemk.at[no - 1, i], recv_sem=rsemk.at[no - 1, lands[i]],
                device_id=targets[i],
            )
            for i in range(2)
        ]

    polar, azimuth = angles[0], angles[1]
    parts = (jnp.sin(polar), jnp.cos(polar), jnp.sin(azimuth), jnp.cos(azimuth))
    own[...] = jnp.zeros_like(own)
    for f in range(4):
        for i in range(4):
            own[f * 8 + i : f * 8 + i + 1, :] = parts[i][f : f + 1, :]
        own[f * 8 + 4 : f * 8 + 5, :] = 0.5 * scale[f : f + 1, :]
    lists = jnp.concatenate([send_dom[0:1, :], send_dom[1:2, :], send_part[...]], axis=1)
    down = lax.broadcasted_iota(i32, (el, 3 * SUB), 0)
    ohs[...] = jnp.where(down == (lists & (el - 1)), 1.0, 0.0).astype(bf16)
    xs[2 * HB : 2 * HB + 32, :], xs[2 * HB + 32 : 2 * HB + 64, :] = split(own[...])

    loads[0].wait()
    for c in range(NC):
        fpad[c * RP + 32 : (c + 1) * RP, :] = jnp.zeros((8, el), f32)
        fpad[c * RP : c * RP + NP, :] = fraw[c]
    xs[0:HB, :], xs[HB : 2 * HB, :] = split(fpad[...])
    loads[1].wait()
    y = dot(xs[...], ohs[...])
    at_list = y[2 * HB : 2 * HB + 32] + y[2 * HB + 32 : 2 * HB + 64]
    face = lists >> shift
    mine = at_list[0:8]
    for f in range(1, 4):
        mine = jnp.where(face == f, at_list[f * 8 : (f + 1) * 8], mine)
    lnorm[...] = mine
    t = dot(tracep[...], stacked(y[0:HB] + y[HB : 2 * HB]))
    for c in range(NC):
        v = t[c * 4 * FP : c * 4 * FP + FP]
        for f in range(1, 4):
            v = jnp.where(face == f, t[(c * 4 + f) * FP : (c * 4 + f + 1) * FP], v)
        for i in range(3):
            send0[i, c * FP : (c + 1) * FP, :] = v[:, i * SUB : (i + 1) * SUB]
    for i in range(3):
        send0[i, NC * FP : MSG, :] = mine[:, i * SUB : (i + 1) * SUB]

    pl.semaphore_wait(barrier, 1 + has_prev.astype(i32) + has_next.astype(i32))

    @pl.when(has_prev)
    def _():
        first[0].start()

    @pl.when(has_next)
    def _():
        first[1].start()

    first[2].start()

    @pl.when(coarse)
    def _():
        for f in range(4):
            row = nb[f : f + 1, :]
            lane = lax.broadcasted_iota(i32, (1, el), 1)
            slots[f : f + 1, :] = jnp.where(row < 0, lane + f * el, row)
            sgn[f : f + 1, :] = jnp.where(row < 0, -1.0, 1.0)

    @pl.when(fine)
    def _():
        def square(row):
            return jnp.concatenate([row[:, i * SUB : (i + 1) * SUB] for i in range(lines)], axis=0)

        def line(sq):
            return jnp.concatenate([sq[i : i + 1] for i in range(lines)], axis=1)

        faces = [square(nb[f : f + 1, :]) for f in range(4)]
        which = square(kind[...])
        edge = functools.reduce(
            jnp.logical_or,
            [jnp.logical_and(n >= 4 * el, n < 4 * el + 2 * SUB) for n in faces],
        )
        group = jnp.where(edge, 0, which)
        masks = jnp.concatenate(
            [jnp.where(group == k, 1.0, 0.0) for k in range(kinds + 1)], axis=0
        )
        pre = dot(masks.astype(bf16), upper[...])
        before = dot(lower[...], pre[:, SUB:].astype(bf16))
        ranks = masks * (pre[:, :SUB] + before)
        pos = sum(ranks[k * lines : (k + 1) * lines] for k in range(kinds + 1))
        offs[...] = before.astype(i32)
        for k in range(kinds):
            off[k] = offs[(k + 1) * lines, 0]
        off[kinds] = jnp.int32(el)
        t, k = jnp.int32(1), jnp.int32(1)
        seen = [jnp.int32(-1)] * nt
        for s in range(steps):
            lo, hi = off[k - 1], off[k]
            walk[0, s] = t
            walk[1, s] = k - 1
            walk[2, s] = lo - t * TILE
            walk[3, s] = hi - t * TILE
            seen = [n + jnp.where(t <= i, 1, 0) for i, n in enumerate(seen)]
            stay = jnp.logical_and(hi <= (t + 1) * TILE, k < kinds)
            k, t = jnp.where(stay, k + 1, k), jnp.where(stay, t, jnp.minimum(t + 1, nt - 1))
        for i in range(nt):
            walk[4, i] = jnp.clip(seen[i], 0, steps - 1)

        def lookup(e):
            lane, row = e & (SUB - 1), e >> (SUB.bit_length() - 1)
            res = jnp.zeros((lines, SUB), f32)
            for r in range(lines):
                table = jnp.broadcast_to(pos[r : r + 1], (lines, SUB))
                res = jnp.where(row == r, jnp.take_along_axis(table, lane, axis=1), res)
            return res.astype(i32)

        place = pos.astype(i32)
        for f in range(4):
            n = faces[f]
            inner = (n >> shift) * el + lookup(n & (el - 1))
            m = jnp.where(n < 0, f * el + place, jnp.where(n >= 4 * el, n, inner))
            flag = 2 * which + jnp.where(n < 0, 1, 0)
            for i, v in enumerate((m >> 6, m & 63, flag)):
                own[f * 8 + 5 + i : f * 8 + 6 + i, :] = line(v.astype(f32))
        mine = jnp.concatenate([send_dom[...]] * (lines // 2), axis=0)
        lsl[...] = (mine >> shift) * TILE + lookup(mine & (el - 1))

        row = line(place)
        for i in range(nt):
            down = lax.broadcasted_iota(i32, (TILE, el), 0) + i * TILE
            pm[i * TILE : (i + 1) * TILE, :] = jnp.where(down == row, 1.0, 0.0).astype(bf16)
        xs[2 * HB : 2 * HB + 32, :], xs[2 * HB + 32 : 2 * HB + 64, :] = split(own[...])
        y = lax.dot_general(
            xs[...], pm[...], (((1,), (1,)), ((), ())), preferred_element_type=f32
        )
        fpad[...] = y[0:HB] + y[HB : 2 * HB]
        own[...] = y[2 * HB : 2 * HB + 32] + y[2 * HB + 32 : 2 * HB + 64]
        for f in range(4):
            at = f * 8 + 5
            slots[f : f + 1, :] = (own[at : at + 1, :] * 64 + own[at + 1 : at + 2, :]).astype(i32)
            flag = own[at + 2 : at + 3, :].astype(i32)
            sgn[f : f + 1, :] = jnp.where((flag & 1) == 1, -1.0, 1.0)
            if f == 0:
                kindrow[...] = flag >> 1

    def pick(y, f, rows, total):
        which = slots[f : f + 1, :] >> (TILE.bit_length() - 1)
        for h in range(4 * nt):
            total = jnp.where(which == h, y[h * rows : (h + 1) * rows], total)
        return total

    def gather_direct(tiles, under, dest):
        for f in range(4 - DIRECT, 4):
            for j in range(lines):
                cols = slice(j * SUB, (j + 1) * SUB)
                at = slots[f : f + 1, cols]
                total = jnp.zeros((2 * FP, SUB), f32) if under is None else under[f, :, cols]
                for t in tiles:
                    for g in range(4):
                        for i in range(TILE // SUB):
                            h = g * lines + t * (TILE // SUB) + i
                            x = lanes(pqs[t, g, :, i * SUB : (i + 1) * SUB], at & (SUB - 1))
                            total = jnp.where((at >> (SUB.bit_length() - 1)) == h, x, total)
                dest[f, :, cols] = total

    def gather(source, rows, dest, under=None, faces=4):
        for f in range(faces):
            s = sel[:, f * el : (f + 1) * el]
            y = dot(source[...], jnp.concatenate([s, s], axis=0))
            dest[f] = pick(y, f, rows, jnp.zeros((rows, el), f32) if under is None else under[f])

    def place_at(dest, source, f, j, sources):
        s = slots[f : f + 1, j * SUB : (j + 1) * SUB]
        v = dest[f, :, j * SUB : (j + 1) * SUB]
        for i in sources:
            here = (s >> (SUB.bit_length() - 1)) == 4 * el // SUB + i
            v = jnp.where(here, lanes(source[i], s & (SUB - 1)), v)
        dest[f, :, j * SUB : (j + 1) * SUB] = v

    def fill(t, at_rows):
        cols = slice(t * TILE, (t + 1) * TILE)
        for f in range(4):
            at = [at_rows(c * 4 * FP + f * FP) for c in range(NC)]
            sign = sgn[f : f + 1, cols]
            at[:3] = [sign * e for e in at[:3]]
            pq = project(at, [recvn[f, i : i + 1, cols] for i in range(4)])
            hi, lo = split(pq)
            h = f * nt + t
            pool[h * 2 * FP : (h + 1) * 2 * FP, 0:TILE] = hi
            pool[h * 2 * FP : (h + 1) * 2 * FP, TILE : 2 * TILE] = lo
            pqs[t, f] = pq

    down = lax.broadcasted_iota(i32, (TILE, el), 0)
    for f in range(4):
        low = slots[f : f + 1, :] & (TILE - 1)
        sel[:, f * el : (f + 1) * el] = jnp.where(down == low, 1.0, 0.0).astype(bf16)
    for f in range(4):
        for t in range(0, nt, 2):
            both = [own[f * 8 : f * 8 + 8, (t + i) * TILE : (t + i + 1) * TILE] for i in range(2)]
            h = (f * nt + t) * 8
            pooln[h : h + 16, 0:TILE], pooln[h : h + 16, TILE : 2 * TILE] = split(
                jnp.concatenate(both, axis=0)
            )
        sa, ca, sb, cb, w = (own[f * 8 + i : f * 8 + i + 1, :] for i in range(5))
        for i, row in enumerate((w * ca * cb, w * ca * sb, -w * sa, -w * sb, w * cb)):
            coef[f, i : i + 1, :] = row
    gather(pooln, 8, recvn)
    for t in range(nt):
        z = dot(tracep[...], stacked(fpad[:, t * TILE : (t + 1) * TILE]))
        trs[t] = z
        fill(t, lambda r: z[r : r + FP])
    gather_direct(range(nt), None, ext)
    gather(pool, 2 * FP, ext, None, 4 - DIRECT)

    l2[...] = jnp.zeros_like(l2)
    hi, lo = split(lift[...])
    for i in range(4):
        l2[i * RP : i * RP + NP, :] = dot(lo if i % 2 else hi, lift_spread[i])
    for load in loads[2:]:
        load.wait()

    @pl.when(fine)
    def _():
        for k in range(kinds):
            b2 = dot(binv[k], cols6[...]).astype(bf16)
            a = dot(trace6[...], b2).astype(bf16)
            b = dot(rows6[...], b2).astype(bf16)
            for i in range(2):
                wt[k, :, i * KB : (i + 1) * KB] = a
                wf[k, :, i * KB : (i + 1) * KB] = b

    @pl.when(coarse)
    def _():
        d3[...] = jnp.zeros_like(d3)
        for b in range(3):
            hi, lo = split(deriv[b])
            d3[b * RP : b * RP + NP, :] = dot(hi, spread[0]) + dot(lo, spread[1])
        db = d3[...].astype(bf16)
        for c in range(NC):
            x = fpad[c * RP : (c + 1) * RP, :]
            hi = x.astype(bf16).astype(f32)
            grads[c] = dot(db, jnp.concatenate([hi, x - hi, hi], axis=0).astype(bf16))

    def arrive(i):
        at = [recv0[i, c * FP : (c + 1) * FP, :] for c in range(NC)]
        rem[i] = project(at, [lnorm[r : r + 1, i * SUB : (i + 1) * SUB] for r in range(4)])
        remn[i] = recv0[i, NC * FP : MSG, :]

    rem[...] = jnp.zeros_like(rem)
    remn[...] = jnp.zeros_like(remn)

    @pl.when(has_prev)
    def _():
        first[0].wait_send()
        first[1].wait_recv()
        arrive(0)

    @pl.when(has_next)
    def _():
        first[1].wait_send()
        first[0].wait_recv()
        arrive(1)

    first[2].wait()
    arrive(2)

    def lifted(t, pq):
        cols = slice(t * TILE, (t + 1) * TILE)
        for pair in range(NC // 2):
            pieces = []
            for c in (2 * pair, 2 * pair + 1):
                rows = []
                k = c % 3
                for f in range(4):
                    p, q = pq[f][:FP], pq[f][FP:]
                    a, b = (p, q) if c < 3 else (q, -p)
                    row = coef[f, k : k + 1, cols] * a
                    if k < 2:
                        row = row + coef[f, 3 + k : 4 + k, cols] * b
                    rows.append(row)
                pieces.extend(split(jnp.concatenate(rows, axis=0)))
            y = dot(l2[...].astype(bf16), jnp.concatenate(pieces, axis=0))
            for i in range(2):
                at = 2 * i * RP
                yield 2 * pair + i, y[at : at + RP] + y[at + RP : at + 2 * RP]

    @pl.when(coarse)
    def _():
        for f in range(4):
            for j in range(lines):
                place_at(ext, rem, f, j, range(3))
        for t in range(nt):
            cols = slice(t * TILE, (t + 1) * TILE)

            def along(c, axis):
                return sum(
                    metric[3 * axis + b : 3 * axis + b + 1, cols]
                    * grads[c, b * RP : (b + 1) * RP, cols]
                    for b in range(3)
                )

            pq = []
            for f in range(4):
                at = [trs[t, (c * 4 + f) * FP : (c * 4 + f + 1) * FP, :] for c in range(NC)]
                n = [own[f * 8 + i : f * 8 + i + 1, cols] for i in range(4)]
                pq.append(project(at, n) - ext[f, :, cols])
            for c, s in lifted(t, pq):
                k, other = c % 3, 3 - 3 * (c // 3)
                one, two = (k + 1) % 3, (k + 2) % 3
                curl = along(other + two, one) - along(other + one, two)
                vol = curl if c < 3 else -curl
                value = fpad[c * RP : (c + 1) * RP, cols] + STEP * (vol + s)
                out[c, :, cols] = value[:NP]

    @pl.when(fine)
    def _():
        for f in range(4):
            for j in range(lines):
                edge = j < TILE // SUB
                place_at(ext, rem, f, j, range(3) if edge else (2,))
                if edge:
                    place_at(recvn, remn, f, j, range(2))
            base[f] = jnp.where(slots[f : f + 1, :] >= 4 * el, ext[f], 0.0)

        def right_side(t):
            cols = slice(t * TILE, (t + 1) * TILE)
            terms = [
                fpad[c * RP : (c + 1) * RP, cols] - STEP * s
                for c, s in lifted(t, [ext[f, :, cols] for f in range(4)])
            ]
            rhs[t] = stacked(jnp.concatenate(terms, axis=0))

        def edge_blocks(weights, rows):
            z = dot(weights[0], rhs[0])
            for k in range(1, kinds):
                z = jnp.where(kindrow[:, 0:TILE] == k + 1, dot(weights[k], rhs[0]), z)
            zs[0, 0:rows, :] = z

        def inside(row, at, size):
            return jnp.clip(walk[row, at], 0, size - 1)

        def inner_blocks(weights, rows):
            lane = lax.broadcasted_iota(i32, (1, TILE), 1)
            for s in range(steps):
                y = dot(weights[inside(1, s, kinds)], rhs[inside(0, s, nt)])
                if s:
                    here = jnp.logical_and(lane >= walk[2, s], lane < walk[3, s])
                    y = jnp.where(here, y, zs[s, 0:rows, :])
                zs[1 + s, 0:rows, :] = y

        def sweep(no, carry):
            right_side(0)
            edge_blocks(wt, TR)
            fill(0, lambda r: zs[0, r : r + FP, :])
            for i in range(2):
                at = lsl[i : i + 1, :]
                v = jnp.zeros((2 * FP, SUB), f32)
                for h in range(4 * TILE // SUB):
                    f, j = h // (TILE // SUB), h % (TILE // SUB)
                    x = lanes(pqs[0, f, :, j * SUB : (j + 1) * SUB], at & (SUB - 1))
                    v = jnp.where((at >> (SUB.bit_length() - 1)) == h, x, v)
                sendk[no - 1, i] = v
            copies = later(no)

            @pl.when(fine_prev)
            def _():
                copies[0].start()

            @pl.when(fine_next)
            def _():
                copies[1].start()

            for t in range(1, nt):
                right_side(t)
            inner_blocks(wt, TR)
            for t in range(1, nt):
                last = inside(4, t, steps)
                fill(t, lambda r: zs[1 + last, r : r + FP, :])
            gather_direct(range(nt), base, ext)
            gather(pool, 2 * FP, ext, base, 4 - DIRECT)

            @pl.when(fine_prev)
            def _():
                copies[0].wait_send()
                copies[1].wait_recv()
                rem[0] = recvk[no - 1, 0]

            @pl.when(fine_next)
            def _():
                copies[1].wait_send()
                copies[0].wait_recv()
                rem[1] = recvk[no - 1, 1]

            for f in range(4):
                for j in range(TILE // SUB):
                    place_at(ext, rem, f, j, range(2))
            return carry

        lax.fori_loop(1, SWEEPS, sweep, 0)
        for t in range(nt):
            right_side(t)
        edge_blocks(wf, HB)
        inner_blocks(wf, HB)
        for t in range(nt):
            at = 1 + inside(4, t, steps) if t else 0
            cols = slice(t * TILE, (t + 1) * TILE)
            xs[0:HB, cols], xs[HB : 2 * HB, cols] = split(zs[at, 0:HB, :])
        y = dot(xs[0 : 2 * HB, :], pm[...])
        for c in range(NC):
            at = c * RP
            out[c] = y[at : at + NP] + y[HB + at : HB + at + NP]


def shards(*args):
    (fields, metric, scale, angles, nb, send_dom, send_part, kind, deriv, lift, binv) = args
    el = fields.shape[2]
    kinds = binv.shape[0]
    nt, lines = el // TILE, el // SUB
    steps = nt - 1 + kinds - 1
    small, large = constants(el, kinds)
    near = [
        scale, angles, nb, send_dom, send_part.reshape(1, -1), kind.reshape(1, -1), deriv, lift,
        *small,
    ]
    far = [fields, metric, binv, *large]
    vmem, dma = pltpu.VMEM, pltpu.SemaphoreType.DMA
    return pl.pallas_call(
        functools.partial(kernel, el, kinds),
        out_shape=pltpu.VMEM(fields.shape, f32),
        in_specs=[pl.BlockSpec(memory_space=vmem)] * len(near)
        + [pl.BlockSpec(memory_space=pl.ANY)] * len(far),
        out_specs=pl.BlockSpec(memory_space=vmem),
        scratch_shapes=[
            *[vmem(a.shape, a.dtype) for a in far],
            vmem((HB, el), f32),
            vmem((32, el), f32),
            vmem((2 * HB + 64, el), bf16),
            vmem((el, 3 * SUB), bf16),
            vmem((8, 3 * SUB), f32),
            vmem((4, el), i32),
            vmem((4, el), f32),
            vmem((1, el), i32),
            vmem(((kinds + 1) * lines, SUB), i32),
            vmem((lines, SUB), i32),
            vmem((el, el), bf16),
            vmem((TILE, 4 * el), bf16),
            vmem((4 * nt * 8, 2 * TILE), bf16),
            vmem((4 * nt * 2 * FP, 2 * TILE), bf16),
            vmem((4, 8, el), f32),
            vmem((4, 8, el), f32),
            vmem((3 * RP, 3 * RP), f32),
            vmem((4 * RP, 16 * FP), f32),
            vmem((nt, TR, TILE), f32),
            vmem((4, 2 * FP, el), f32),
            vmem((4, 2 * FP, el), f32),
            vmem((3, 2 * FP, SUB), f32),
            vmem((3, 8, SUB), f32),
            vmem((kinds, TR, 2 * KB), bf16),
            vmem((kinds, HB, 2 * KB), bf16),
            vmem((nt, 2 * KB, TILE), bf16),
            vmem((1 + steps, TR, TILE), f32),
            vmem((nt, 4, 2 * FP, TILE), f32),
            vmem((4, 2 * FP, el), f32),
            vmem((NC, 3 * RP, el), f32),
            vmem((3, MSG, SUB), f32),
            vmem((3, MSG, SUB), f32),
            vmem((SWEEPS - 1, 2, 2 * FP, SUB), f32),
            vmem((SWEEPS - 1, 2, 2 * FP, SUB), f32),
            pltpu.SMEM((kinds + 1,), i32),
            pltpu.SMEM((5, max(steps, nt)), i32),
            dma((len(far),)), dma((3,)), dma((3,)), dma((SWEEPS - 1, 2)), dma((SWEEPS - 1, 2)),
        ],
        compiler_params=pltpu.CompilerParams(
            collective_id=0, has_side_effects=True, vmem_limit_bytes=56 * 2**20
        ),
    )(*near, *far)


def solution(mesh):
    both = ("group", "dom")
    in_specs = (
        P(None, None, both), P(None, both), P(None, both), P(None, None, both), P(None, both),
        P(None, both), P(both), P(both), P(), P(), P(),
    )
    return jax.shard_map(
        shards, mesh=mesh, in_specs=in_specs, out_specs=P(None, None, both), check_vma=False
    )
```

```python
import functools

import jax
import jax.numpy as jnp
import numpy as np
from jax import lax
from jax.experimental import pallas as pl
from jax.experimental.pallas import tpu as pltpu
from jax.sharding import PartitionSpec as P

SWEEPS = 4
STEP = 0.2
NC, NP, NFP = 6, 35, 15
RP = 40
HB = NC * RP
KB = 256
FP = 16
TR = NC * 4 * FP
TILE = 256
SUB = 128
DIRECT = 1
SWAPPED = 2
MSG = NC * FP + 8
f32, bf16, i32 = jnp.float32, jnp.bfloat16, jnp.int32


def face_nodes():
    lattice = [(r, s, t) for r in range(5) for s in range(5 - r) for t in range(5 - r - s)]
    tests = [
        lambda p: p[2] == 0,
        lambda p: p[1] == 0,
        lambda p: p[0] == 0,
        lambda p: sum(p) == 4,
    ]
    return [[i for i, p in enumerate(lattice) if test(p)] for test in tests]


def constants(el, kinds):
    trace = np.zeros((4 * FP, NP), np.float32)
    for f, nodes in enumerate(face_nodes()):
        for n, node in enumerate(nodes):
            trace[f * FP + n, node] = 1
    eye6 = np.eye(NC, dtype=np.float32)
    pad = np.eye(RP, NP, dtype=np.float32)
    trace6 = np.kron(eye6, trace)
    rows6 = np.kron(eye6, pad)
    cols6 = np.zeros((NC * NP, KB), np.float32)
    cols6[:, :HB] = rows6.T
    tracep = np.tile(trace6 @ cols6, (1, 2))
    spread = np.zeros((2, NP, 3 * RP), np.float32)
    for i in range(NP):
        spread[0, i, i] = spread[0, i, RP + i] = spread[1, i, 2 * RP + i] = 1
    lift_spread = np.zeros((4, 4 * NFP, 16 * FP), np.float32)
    for f in range(4):
        for n in range(NFP):
            row, col = f * NFP + n, f * FP + n
            for i in range(2):
                lift_spread[2 * i, row, 8 * FP * i + col] = 1
                lift_spread[2 * i, row, 8 * FP * i + 4 * FP + col] = 1
                lift_spread[2 * i + 1, row, 8 * FP * i + col] = 1
    upper = np.concatenate([np.triu(np.ones((SUB, SUB)), 1), np.ones((SUB, SUB))], axis=1)
    lines = (kinds + 1) * (el // SUB)
    lower = np.tril(np.ones((lines, lines)), -1)
    small = [jnp.asarray(a, bf16) for a in (upper, lower, spread, lift_spread)]
    large = [jnp.asarray(a, bf16) for a in (tracep, trace6, rows6, cols6)]
    return small, large


def split(x):
    hi = x.astype(bf16)
    return hi, (x - hi.astype(f32)).astype(bf16)


def dot(a, b):
    return jnp.dot(a, b, preferred_element_type=f32)


def stacked(x):
    hi, lo = split(x)
    gap = jnp.zeros((KB - HB, x.shape[1]), bf16)
    return jnp.concatenate([hi, gap, lo, gap], axis=0)


def project(at, n):
    sa, ca, sb, cb = n
    e_t = ca * (cb * at[0] + sb * at[1]) - sa * at[2]
    e_p = cb * at[1] - sb * at[0]
    h_t = ca * (cb * at[3] + sb * at[4]) - sa * at[5]
    h_p = cb * at[4] - sb * at[3]
    return jnp.concatenate([h_p - e_t, -h_t - e_p], axis=0)


def lanes(x, index):
    return jnp.take_along_axis(x, jnp.broadcast_to(index, x.shape), axis=1)


def kernel(
    el, kinds, scale, angles, nb, send_dom, send_part, kind, deriv, lift,
    upper, lower, spread, lift_spread,
    fields_h, metric_h, binv_h, tracep_h, trace6_h, rows6_h, cols6_h,
    out,
    fraw, metric, binv, tracep, trace6, rows6, cols6,
    fpad, own, xs, ohs, lnorm, slots, sgn, kindrow, offs, lsl, pm, sel, pooln, pool, recvn, coef,
    d3, l2, trs, ext, base, rem, remn, wt, wf, rhs, zs, pqs, rank, last, grads,
    send0, recv0, sendk, recvk, off, walk,
    in_sem, ssem0, rsem0, ssemk, rsemk,
):
    grp, dom = lax.axis_index("group"), lax.axis_index("dom")
    count = lax.axis_size("dom")
    half = count // 2
    fine = jnp.logical_and(grp == 1, dom >= half)
    coarse = jnp.logical_not(fine)
    nt = el // TILE
    shift = el.bit_length() - 1
    lines = el // SUB
    steps = nt - 1 + kinds - 1
    has_prev, has_next = dom > 0, dom < count - 1
    fine_prev = jnp.logical_and(fine, dom > half)
    fine_next = jnp.logical_and(fine, has_next)

    loads = [
        pltpu.make_async_copy(a, b, in_sem.at[i])
        for i, (a, b) in enumerate((
            (fields_h, fraw), (tracep_h, tracep), (cols6_h, cols6), (binv_h, binv),
            (trace6_h, trace6), (rows6_h, rows6), (metric_h, metric),
        ))
    ]
    for load in loads:
        load.start()

    barrier = pltpu.get_barrier_semaphore()

    @pl.when(has_prev)
    def _():
        pl.semaphore_signal(barrier, inc=1, device_id={"dom": dom - 1})

    @pl.when(has_next)
    def _():
        pl.semaphore_signal(barrier, inc=1, device_id={"dom": dom + 1})

    pl.semaphore_signal(barrier, inc=1, device_id={"group": 1 - grp})

    targets = ({"dom": dom - 1}, {"dom": dom + 1}, {"group": 1 - grp})
    lands = (1, 0, 2)
    first = [
        pltpu.make_async_remote_copy(
            src_ref=send0.at[i], dst_ref=recv0.at[lands[i]],
            send_sem=ssem0.at[i], recv_sem=rsem0.at[lands[i]], device_id=targets[i],
        )
        for i in range(3)
    ]

    def later(no):
        return [
            pltpu.make_async_remote_copy(
                src_ref=sendk.at[no - 1, i], dst_ref=recvk.at[no - 1, lands[i]],
                send_sem=ssemk.at[no - 1, i], recv_sem=rsemk.at[no - 1, lands[i]],
                device_id=targets[i],
            )
            for i in range(2)
        ]

    polar, azimuth = angles[0], angles[1]
    parts = (jnp.sin(polar), jnp.cos(polar), jnp.sin(azimuth), jnp.cos(azimuth))
    own[...] = jnp.zeros_like(own)
    for f in range(4):
        for i in range(4):
            own[f * 8 + i : f * 8 + i + 1, :] = parts[i][f : f + 1, :]
        own[f * 8 + 4 : f * 8 + 5, :] = 0.5 * scale[f : f + 1, :]
    lists = jnp.concatenate([send_dom[0:1, :], send_dom[1:2, :], send_part[...]], axis=1)
    down = lax.broadcasted_iota(i32, (el, 3 * SUB), 0)
    ohs[...] = jnp.where(down == (lists & (el - 1)), 1.0, 0.0).astype(bf16)
    @pl.when(fine)
    def _():
        def square(row):
            return jnp.concatenate([row[:, i * SUB : (i + 1) * SUB] for i in range(lines)], axis=0)

        def line(sq):
            return jnp.concatenate([sq[i : i + 1] for i in range(lines)], axis=1)

        faces = [square(nb[f : f + 1, :]) for f in range(4)]
        which = square(kind[...])
        edge = functools.reduce(
            jnp.logical_or,
            [jnp.logical_and(n >= 4 * el, n < 4 * el + 2 * SUB) for n in faces],
        )
        group = jnp.where(edge, 0, which)
        masks = jnp.concatenate(
            [jnp.where(group == k, 1.0, 0.0) for k in range(kinds + 1)], axis=0
        )
        pre = dot(masks.astype(bf16), upper[...])
        before = dot(lower[...], pre[:, SUB:].astype(bf16))
        ranks = masks * (pre[:, :SUB] + before)
        pos = sum(ranks[k * lines : (k + 1) * lines] for k in range(kinds + 1))
        offs[...] = before.astype(i32)
        for k in range(kinds):
            off[k] = offs[(k + 1) * lines, 0]
        off[kinds] = jnp.int32(el)
        t, k = jnp.int32(1), jnp.int32(1)
        seen = [jnp.int32(-1)] * nt
        for s in range(steps):
            lo, hi = off[k - 1], off[k]
            walk[0, s] = t
            walk[1, s] = k - 1
            walk[2, s] = lo - t * TILE
            walk[3, s] = hi - t * TILE
            seen = [n + jnp.where(t <= i, 1, 0) for i, n in enumerate(seen)]
            stay = jnp.logical_and(hi <= (t + 1) * TILE, k < kinds)
            k, t = jnp.where(stay, k + 1, k), jnp.where(stay, t, jnp.minimum(t + 1, nt - 1))
        for i in range(nt):
            walk[4, i] = jnp.clip(seen[i], 0, steps - 1)

        def lookup(e):
            lane, row = e & (SUB - 1), e >> (SUB.bit_length() - 1)
            res = jnp.zeros((lines, SUB), f32)
            for r in range(lines):
                table = jnp.broadcast_to(pos[r : r + 1], (lines, SUB))
                res = jnp.where(row == r, jnp.take_along_axis(table, lane, axis=1), res)
            return res.astype(i32)

        place = pos.astype(i32)
        for f in range(4):
            n = faces[f]
            inner = (n >> shift) * el + lookup(n & (el - 1))
            m = jnp.where(n < 0, f * el + place, jnp.where(n >= 4 * el, n, inner))
            flag = 2 * which + jnp.where(n < 0, 1, 0)
            for i, v in enumerate((m >> 6, m & 63, flag)):
                own[f * 8 + 5 + i : f * 8 + 6 + i, :] = line(v.astype(f32))
        mine = jnp.concatenate([send_dom[...]] * (lines // 2), axis=0)
        lsl[...] = (mine >> shift) * TILE + lookup(mine & (el - 1))

        row = line(place)
        rank[...] = row
        for i in range(nt):
            down = lax.broadcasted_iota(i32, (TILE, el), 0) + i * TILE
            pm[i * TILE : (i + 1) * TILE, :] = jnp.where(down == row, 1.0, 0.0).astype(bf16)

    xs[2 * HB : 2 * HB + 32, :], xs[2 * HB + 32 : 2 * HB + 64, :] = split(own[...])

    loads[0].wait()
    for c in range(NC):
        fpad[c * RP + 32 : (c + 1) * RP, :] = jnp.zeros((8, el), f32)
        fpad[c * RP : c * RP + NP, :] = fraw[c]
    xs[0:HB, :], xs[HB : 2 * HB, :] = split(fpad[...])
    loads[1].wait()
    y = dot(xs[...], ohs[...])
    at_list = y[2 * HB : 2 * HB + 32] + y[2 * HB + 32 : 2 * HB + 64]
    face = lists >> shift
    mine = at_list[0:8]
    for f in range(1, 4):
        mine = jnp.where(face == f, at_list[f * 8 : (f + 1) * 8], mine)
    lnorm[...] = mine
    t = dot(tracep[...], stacked(y[0:HB] + y[HB : 2 * HB]))
    for c in range(NC):
        v = t[c * 4 * FP : c * 4 * FP + FP]
        for f in range(1, 4):
            v = jnp.where(face == f, t[(c * 4 + f) * FP : (c * 4 + f + 1) * FP], v)
        for i in range(3):
            send0[i, c * FP : (c + 1) * FP, :] = v[:, i * SUB : (i + 1) * SUB]
    for i in range(3):
        send0[i, NC * FP : MSG, :] = mine[:, i * SUB : (i + 1) * SUB]

    for load in loads[2:]:
        load.wait()

    @pl.when(fine)
    def _():
        for k in range(kinds):
            b2 = dot(binv[k], cols6[...]).astype(bf16)
            a = dot(trace6[...], b2).astype(bf16)
            b = dot(rows6[...], b2).astype(bf16)
            for i in range(2):
                wt[k, :, i * KB : (i + 1) * KB] = a
                wf[k, :, i * KB : (i + 1) * KB] = b

    pl.semaphore_wait(barrier, 1 + has_prev.astype(i32) + has_next.astype(i32))

    @pl.when(has_prev)
    def _():
        first[0].start()

    @pl.when(has_next)
    def _():
        first[1].start()

    first[2].start()

    @pl.when(coarse)
    def _():
        for f in range(4):
            row = nb[f : f + 1, :]
            lane = lax.broadcasted_iota(i32, (1, el), 1)
            slots[f : f + 1, :] = jnp.where(row < 0, lane + f * el, row)
            sgn[f : f + 1, :] = jnp.where(row < 0, -1.0, 1.0)

    @pl.when(fine)
    def _():
        y = lax.dot_general(
            xs[...], pm[...], (((1,), (1,)), ((), ())), preferred_element_type=f32
        )
        fpad[...] = y[0:HB] + y[HB : 2 * HB]
        own[...] = y[2 * HB : 2 * HB + 32] + y[2 * HB + 32 : 2 * HB + 64]
        for f in range(4):
            at = f * 8 + 5
            slots[f : f + 1, :] = (own[at : at + 1, :] * 64 + own[at + 1 : at + 2, :]).astype(i32)
            flag = own[at + 2 : at + 3, :].astype(i32)
            sgn[f : f + 1, :] = jnp.where((flag & 1) == 1, -1.0, 1.0)
            if f == 0:
                kindrow[...] = flag >> 1

    def pick(y, f, rows, total):
        which = slots[f : f + 1, :] >> (TILE.bit_length() - 1)
        for h in range(4 * nt):
            total = jnp.where(which == h, y[h * rows : (h + 1) * rows], total)
        return total

    def gather_direct(tiles, under, dest):
        for f in range(4 - DIRECT, 4):
            for j in range(lines):
                cols = slice(j * SUB, (j + 1) * SUB)
                at = slots[f : f + 1, cols]
                total = jnp.zeros((2 * FP, SUB), f32) if under is None else under[f, :, cols]
                for t in tiles:
                    for g in range(4):
                        for i in range(TILE // SUB):
                            h = g * lines + t * (TILE // SUB) + i
                            x = lanes(pqs[t, g, :, i * SUB : (i + 1) * SUB], at & (SUB - 1))
                            total = jnp.where((at >> (SUB.bit_length() - 1)) == h, x, total)
                dest[f, :, cols] = total

    def gather(source, rows, dest, under=None, faces=4):
        for f in range(faces):
            s = sel[:, f * el : (f + 1) * el]
            y = dot(source[...], jnp.concatenate([s, s], axis=0))
            dest[f] = pick(y, f, rows, jnp.zeros((rows, el), f32) if under is None else under[f])

    def place_at(dest, source, f, j, sources):
        s = slots[f : f + 1, j * SUB : (j + 1) * SUB]
        v = dest[f, :, j * SUB : (j + 1) * SUB]
        for i in sources:
            here = (s >> (SUB.bit_length() - 1)) == 4 * el // SUB + i
            v = jnp.where(here, lanes(source[i], s & (SUB - 1)), v)
        dest[f, :, j * SUB : (j + 1) * SUB] = v

    def fill(t, at_rows):
        cols = slice(t * TILE, (t + 1) * TILE)
        for f in range(4):
            at = [at_rows(c * 4 * FP + f * FP) for c in range(NC)]
            sign = sgn[f : f + 1, cols]
            at[:3] = [sign * e for e in at[:3]]
            pq = project(at, [recvn[f, i : i + 1, cols] for i in range(4)])
            hi, lo = split(pq)
            h = f * nt + t
            pool[h * 2 * FP : (h + 1) * 2 * FP, 0:TILE] = hi
            pool[h * 2 * FP : (h + 1) * 2 * FP, TILE : 2 * TILE] = lo
            pqs[t, f] = pq

    down = lax.broadcasted_iota(i32, (TILE, el), 0)
    for f in range(4):
        low = slots[f : f + 1, :] & (TILE - 1)
        sel[:, f * el : (f + 1) * el] = jnp.where(down == low, 1.0, 0.0).astype(bf16)
    for f in range(4):
        for t in range(0, nt, 2):
            both = [own[f * 8 : f * 8 + 8, (t + i) * TILE : (t + i + 1) * TILE] for i in range(2)]
            h = (f * nt + t) * 8
            pooln[h : h + 16, 0:TILE], pooln[h : h + 16, TILE : 2 * TILE] = split(
                jnp.concatenate(both, axis=0)
            )
        sa, ca, sb, cb, w = (own[f * 8 + i : f * 8 + i + 1, :] for i in range(5))
        for i, row in enumerate((w * ca * cb, w * ca * sb, -w * sa, -w * sb, w * cb)):
            coef[f, i : i + 1, :] = row
    gather(pooln, 8, recvn)
    for t in range(nt):
        z = dot(tracep[...], stacked(fpad[:, t * TILE : (t + 1) * TILE]))
        trs[t] = z
        fill(t, lambda r: z[r : r + FP])
    gather_direct(range(nt), None, ext)
    gather(pool, 2 * FP, ext, None, 4 - DIRECT)

    l2[...] = jnp.zeros_like(l2)
    hi, lo = split(lift[...])
    for i in range(4):
        l2[i * RP : i * RP + NP, :] = dot(lo if i % 2 else hi, lift_spread[i])
    @pl.when(coarse)
    def _():
        d3[...] = jnp.zeros_like(d3)
        for b in range(3):
            hi, lo = split(deriv[b])
            d3[b * RP : b * RP + NP, :] = dot(hi, spread[0]) + dot(lo, spread[1])
        db = d3[...].astype(bf16)
        for c in range(NC):
            x = fpad[c * RP : (c + 1) * RP, :]
            hi = x.astype(bf16).astype(f32)
            grads[c] = dot(db, jnp.concatenate([hi, x - hi, hi], axis=0).astype(bf16))

    def arrive(i):
        at = [recv0[i, c * FP : (c + 1) * FP, :] for c in range(NC)]
        rem[i] = project(at, [lnorm[r : r + 1, i * SUB : (i + 1) * SUB] for r in range(4)])
        remn[i] = recv0[i, NC * FP : MSG, :]

    rem[...] = jnp.zeros_like(rem)
    remn[...] = jnp.zeros_like(remn)

    @pl.when(has_prev)
    def _():
        first[0].wait_send()
        first[1].wait_recv()
        arrive(0)

    @pl.when(has_next)
    def _():
        first[1].wait_send()
        first[0].wait_recv()
        arrive(1)

    first[2].wait()
    arrive(2)

    def lifted(t, pq):
        cols = slice(t * TILE, (t + 1) * TILE)
        for pair in range(NC // 2):
            pieces = []
            for c in (2 * pair, 2 * pair + 1):
                rows = []
                k = c % 3
                for f in range(4):
                    p, q = pq[f][:FP], pq[f][FP:]
                    a, b = (p, q) if c < 3 else (q, -p)
                    row = coef[f, k : k + 1, cols] * a
                    if k < 2:
                        row = row + coef[f, 3 + k : 4 + k, cols] * b
                    rows.append(row)
                pieces.extend(split(jnp.concatenate(rows, axis=0)))
            y = dot(l2[...].astype(bf16), jnp.concatenate(pieces, axis=0))
            for i in range(2):
                at = 2 * i * RP
                yield 2 * pair + i, y[at : at + RP] + y[at + RP : at + 2 * RP]

    @pl.when(coarse)
    def _():
        for f in range(4):
            for j in range(lines):
                place_at(ext, rem, f, j, range(3))
        for t in range(nt):
            cols = slice(t * TILE, (t + 1) * TILE)

            def along(c, axis):
                return sum(
                    metric[3 * axis + b : 3 * axis + b + 1, cols]
                    * grads[c, b * RP : (b + 1) * RP, cols]
                    for b in range(3)
                )

            pq = []
            for f in range(4):
                at = [trs[t, (c * 4 + f) * FP : (c * 4 + f + 1) * FP, :] for c in range(NC)]
                n = [own[f * 8 + i : f * 8 + i + 1, cols] for i in range(4)]
                pq.append(project(at, n) - ext[f, :, cols])
            for c, s in lifted(t, pq):
                k, other = c % 3, 3 - 3 * (c // 3)
                one, two = (k + 1) % 3, (k + 2) % 3
                curl = along(other + two, one) - along(other + one, two)
                vol = curl if c < 3 else -curl
                value = fpad[c * RP : (c + 1) * RP, cols] + STEP * (vol + s)
                out[c, :, cols] = value[:NP]

    @pl.when(fine)
    def _():
        for f in range(4):
            for j in range(lines):
                edge = j < TILE // SUB
                place_at(ext, rem, f, j, range(3) if edge else (2,))
                if edge:
                    place_at(recvn, remn, f, j, range(2))
            base[f] = jnp.where(slots[f : f + 1, :] >= 4 * el, ext[f], 0.0)

        def right_side(t):
            cols = slice(t * TILE, (t + 1) * TILE)
            terms = [
                fpad[c * RP : (c + 1) * RP, cols] - STEP * s
                for c, s in lifted(t, [ext[f, :, cols] for f in range(4)])
            ]
            rhs[t] = stacked(jnp.concatenate(terms, axis=0))

        def edge_blocks(weights, rows):
            z = dot(weights[0], rhs[0])
            for k in range(1, kinds):
                z = jnp.where(kindrow[:, 0:TILE] == k + 1, dot(weights[k], rhs[0]), z)
            zs[0, 0:rows, :] = z

        def inside(row, at, size):
            return jnp.clip(walk[row, at], 0, size - 1)

        def inner_blocks(weights, rows):
            lane = lax.broadcasted_iota(i32, (1, TILE), 1)
            for s in range(steps):
                y = dot(weights[inside(1, s, kinds)], rhs[inside(0, s, nt)])
                if s:
                    here = jnp.logical_and(lane >= walk[2, s], lane < walk[3, s])
                    y = jnp.where(here, y, zs[s, 0:rows, :])
                zs[1 + s, 0:rows, :] = y

        def sweep(no, carry):
            right_side(0)
            edge_blocks(wt, TR)
            for t in range(1, nt):
                right_side(t)
            fill(0, lambda r: zs[0, r : r + FP, :])
            for i in range(2):
                at = lsl[i : i + 1, :]
                v = jnp.zeros((2 * FP, SUB), f32)
                for h in range(4 * TILE // SUB):
                    f, j = h // (TILE // SUB), h % (TILE // SUB)
                    x = lanes(pqs[0, f, :, j * SUB : (j + 1) * SUB], at & (SUB - 1))
                    v = jnp.where((at >> (SUB.bit_length() - 1)) == h, x, v)
                sendk[no - 1, i] = v
            copies = later(no)

            @pl.when(fine_prev)
            def _():
                copies[0].start()

            @pl.when(fine_next)
            def _():
                copies[1].start()

            inner_blocks(wt, TR)
            for t in range(1, nt):
                end = inside(4, t, steps)
                fill(t, lambda r: zs[1 + end, r : r + FP, :])
            gather_direct(range(nt), base, ext)
            gather(pool, 2 * FP, ext, base, 4 - DIRECT)

            @pl.when(fine_prev)
            def _():
                copies[0].wait_send()
                copies[1].wait_recv()
                rem[0] = recvk[no - 1, 0]

            @pl.when(fine_next)
            def _():
                copies[1].wait_send()
                copies[0].wait_recv()
                rem[1] = recvk[no - 1, 1]

            for f in range(4):
                for j in range(TILE // SUB):
                    place_at(ext, rem, f, j, range(2))
            return carry

        lax.fori_loop(1, SWEEPS, sweep, 0)
        for t in range(nt):
            right_side(t)
        edge_blocks(wf, HB)
        inner_blocks(wf, HB)
        part = NC - SWAPPED
        for t in range(nt):
            at = 1 + inside(4, t, steps) if t else 0
            cols = slice(t * TILE, (t + 1) * TILE)
            z = zs[at, 0:HB, :]
            xs[0 : part * RP, cols], xs[HB : HB + part * RP, cols] = split(z[: part * RP])
            last[:, cols] = z[part * RP :]
        for j in range(lines):
            at = rank[:, j * SUB : (j + 1) * SUB]
            total = jnp.zeros((SWAPPED * RP, SUB), f32)
            for h in range(lines):
                x = lanes(last[:, h * SUB : (h + 1) * SUB], at & (SUB - 1))
                total = jnp.where((at >> (SUB.bit_length() - 1)) == h, x, total)
            for c in range(SWAPPED):
                out[part + c, :, j * SUB : (j + 1) * SUB] = total[c * RP : c * RP + NP]
        x = jnp.concatenate([xs[0 : part * RP, :], xs[HB : HB + part * RP, :]], axis=0)
        y = dot(x, pm[...])
        for c in range(part):
            at = c * RP
            out[c] = y[at : at + NP] + y[part * RP + at : part * RP + at + NP]


def shards(*args):
    (fields, metric, scale, angles, nb, send_dom, send_part, kind, deriv, lift, binv) = args
    el = fields.shape[2]
    kinds = binv.shape[0]
    nt, lines = el // TILE, el // SUB
    steps = nt - 1 + kinds - 1
    small, large = constants(el, kinds)
    near = [
        scale, angles, nb, send_dom, send_part.reshape(1, -1), kind.reshape(1, -1), deriv, lift,
        *small,
    ]
    far = [fields, metric, binv, *large]
    vmem, dma = pltpu.VMEM, pltpu.SemaphoreType.DMA
    return pl.pallas_call(
        functools.partial(kernel, el, kinds),
        out_shape=pltpu.VMEM(fields.shape, f32),
        in_specs=[pl.BlockSpec(memory_space=vmem)] * len(near)
        + [pl.BlockSpec(memory_space=pl.ANY)] * len(far),
        out_specs=pl.BlockSpec(memory_space=vmem),
        scratch_shapes=[
            *[vmem(a.shape, a.dtype) for a in far],
            vmem((HB, el), f32),
            vmem((32, el), f32),
            vmem((2 * HB + 64, el), bf16),
            vmem((el, 3 * SUB), bf16),
            vmem((8, 3 * SUB), f32),
            vmem((4, el), i32),
            vmem((4, el), f32),
            vmem((1, el), i32),
            vmem(((kinds + 1) * lines, SUB), i32),
            vmem((lines, SUB), i32),
            vmem((el, el), bf16),
            vmem((TILE, 4 * el), bf16),
            vmem((4 * nt * 8, 2 * TILE), bf16),
            vmem((4 * nt * 2 * FP, 2 * TILE), bf16),
            vmem((4, 8, el), f32),
            vmem((4, 8, el), f32),
            vmem((3 * RP, 3 * RP), f32),
            vmem((4 * RP, 16 * FP), f32),
            vmem((nt, TR, TILE), f32),
            vmem((4, 2 * FP, el), f32),
            vmem((4, 2 * FP, el), f32),
            vmem((3, 2 * FP, SUB), f32),
            vmem((3, 8, SUB), f32),
            vmem((kinds, TR, 2 * KB), bf16),
            vmem((kinds, HB, 2 * KB), bf16),
            vmem((nt, 2 * KB, TILE), bf16),
            vmem((1 + steps, TR, TILE), f32),
            vmem((nt, 4, 2 * FP, TILE), f32),
            vmem((1, el), i32),
            vmem((SWAPPED * RP, el), f32),
            vmem((NC, 3 * RP, el), f32),
            vmem((3, MSG, SUB), f32),
            vmem((3, MSG, SUB), f32),
            vmem((SWEEPS - 1, 2, 2 * FP, SUB), f32),
            vmem((SWEEPS - 1, 2, 2 * FP, SUB), f32),
            pltpu.SMEM((kinds + 1,), i32),
            pltpu.SMEM((5, max(steps, nt)), i32),
            dma((len(far),)), dma((3,)), dma((3,)), dma((SWEEPS - 1, 2)), dma((SWEEPS - 1, 2)),
        ],
        compiler_params=pltpu.CompilerParams(
            collective_id=0, has_side_effects=True, vmem_limit_bytes=56 * 2**20
        ),
    )(*near, *far)


def solution(mesh):
    both = ("group", "dom")
    in_specs = (
        P(None, None, both), P(None, both), P(None, both), P(None, None, both), P(None, both),
        P(None, both), P(both), P(both), P(), P(), P(),
    )
    return jax.shard_map(
        shards, mesh=mesh, in_specs=in_specs, out_specs=P(None, None, both), check_vma=False
    )
```

```python
import functools

import jax
import jax.numpy as jnp
import numpy as np
from jax import lax
from jax.experimental import pallas as pl
from jax.experimental.pallas import tpu as pltpu
from jax.sharding import PartitionSpec as P

SWEEPS = 4
STEP = 0.2
NC, NP, NFP = 6, 35, 15
RP = 40
HB = NC * RP
KB = 256
FP = 16
TR = NC * 4 * FP
TILE = 256
SUB = 128
DIRECT = 1
EXTRA = 2
SWAPPED = 2
MSG = NC * FP + 8
f32, bf16, i32 = jnp.float32, jnp.bfloat16, jnp.int32


def face_nodes():
    lattice = [(r, s, t) for r in range(5) for s in range(5 - r) for t in range(5 - r - s)]
    tests = [
        lambda p: p[2] == 0,
        lambda p: p[1] == 0,
        lambda p: p[0] == 0,
        lambda p: sum(p) == 4,
    ]
    return [[i for i, p in enumerate(lattice) if test(p)] for test in tests]


def constants(el, kinds):
    trace = np.zeros((4 * FP, NP), np.float32)
    for f, nodes in enumerate(face_nodes()):
        for n, node in enumerate(nodes):
            trace[f * FP + n, node] = 1
    eye6 = np.eye(NC, dtype=np.float32)
    pad = np.eye(RP, NP, dtype=np.float32)
    trace6 = np.kron(eye6, trace)
    rows6 = np.kron(eye6, pad)
    cols6 = np.zeros((NC * NP, KB), np.float32)
    cols6[:, :HB] = rows6.T
    tracep = np.tile(trace6 @ cols6, (1, 2))
    spread = np.zeros((2, NP, 3 * RP), np.float32)
    for i in range(NP):
        spread[0, i, i] = spread[0, i, RP + i] = spread[1, i, 2 * RP + i] = 1
    lift_spread = np.zeros((4, 4 * NFP, 16 * FP), np.float32)
    for f in range(4):
        for n in range(NFP):
            row, col = f * NFP + n, f * FP + n
            for i in range(2):
                lift_spread[2 * i, row, 8 * FP * i + col] = 1
                lift_spread[2 * i, row, 8 * FP * i + 4 * FP + col] = 1
                lift_spread[2 * i + 1, row, 8 * FP * i + col] = 1
    upper = np.concatenate([np.triu(np.ones((SUB, SUB)), 1), np.ones((SUB, SUB))], axis=1)
    lines = (kinds + 1) * (el // SUB)
    lower = np.tril(np.ones((lines, lines)), -1)
    small = [jnp.asarray(a, bf16) for a in (upper, lower, spread, lift_spread)]
    large = [jnp.asarray(a, bf16) for a in (tracep, trace6, rows6, cols6)]
    return small, large


def split(x):
    hi = x.astype(bf16)
    return hi, (x - hi.astype(f32)).astype(bf16)


def dot(a, b):
    return jnp.dot(a, b, preferred_element_type=f32)


def stacked(x):
    hi, lo = split(x)
    gap = jnp.zeros((KB - HB, x.shape[1]), bf16)
    return jnp.concatenate([hi, gap, lo, gap], axis=0)


def project(at, n):
    sa, ca, sb, cb = n
    e_t = ca * (cb * at[0] + sb * at[1]) - sa * at[2]
    e_p = cb * at[1] - sb * at[0]
    h_t = ca * (cb * at[3] + sb * at[4]) - sa * at[5]
    h_p = cb * at[4] - sb * at[3]
    return jnp.concatenate([h_p - e_t, -h_t - e_p], axis=0)


def lanes(x, index):
    return jnp.take_along_axis(x, jnp.broadcast_to(index, x.shape), axis=1)


def kernel(
    el, kinds, scale, angles, nb, send_dom, send_part, kind, deriv, lift,
    upper, lower, spread, lift_spread,
    fields_h, metric_h, binv_h, tracep_h, trace6_h, rows6_h, cols6_h,
    out,
    fraw, metric, binv, tracep, trace6, rows6, cols6,
    fpad, own, xs, lnorm, slots, sgn, kindrow, offs, lsl, pm, sel, pooln, pool, recvn, coef,
    d3, l2, trs, ext, base, rem, remn, wt, wf, rhs, zs, pqs, rank, last, grads,
    send0, recv0, sendk, recvk, off, walk,
    in_sem, ssem0, rsem0, ssemk, rsemk,
):
    grp, dom = lax.axis_index("group"), lax.axis_index("dom")
    count = lax.axis_size("dom")
    half = count // 2
    fine = jnp.logical_and(grp == 1, dom >= half)
    coarse = jnp.logical_not(fine)
    nt = el // TILE
    shift = el.bit_length() - 1
    lines = el // SUB
    steps = nt - 1 + kinds - 1
    has_prev, has_next = dom > 0, dom < count - 1
    fine_prev = jnp.logical_and(fine, dom > half)
    fine_next = jnp.logical_and(fine, has_next)

    loads = [
        pltpu.make_async_copy(a, b, in_sem.at[i])
        for i, (a, b) in enumerate((
            (fields_h, fraw), (tracep_h, tracep), (cols6_h, cols6), (binv_h, binv),
            (trace6_h, trace6), (rows6_h, rows6), (metric_h, metric),
        ))
    ]
    for load in loads:
        load.start()

    barrier = pltpu.get_barrier_semaphore()

    @pl.when(has_prev)
    def _():
        pl.semaphore_signal(barrier, inc=1, device_id={"dom": dom - 1})

    @pl.when(has_next)
    def _():
        pl.semaphore_signal(barrier, inc=1, device_id={"dom": dom + 1})

    pl.semaphore_signal(barrier, inc=1, device_id={"group": 1 - grp})

    targets = ({"dom": dom - 1}, {"dom": dom + 1}, {"group": 1 - grp})
    lands = (1, 0, 2)
    first = [
        pltpu.make_async_remote_copy(
            src_ref=send0.at[i], dst_ref=recv0.at[lands[i]],
            send_sem=ssem0.at[i], recv_sem=rsem0.at[lands[i]], device_id=targets[i],
        )
        for i in range(3)
    ]

    def later(no):
        return [
            pltpu.make_async_remote_copy(
                src_ref=sendk.at[no - 1, i], dst_ref=recvk.at[no - 1, lands[i]],
                send_sem=ssemk.at[no - 1, i], recv_sem=rsemk.at[no - 1, lands[i]],
                device_id=targets[i],
            )
            for i in range(2)
        ]

    polar, azimuth = angles[0], angles[1]
    parts = (jnp.sin(polar), jnp.cos(polar), jnp.sin(azimuth), jnp.cos(azimuth))
    own[...] = jnp.zeros_like(own)
    for f in range(4):
        for i in range(4):
            own[f * 8 + i : f * 8 + i + 1, :] = parts[i][f : f + 1, :]
        own[f * 8 + 4 : f * 8 + 5, :] = 0.5 * scale[f : f + 1, :]
    lists = jnp.concatenate([send_dom[0:1, :], send_dom[1:2, :], send_part[...]], axis=1)
    @pl.when(fine)
    def _():
        def square(row):
            return jnp.concatenate([row[:, i * SUB : (i + 1) * SUB] for i in range(lines)], axis=0)

        def line(sq):
            return jnp.concatenate([sq[i : i + 1] for i in range(lines)], axis=1)

        faces = [square(nb[f : f + 1, :]) for f in range(4)]
        which = square(kind[...])
        edge = functools.reduce(
            jnp.logical_or,
            [jnp.logical_and(n >= 4 * el, n < 4 * el + 2 * SUB) for n in faces],
        )
        group = jnp.where(edge, 0, which)
        masks = jnp.concatenate(
            [jnp.where(group == k, 1.0, 0.0) for k in range(kinds + 1)], axis=0
        )
        pre = dot(masks.astype(bf16), upper[...])
        before = dot(lower[...], pre[:, SUB:].astype(bf16))
        ranks = masks * (pre[:, :SUB] + before)
        pos = sum(ranks[k * lines : (k + 1) * lines] for k in range(kinds + 1))
        offs[...] = before.astype(i32)
        for k in range(kinds):
            off[k] = offs[(k + 1) * lines, 0]
        off[kinds] = jnp.int32(el)
        t, k = jnp.int32(1), jnp.int32(1)
        seen = [jnp.int32(-1)] * nt
        for s in range(steps):
            lo, hi = off[k - 1], off[k]
            walk[0, s] = t
            walk[1, s] = k - 1
            walk[2, s] = lo - t * TILE
            walk[3, s] = hi - t * TILE
            seen = [n + jnp.where(t <= i, 1, 0) for i, n in enumerate(seen)]
            stay = jnp.logical_and(hi <= (t + 1) * TILE, k < kinds)
            k, t = jnp.where(stay, k + 1, k), jnp.where(stay, t, jnp.minimum(t + 1, nt - 1))
        for i in range(nt):
            walk[4, i] = jnp.clip(seen[i], 0, steps - 1)

        def lookup(e):
            lane, row = e & (SUB - 1), e >> (SUB.bit_length() - 1)
            res = jnp.zeros((lines, SUB), f32)
            for r in range(lines):
                table = jnp.broadcast_to(pos[r : r + 1], (lines, SUB))
                res = jnp.where(row == r, jnp.take_along_axis(table, lane, axis=1), res)
            return res.astype(i32)

        place = pos.astype(i32)
        for f in range(4):
            n = faces[f]
            inner = (n >> shift) * el + lookup(n & (el - 1))
            m = jnp.where(n < 0, f * el + place, jnp.where(n >= 4 * el, n, inner))
            flag = 2 * which + jnp.where(n < 0, 1, 0)
            for i, v in enumerate((m >> 6, m & 63, flag)):
                own[f * 8 + 5 + i : f * 8 + 6 + i, :] = line(v.astype(f32))
        mine = jnp.concatenate([send_dom[...]] * (lines // 2), axis=0)
        lsl[...] = (mine >> shift) * TILE + lookup(mine & (el - 1))

        row = line(place)
        rank[...] = row
        for i in range(nt):
            down = lax.broadcasted_iota(i32, (TILE, el), 0) + i * TILE
            pm[i * TILE : (i + 1) * TILE, :] = jnp.where(down == row, 1.0, 0.0).astype(bf16)

    loads[0].wait()
    for c in range(NC):
        fpad[c * RP + 32 : (c + 1) * RP, :] = jnp.zeros((8, el), f32)
        fpad[c * RP : c * RP + NP, :] = fraw[c]
    for load in loads[1:]:
        load.wait()

    def listed(source):
        parts = []
        for i in range(3):
            at = lists[:, i * SUB : (i + 1) * SUB] & (el - 1)
            v = jnp.zeros((source.shape[0], SUB), f32)
            for h in range(lines):
                x = lanes(source[:, h * SUB : (h + 1) * SUB], at & (SUB - 1))
                v = jnp.where((at >> (SUB.bit_length() - 1)) == h, x, v)
            parts.append(v)
        return jnp.concatenate(parts, axis=1)

    at_list = listed(own)
    for k in range(kinds):
        b2 = dot(binv[k], cols6[...]).astype(bf16)
        a = dot(trace6[...], b2).astype(bf16)
        b = dot(rows6[...], b2).astype(bf16)
        for i in range(2):
            wt[k, :, i * KB : (i + 1) * KB] = a
            wf[k, :, i * KB : (i + 1) * KB] = b
    face = lists >> shift
    mine = at_list[0:8]
    for f in range(1, 4):
        mine = jnp.where(face == f, at_list[f * 8 : (f + 1) * 8], mine)
    lnorm[...] = mine
    t = dot(tracep[...], stacked(listed(fpad)))
    for c in range(NC):
        v = t[c * 4 * FP : c * 4 * FP + FP]
        for f in range(1, 4):
            v = jnp.where(face == f, t[(c * 4 + f) * FP : (c * 4 + f + 1) * FP], v)
        for i in range(3):
            send0[i, c * FP : (c + 1) * FP, :] = v[:, i * SUB : (i + 1) * SUB]
    for i in range(3):
        send0[i, NC * FP : MSG, :] = mine[:, i * SUB : (i + 1) * SUB]

    pl.semaphore_wait(barrier, 1 + has_prev.astype(i32) + has_next.astype(i32))

    @pl.when(has_prev)
    def _():
        first[0].start()

    @pl.when(has_next)
    def _():
        first[1].start()

    first[2].start()

    @pl.when(coarse)
    def _():
        for f in range(4):
            row = nb[f : f + 1, :]
            lane = lax.broadcasted_iota(i32, (1, el), 1)
            slots[f : f + 1, :] = jnp.where(row < 0, lane + f * el, row)
            sgn[f : f + 1, :] = jnp.where(row < 0, -1.0, 1.0)

    @pl.when(fine)
    def _():
        xs[0:HB, :], xs[HB : 2 * HB, :] = split(fpad[...])
        xs[2 * HB : 2 * HB + 32, :], xs[2 * HB + 32 : 2 * HB + 64, :] = split(own[...])
        y = lax.dot_general(
            xs[...], pm[...], (((1,), (1,)), ((), ())), preferred_element_type=f32
        )
        fpad[...] = y[0:HB] + y[HB : 2 * HB]
        own[...] = y[2 * HB : 2 * HB + 32] + y[2 * HB + 32 : 2 * HB + 64]
        for f in range(4):
            at = f * 8 + 5
            slots[f : f + 1, :] = (own[at : at + 1, :] * 64 + own[at + 1 : at + 2, :]).astype(i32)
            flag = own[at + 2 : at + 3, :].astype(i32)
            sgn[f : f + 1, :] = jnp.where((flag & 1) == 1, -1.0, 1.0)
            if f == 0:
                kindrow[...] = flag >> 1

    def pick(y, f, rows, total):
        which = slots[f : f + 1, 0 : total.shape[1]] >> (TILE.bit_length() - 1)
        for h in range(4 * nt):
            total = jnp.where(which == h, y[h * rows : (h + 1) * rows], total)
        return total

    def gather_direct(tiles, under, dest):
        for f in range(2, 4):
            for j in range(0 if f == 3 else lines - EXTRA, lines):
                cols = slice(j * SUB, (j + 1) * SUB)
                at = slots[f : f + 1, cols]
                total = jnp.zeros((2 * FP, SUB), f32) if under is None else under[f, :, cols]
                for t in tiles:
                    for g in range(4):
                        for i in range(TILE // SUB):
                            h = g * lines + t * (TILE // SUB) + i
                            x = lanes(pqs[t, g, :, i * SUB : (i + 1) * SUB], at & (SUB - 1))
                            total = jnp.where((at >> (SUB.bit_length() - 1)) == h, x, total)
                dest[f, :, cols] = total

    def gather(source, rows, dest, under=None, faces=4):
        for f in range(faces):
            n = el - EXTRA * SUB if f == 2 and faces < 4 else el
            s = sel[:, f * el : f * el + n]
            y = dot(source[...], jnp.concatenate([s, s], axis=0))
            total = jnp.zeros((rows, n), f32) if under is None else under[f, :, 0:n]
            dest[f, :, 0:n] = pick(y, f, rows, total)

    def place_at(dest, source, f, j, sources):
        s = slots[f : f + 1, j * SUB : (j + 1) * SUB]
        v = dest[f, :, j * SUB : (j + 1) * SUB]
        for i in sources:
            here = (s >> (SUB.bit_length() - 1)) == 4 * el // SUB + i
            v = jnp.where(here, lanes(source[i], s & (SUB - 1)), v)
        dest[f, :, j * SUB : (j + 1) * SUB] = v

    def fill(t, at_rows):
        cols = slice(t * TILE, (t + 1) * TILE)
        for f in range(4):
            at = [at_rows(c * 4 * FP + f * FP) for c in range(NC)]
            sign = sgn[f : f + 1, cols]
            at[:3] = [sign * e for e in at[:3]]
            pq = project(at, [recvn[f, i : i + 1, cols] for i in range(4)])
            hi, lo = split(pq)
            h = f * nt + t
            pool[h * 2 * FP : (h + 1) * 2 * FP, 0:TILE] = hi
            pool[h * 2 * FP : (h + 1) * 2 * FP, TILE : 2 * TILE] = lo
            pqs[t, f] = pq

    down = lax.broadcasted_iota(i32, (TILE, el), 0)
    for f in range(4):
        low = slots[f : f + 1, :] & (TILE - 1)
        sel[:, f * el : (f + 1) * el] = jnp.where(down == low, 1.0, 0.0).astype(bf16)
    for f in range(4):
        for t in range(0, nt, 2):
            both = [own[f * 8 : f * 8 + 8, (t + i) * TILE : (t + i + 1) * TILE] for i in range(2)]
            h = (f * nt + t) * 8
            pooln[h : h + 16, 0:TILE], pooln[h : h + 16, TILE : 2 * TILE] = split(
                jnp.concatenate(both, axis=0)
            )
        sa, ca, sb, cb, w = (own[f * 8 + i : f * 8 + i + 1, :] for i in range(5))
        for i, row in enumerate((w * ca * cb, w * ca * sb, -w * sa, -w * sb, w * cb)):
            coef[f, i : i + 1, :] = row
    gather(pooln, 8, recvn, None, 2)
    for f in range(2, 4):
        for j in range(lines):
            cols = slice(j * SUB, (j + 1) * SUB)
            at = slots[f : f + 1, cols]
            total = jnp.zeros((8, SUB), f32)
            for h in range(4 * lines):
                g, i = h // lines, h % lines
                x = lanes(own[g * 8 : g * 8 + 8, i * SUB : (i + 1) * SUB], at & (SUB - 1))
                total = jnp.where((at >> (SUB.bit_length() - 1)) == h, x, total)
            recvn[f, :, cols] = total
    for t in range(nt):
        z = dot(tracep[...], stacked(fpad[:, t * TILE : (t + 1) * TILE]))
        trs[t] = z
        fill(t, lambda r: z[r : r + FP])
    gather_direct(range(nt), None, ext)
    gather(pool, 2 * FP, ext, None, 4 - DIRECT)

    l2[...] = jnp.zeros_like(l2)
    hi, lo = split(lift[...])
    for i in range(4):
        l2[i * RP : i * RP + NP, :] = dot(lo if i % 2 else hi, lift_spread[i])
    @pl.when(coarse)
    def _():
        d3[...] = jnp.zeros_like(d3)
        for b in range(3):
            hi, lo = split(deriv[b])
            d3[b * RP : b * RP + NP, :] = dot(hi, spread[0]) + dot(lo, spread[1])
        db = d3[...].astype(bf16)
        for c in range(NC):
            x = fpad[c * RP : (c + 1) * RP, :]
            hi = x.astype(bf16).astype(f32)
            grads[c] = dot(db, jnp.concatenate([hi, x - hi, hi], axis=0).astype(bf16))

    def arrive(i):
        at = [recv0[i, c * FP : (c + 1) * FP, :] for c in range(NC)]
        rem[i] = project(at, [lnorm[r : r + 1, i * SUB : (i + 1) * SUB] for r in range(4)])
        remn[i] = recv0[i, NC * FP : MSG, :]

    rem[...] = jnp.zeros_like(rem)
    remn[...] = jnp.zeros_like(remn)

    @pl.when(has_prev)
    def _():
        first[0].wait_send()
        first[1].wait_recv()
        arrive(0)

    @pl.when(has_next)
    def _():
        first[1].wait_send()
        first[0].wait_recv()
        arrive(1)

    first[2].wait()
    arrive(2)

    def lifted(t, pq):
        cols = slice(t * TILE, (t + 1) * TILE)
        for pair in range(NC // 2):
            pieces = []
            for c in (2 * pair, 2 * pair + 1):
                rows = []
                k = c % 3
                for f in range(4):
                    p, q = pq[f][:FP], pq[f][FP:]
                    a, b = (p, q) if c < 3 else (q, -p)
                    row = coef[f, k : k + 1, cols] * a
                    if k < 2:
                        row = row + coef[f, 3 + k : 4 + k, cols] * b
                    rows.append(row)
                pieces.extend(split(jnp.concatenate(rows, axis=0)))
            y = dot(l2[...].astype(bf16), jnp.concatenate(pieces, axis=0))
            for i in range(2):
                at = 2 * i * RP
                yield 2 * pair + i, y[at : at + RP] + y[at + RP : at + 2 * RP]

    @pl.when(coarse)
    def _():
        for f in range(4):
            for j in range(lines):
                place_at(ext, rem, f, j, range(3))
        for t in range(nt):
            cols = slice(t * TILE, (t + 1) * TILE)

            def along(c, axis):
                return sum(
                    metric[3 * axis + b : 3 * axis + b + 1, cols]
                    * grads[c, b * RP : (b + 1) * RP, cols]
                    for b in range(3)
                )

            pq = []
            for f in range(4):
                at = [trs[t, (c * 4 + f) * FP : (c * 4 + f + 1) * FP, :] for c in range(NC)]
                n = [own[f * 8 + i : f * 8 + i + 1, cols] for i in range(4)]
                pq.append(project(at, n) - ext[f, :, cols])
            for c, s in lifted(t, pq):
                k, other = c % 3, 3 - 3 * (c // 3)
                one, two = (k + 1) % 3, (k + 2) % 3
                curl = along(other + two, one) - along(other + one, two)
                vol = curl if c < 3 else -curl
                value = fpad[c * RP : (c + 1) * RP, cols] + STEP * (vol + s)
                out[c, :, cols] = value[:NP]

    @pl.when(fine)
    def _():
        for f in range(4):
            for j in range(lines):
                edge = j < TILE // SUB
                place_at(ext, rem, f, j, range(3) if edge else (2,))
                if edge:
                    place_at(recvn, remn, f, j, range(2))
            base[f] = jnp.where(slots[f : f + 1, :] >= 4 * el, ext[f], 0.0)

        def right_side(t):
            cols = slice(t * TILE, (t + 1) * TILE)
            terms = [
                fpad[c * RP : (c + 1) * RP, cols] - STEP * s
                for c, s in lifted(t, [ext[f, :, cols] for f in range(4)])
            ]
            rhs[t] = stacked(jnp.concatenate(terms, axis=0))

        def edge_blocks(weights, rows):
            z = dot(weights[0], rhs[0])
            for k in range(1, kinds):
                z = jnp.where(kindrow[:, 0:TILE] == k + 1, dot(weights[k], rhs[0]), z)
            zs[0, 0:rows, :] = z

        def inside(row, at, size):
            return jnp.clip(walk[row, at], 0, size - 1)

        def inner_blocks(weights, rows):
            lane = lax.broadcasted_iota(i32, (1, TILE), 1)
            for s in range(steps):
                y = dot(weights[inside(1, s, kinds)], rhs[inside(0, s, nt)])
                if s:
                    here = jnp.logical_and(lane >= walk[2, s], lane < walk[3, s])
                    y = jnp.where(here, y, zs[s, 0:rows, :])
                zs[1 + s, 0:rows, :] = y

        def sweep(no, carry):
            right_side(0)
            edge_blocks(wt, TR)
            for t in range(1, nt):
                right_side(t)
            fill(0, lambda r: zs[0, r : r + FP, :])
            for i in range(2):
                at = lsl[i : i + 1, :]
                v = jnp.zeros((2 * FP, SUB), f32)
                for h in range(4 * TILE // SUB):
                    f, j = h // (TILE // SUB), h % (TILE // SUB)
                    x = lanes(pqs[0, f, :, j * SUB : (j + 1) * SUB], at & (SUB - 1))
                    v = jnp.where((at >> (SUB.bit_length() - 1)) == h, x, v)
                sendk[no - 1, i] = v
            copies = later(no)

            @pl.when(fine_prev)
            def _():
                copies[0].start()

            @pl.when(fine_next)
            def _():
                copies[1].start()

            inner_blocks(wt, TR)
            for t in range(1, nt):
                end = inside(4, t, steps)
                fill(t, lambda r: zs[1 + end, r : r + FP, :])
            gather_direct(range(nt), base, ext)
            gather(pool, 2 * FP, ext, base, 4 - DIRECT)

            @pl.when(fine_prev)
            def _():
                copies[0].wait_send()
                copies[1].wait_recv()
                rem[0] = recvk[no - 1, 0]

            @pl.when(fine_next)
            def _():
                copies[1].wait_send()
                copies[0].wait_recv()
                rem[1] = recvk[no - 1, 1]

            for f in range(4):
                for j in range(TILE // SUB):
                    place_at(ext, rem, f, j, range(2))
            return carry

        lax.fori_loop(1, SWEEPS, sweep, 0)
        for t in range(nt):
            right_side(t)
        edge_blocks(wf, HB)
        inner_blocks(wf, HB)
        part = NC - SWAPPED
        for t in range(nt):
            at = 1 + inside(4, t, steps) if t else 0
            cols = slice(t * TILE, (t + 1) * TILE)
            z = zs[at, 0:HB, :]
            xs[0 : part * RP, cols], xs[HB : HB + part * RP, cols] = split(z[: part * RP])
            last[:, cols] = z[part * RP :]
        for j in range(lines):
            at = rank[:, j * SUB : (j + 1) * SUB]
            total = jnp.zeros((SWAPPED * RP, SUB), f32)
            for h in range(lines):
                x = lanes(last[:, h * SUB : (h + 1) * SUB], at & (SUB - 1))
                total = jnp.where((at >> (SUB.bit_length() - 1)) == h, x, total)
            for c in range(SWAPPED):
                out[part + c, :, j * SUB : (j + 1) * SUB] = total[c * RP : c * RP + NP]
        x = jnp.concatenate([xs[0 : part * RP, :], xs[HB : HB + part * RP, :]], axis=0)
        y = dot(x, pm[...])
        for c in range(part):
            at = c * RP
            out[c] = y[at : at + NP] + y[part * RP + at : part * RP + at + NP]


def shards(*args):
    (fields, metric, scale, angles, nb, send_dom, send_part, kind, deriv, lift, binv) = args
    el = fields.shape[2]
    kinds = binv.shape[0]
    nt, lines = el // TILE, el // SUB
    steps = nt - 1 + kinds - 1
    small, large = constants(el, kinds)
    near = [
        scale, angles, nb, send_dom, send_part.reshape(1, -1), kind.reshape(1, -1), deriv, lift,
        *small,
    ]
    far = [fields, metric, binv, *large]
    vmem, dma = pltpu.VMEM, pltpu.SemaphoreType.DMA
    return pl.pallas_call(
        functools.partial(kernel, el, kinds),
        out_shape=pltpu.VMEM(fields.shape, f32),
        in_specs=[pl.BlockSpec(memory_space=vmem)] * len(near)
        + [pl.BlockSpec(memory_space=pl.ANY)] * len(far),
        out_specs=pl.BlockSpec(memory_space=vmem),
        scratch_shapes=[
            *[vmem(a.shape, a.dtype) for a in far],
            vmem((HB, el), f32),
            vmem((32, el), f32),
            vmem((2 * HB + 64, el), bf16),
            vmem((8, 3 * SUB), f32),
            vmem((4, el), i32),
            vmem((4, el), f32),
            vmem((1, el), i32),
            vmem(((kinds + 1) * lines, SUB), i32),
            vmem((lines, SUB), i32),
            vmem((el, el), bf16),
            vmem((TILE, 4 * el), bf16),
            vmem((4 * nt * 8, 2 * TILE), bf16),
            vmem((4 * nt * 2 * FP, 2 * TILE), bf16),
            vmem((4, 8, el), f32),
            vmem((4, 8, el), f32),
            vmem((3 * RP, 3 * RP), f32),
            vmem((4 * RP, 16 * FP), f32),
            vmem((nt, TR, TILE), f32),
            vmem((4, 2 * FP, el), f32),
            vmem((4, 2 * FP, el), f32),
            vmem((3, 2 * FP, SUB), f32),
            vmem((3, 8, SUB), f32),
            vmem((kinds, TR, 2 * KB), bf16),
            vmem((kinds, HB, 2 * KB), bf16),
            vmem((nt, 2 * KB, TILE), bf16),
            vmem((1 + steps, TR, TILE), f32),
            vmem((nt, 4, 2 * FP, TILE), f32),
            vmem((1, el), i32),
            vmem((SWAPPED * RP, el), f32),
            vmem((NC, 3 * RP, el), f32),
            vmem((3, MSG, SUB), f32),
            vmem((3, MSG, SUB), f32),
            vmem((SWEEPS - 1, 2, 2 * FP, SUB), f32),
            vmem((SWEEPS - 1, 2, 2 * FP, SUB), f32),
            pltpu.SMEM((kinds + 1,), i32),
            pltpu.SMEM((5, max(steps, nt)), i32),
            dma((len(far),)), dma((3,)), dma((3,)), dma((SWEEPS - 1, 2)), dma((SWEEPS - 1, 2)),
        ],
        compiler_params=pltpu.CompilerParams(
            collective_id=0, has_side_effects=True, vmem_limit_bytes=56 * 2**20
        ),
    )(*near, *far)


def solution(mesh):
    both = ("group", "dom")
    in_specs = (
        P(None, None, both), P(None, both), P(None, both), P(None, None, both), P(None, both),
        P(None, both), P(both), P(both), P(), P(), P(),
    )
    return jax.shard_map(
        shards, mesh=mesh, in_specs=in_specs, out_specs=P(None, None, both), check_vma=False
    )
```

```python
import functools

import jax
import jax.numpy as jnp
import numpy as np
from jax import lax
from jax.experimental import pallas as pl
from jax.experimental.pallas import tpu as pltpu
from jax.sharding import PartitionSpec as P

SWEEPS = 4
STEP = 0.2
NC, NP, NFP = 6, 35, 15
RP = 40
HB = NC * RP
KB = 256
FP = 16
TR = NC * 4 * FP
TILE = 256
SUB = 128
DIRECT = 1
EXTRA = 2
SWAPPED = 2
MSG = NC * FP + 8
f32, bf16, i32 = jnp.float32, jnp.bfloat16, jnp.int32


def face_nodes():
    lattice = [(r, s, t) for r in range(5) for s in range(5 - r) for t in range(5 - r - s)]
    tests = [
        lambda p: p[2] == 0,
        lambda p: p[1] == 0,
        lambda p: p[0] == 0,
        lambda p: sum(p) == 4,
    ]
    return [[i for i, p in enumerate(lattice) if test(p)] for test in tests]


def constants(el, kinds):
    trace = np.zeros((4 * FP, NP), np.float32)
    for f, nodes in enumerate(face_nodes()):
        for n, node in enumerate(nodes):
            trace[f * FP + n, node] = 1
    eye6 = np.eye(NC, dtype=np.float32)
    pad = np.eye(RP, NP, dtype=np.float32)
    trace6 = np.kron(eye6, trace)
    rows6 = np.kron(eye6, pad)
    cols6 = np.zeros((NC * NP, KB), np.float32)
    cols6[:, :HB] = rows6.T
    tracep = trace6 @ cols6
    spread = np.zeros((2, NP, 3 * RP), np.float32)
    for i in range(NP):
        spread[0, i, i] = spread[0, i, RP + i] = spread[1, i, 2 * RP + i] = 1
    lift_spread = np.zeros((4, 4 * NFP, 16 * FP), np.float32)
    for f in range(4):
        for n in range(NFP):
            row, col = f * NFP + n, f * FP + n
            for i in range(2):
                lift_spread[2 * i, row, 8 * FP * i + col] = 1
                lift_spread[2 * i, row, 8 * FP * i + 4 * FP + col] = 1
                lift_spread[2 * i + 1, row, 8 * FP * i + col] = 1
    upper = np.concatenate([np.triu(np.ones((SUB, SUB)), 1), np.ones((SUB, SUB))], axis=1)
    lines = (kinds + 1) * (el // SUB)
    lower = np.tril(np.ones((lines, lines)), -1)
    small = [jnp.asarray(a, bf16) for a in (upper, lower, spread, lift_spread)]
    large = [jnp.asarray(a, bf16) for a in (tracep, rows6, cols6)]
    return small, large


def split(x):
    hi = x.astype(bf16)
    return hi, (x - hi.astype(f32)).astype(bf16)


def dot(a, b):
    return jnp.dot(a, b, preferred_element_type=f32)


def stacked(x):
    hi, lo = split(x)
    gap = jnp.zeros((KB - HB, x.shape[1]), bf16)
    return jnp.concatenate([hi, gap, lo, gap], axis=0)


def project(at, n):
    sa, ca, sb, cb = n
    e_t = ca * (cb * at[0] + sb * at[1]) - sa * at[2]
    e_p = cb * at[1] - sb * at[0]
    h_t = ca * (cb * at[3] + sb * at[4]) - sa * at[5]
    h_p = cb * at[4] - sb * at[3]
    return jnp.concatenate([h_p - e_t, -h_t - e_p], axis=0)


def lanes(x, index):
    return jnp.take_along_axis(x, jnp.broadcast_to(index, x.shape), axis=1)


def kernel(
    el, kinds, scale, angles, nb, send_dom, send_part, kind, deriv, lift,
    upper, lower, spread, lift_spread,
    fields_h, metric_h, binv_h, tracep_h, rows6_h, cols6_h,
    out,
    fraw, metric, binv, tracep, rows6, cols6,
    fpad, own, xs, lnorm, slots, sgn, kindrow, offs, lsl, pm, sel, pooln, pool, recvn, pc, coef,
    d3, l2, trs, ext, base, rem, remn, wt, wf, rhs, zs, pqs, rank, last, grads,
    send0, recv0, sendk, recvk, off, walk,
    in_sem, ssem0, rsem0, ssemk, rsemk,
):
    grp, dom = lax.axis_index("group"), lax.axis_index("dom")
    count = lax.axis_size("dom")
    half = count // 2
    fine = jnp.logical_and(grp == 1, dom >= half)
    coarse = jnp.logical_not(fine)
    nt = el // TILE
    shift = el.bit_length() - 1
    lines = el // SUB
    steps = nt - 1 + kinds - 1
    has_prev, has_next = dom > 0, dom < count - 1
    fine_prev = jnp.logical_and(fine, dom > half)
    fine_next = jnp.logical_and(fine, has_next)

    loads = [
        pltpu.make_async_copy(a, b, in_sem.at[i])
        for i, (a, b) in enumerate((
            (fields_h, fraw), (tracep_h, tracep), (cols6_h, cols6), (binv_h, binv),
            (rows6_h, rows6), (metric_h, metric),
        ))
    ]
    for load in loads:
        load.start()

    barrier = pltpu.get_barrier_semaphore()

    @pl.when(has_prev)
    def _():
        pl.semaphore_signal(barrier, inc=1, device_id={"dom": dom - 1})

    @pl.when(has_next)
    def _():
        pl.semaphore_signal(barrier, inc=1, device_id={"dom": dom + 1})

    pl.semaphore_signal(barrier, inc=1, device_id={"group": 1 - grp})

    targets = ({"dom": dom - 1}, {"dom": dom + 1}, {"group": 1 - grp})
    lands = (1, 0, 2)
    first = [
        pltpu.make_async_remote_copy(
            src_ref=send0.at[i], dst_ref=recv0.at[lands[i]],
            send_sem=ssem0.at[i], recv_sem=rsem0.at[lands[i]], device_id=targets[i],
        )
        for i in range(3)
    ]

    def later(no):
        return [
            pltpu.make_async_remote_copy(
                src_ref=sendk.at[no - 1, i], dst_ref=recvk.at[no - 1, lands[i]],
                send_sem=ssemk.at[no - 1, i], recv_sem=rsemk.at[no - 1, lands[i]],
                device_id=targets[i],
            )
            for i in range(2)
        ]

    polar, azimuth = angles[0], angles[1]
    parts = (jnp.sin(polar), jnp.cos(polar), jnp.sin(azimuth), jnp.cos(azimuth))
    own[...] = jnp.zeros_like(own)
    for f in range(4):
        for i in range(4):
            own[f * 8 + i : f * 8 + i + 1, :] = parts[i][f : f + 1, :]
        own[f * 8 + 4 : f * 8 + 5, :] = 0.5 * scale[f : f + 1, :]
    lists = jnp.concatenate([send_dom[0:1, :], send_dom[1:2, :], send_part[...]], axis=1)
    @pl.when(fine)
    def _():
        def square(row):
            return jnp.concatenate([row[:, i * SUB : (i + 1) * SUB] for i in range(lines)], axis=0)

        def line(sq):
            return jnp.concatenate([sq[i : i + 1] for i in range(lines)], axis=1)

        faces = [square(nb[f : f + 1, :]) for f in range(4)]
        which = square(kind[...])
        edge = functools.reduce(
            jnp.logical_or,
            [jnp.logical_and(n >= 4 * el, n < 4 * el + 2 * SUB) for n in faces],
        )
        group = jnp.where(edge, 0, which)
        masks = jnp.concatenate(
            [jnp.where(group == k, 1.0, 0.0) for k in range(kinds + 1)], axis=0
        )
        pre = dot(masks.astype(bf16), upper[...])
        before = dot(lower[...], pre[:, SUB:].astype(bf16))
        ranks = masks * (pre[:, :SUB] + before)
        pos = sum(ranks[k * lines : (k + 1) * lines] for k in range(kinds + 1))
        offs[...] = before.astype(i32)
        for k in range(kinds):
            off[k] = offs[(k + 1) * lines, 0]
        off[kinds] = jnp.int32(el)
        t, k = jnp.int32(1), jnp.int32(1)
        seen = [jnp.int32(-1)] * nt
        for s in range(steps):
            lo, hi = off[k - 1], off[k]
            walk[0, s] = t
            walk[1, s] = k - 1
            walk[2, s] = lo - t * TILE
            walk[3, s] = hi - t * TILE
            seen = [n + jnp.where(t <= i, 1, 0) for i, n in enumerate(seen)]
            stay = jnp.logical_and(hi <= (t + 1) * TILE, k < kinds)
            k, t = jnp.where(stay, k + 1, k), jnp.where(stay, t, jnp.minimum(t + 1, nt - 1))
        for i in range(nt):
            walk[4, i] = jnp.clip(seen[i], 0, steps - 1)

        def lookup(e):
            lane, row = e & (SUB - 1), e >> (SUB.bit_length() - 1)
            res = jnp.zeros((lines, SUB), f32)
            for r in range(lines):
                table = jnp.broadcast_to(pos[r : r + 1], (lines, SUB))
                res = jnp.where(row == r, jnp.take_along_axis(table, lane, axis=1), res)
            return res.astype(i32)

        place = pos.astype(i32)
        for f in range(4):
            n = faces[f]
            inner = (n >> shift) * el + lookup(n & (el - 1))
            m = jnp.where(n < 0, f * el + place, jnp.where(n >= 4 * el, n, inner))
            flag = 2 * which + jnp.where(n < 0, 1, 0)
            for i, v in enumerate((m >> 6, m & 63, flag)):
                own[f * 8 + 5 + i : f * 8 + 6 + i, :] = line(v.astype(f32))
        mine = jnp.concatenate([send_dom[...]] * (lines // 2), axis=0)
        lsl[...] = (mine >> shift) * TILE + lookup(mine & (el - 1))

        row = line(place)
        rank[...] = row
        for i in range(nt):
            down = lax.broadcasted_iota(i32, (TILE, el), 0) + i * TILE
            pm[i * TILE : (i + 1) * TILE, :] = jnp.where(down == row, 1.0, 0.0).astype(bf16)

    loads[0].wait()
    for c in range(NC):
        fpad[c * RP + 32 : (c + 1) * RP, :] = jnp.zeros((8, el), f32)
        fpad[c * RP : c * RP + NP, :] = fraw[c]
    for load in loads[1:]:
        load.wait()

    def listed(source):
        parts = []
        for i in range(3):
            at = lists[:, i * SUB : (i + 1) * SUB] & (el - 1)
            v = jnp.zeros((source.shape[0], SUB), f32)
            for h in range(lines):
                x = lanes(source[:, h * SUB : (h + 1) * SUB], at & (SUB - 1))
                v = jnp.where((at >> (SUB.bit_length() - 1)) == h, x, v)
            parts.append(v)
        return jnp.concatenate(parts, axis=1)

    at_list = listed(own)
    for k in range(kinds):
        b2 = dot(binv[k], cols6[...]).astype(bf16)
        b = dot(rows6[...], b2).astype(bf16)
        a = dot(tracep[:, 0:HB], b).astype(bf16)
        for i in range(2):
            wt[k, :, i * KB : (i + 1) * KB] = a
            wf[k, :, i * KB : (i + 1) * KB] = b
    face = lists >> shift
    mine = at_list[0:8]
    for f in range(1, 4):
        mine = jnp.where(face == f, at_list[f * 8 : (f + 1) * 8], mine)
    lnorm[...] = mine
    t = dot(jnp.concatenate([tracep[...]] * 2, axis=1), stacked(listed(fpad)))
    for c in range(NC):
        v = t[c * 4 * FP : c * 4 * FP + FP]
        for f in range(1, 4):
            v = jnp.where(face == f, t[(c * 4 + f) * FP : (c * 4 + f + 1) * FP], v)
        for i in range(3):
            send0[i, c * FP : (c + 1) * FP, :] = v[:, i * SUB : (i + 1) * SUB]
    for i in range(3):
        send0[i, NC * FP : MSG, :] = mine[:, i * SUB : (i + 1) * SUB]

    pl.semaphore_wait(barrier, 1 + has_prev.astype(i32) + has_next.astype(i32))

    @pl.when(has_prev)
    def _():
        first[0].start()

    @pl.when(has_next)
    def _():
        first[1].start()

    first[2].start()

    @pl.when(coarse)
    def _():
        for f in range(4):
            row = nb[f : f + 1, :]
            lane = lax.broadcasted_iota(i32, (1, el), 1)
            slots[f : f + 1, :] = jnp.where(row < 0, lane + f * el, row)
            sgn[f : f + 1, :] = jnp.where(row < 0, -1.0, 1.0)

    @pl.when(fine)
    def _():
        xs[0:HB, :], xs[HB : 2 * HB, :] = split(fpad[...])
        xs[2 * HB : 2 * HB + 32, :], xs[2 * HB + 32 : 2 * HB + 64, :] = split(own[...])
        y = lax.dot_general(
            xs[...], pm[...], (((1,), (1,)), ((), ())), preferred_element_type=f32
        )
        fpad[...] = y[0:HB] + y[HB : 2 * HB]
        own[...] = y[2 * HB : 2 * HB + 32] + y[2 * HB + 32 : 2 * HB + 64]
        for f in range(4):
            at = f * 8 + 5
            slots[f : f + 1, :] = (own[at : at + 1, :] * 64 + own[at + 1 : at + 2, :]).astype(i32)
            flag = own[at + 2 : at + 3, :].astype(i32)
            sgn[f : f + 1, :] = jnp.where((flag & 1) == 1, -1.0, 1.0)
            if f == 0:
                kindrow[...] = flag >> 1

    def pick(y, f, rows, total):
        which = slots[f : f + 1, 0 : total.shape[1]] >> (TILE.bit_length() - 1)
        for h in range(4 * nt):
            total = jnp.where(which == h, y[h * rows : (h + 1) * rows], total)
        return total

    def gather_direct(tiles, under, dest):
        for f in range(2, 4):
            for j in range(0 if f == 3 else lines - EXTRA, lines):
                cols = slice(j * SUB, (j + 1) * SUB)
                at = slots[f : f + 1, cols]
                total = jnp.zeros((2 * FP, SUB), f32) if under is None else under[f, :, cols]
                for t in tiles:
                    for g in range(4):
                        for i in range(TILE // SUB):
                            h = g * lines + t * (TILE // SUB) + i
                            x = lanes(pqs[t, g, :, i * SUB : (i + 1) * SUB], at & (SUB - 1))
                            total = jnp.where((at >> (SUB.bit_length() - 1)) == h, x, total)
                dest[f, :, cols] = total

    def gather(source, rows, dest, under=None, faces=4):
        for f in range(faces):
            n = el - EXTRA * SUB if f == 2 and faces < 4 else el
            s = sel[:, f * el : f * el + n]
            y = dot(source[...], jnp.concatenate([s, s], axis=0))
            total = jnp.zeros((rows, n), f32) if under is None else under[f, :, 0:n]
            dest[f, :, 0:n] = pick(y, f, rows, total)

    def place_at(dest, source, f, j, sources):
        s = slots[f : f + 1, j * SUB : (j + 1) * SUB]
        v = dest[f, :, j * SUB : (j + 1) * SUB]
        for i in sources:
            here = (s >> (SUB.bit_length() - 1)) == 4 * el // SUB + i
            v = jnp.where(here, lanes(source[i], s & (SUB - 1)), v)
        dest[f, :, j * SUB : (j + 1) * SUB] = v

    def weigh(cols):
        for f in range(4):
            sa, ca, sb, cb = (recvn[f, i : i + 1, cols] for i in range(4))
            sign = sgn[f : f + 1, cols]
            for i, row in enumerate((ca * cb, ca * sb, sa, cb, sb)):
                pc[f, i : i + 1, cols] = row
                pc[f, 8 + i : 9 + i, cols] = sign * row

    def fill(t, at_rows):
        cols = slice(t * TILE, (t + 1) * TILE)
        for f in range(4):
            at = [at_rows(c * 4 * FP + f * FP) for c in range(NC)]
            u, v, sa, cb, sb = (pc[f, i : i + 1, cols] for i in range(5))
            ue, ve, sae, cbe, sbe = (pc[f, 8 + i : 9 + i, cols] for i in range(5))
            p = cb * at[4] - sb * at[3] - ue * at[0] - ve * at[1] + sae * at[2]
            q = sa * at[5] - u * at[3] - v * at[4] - cbe * at[1] + sbe * at[0]
            pq = jnp.concatenate([p, q], axis=0)
            hi, lo = split(pq)
            h = f * nt + t
            pool[h * 2 * FP : (h + 1) * 2 * FP, 0:TILE] = hi
            pool[h * 2 * FP : (h + 1) * 2 * FP, TILE : 2 * TILE] = lo
            pqs[t, f] = pq

    down = lax.broadcasted_iota(i32, (TILE, el), 0)
    for f in range(4):
        low = slots[f : f + 1, :] & (TILE - 1)
        sel[:, f * el : (f + 1) * el] = jnp.where(down == low, 1.0, 0.0).astype(bf16)
    for f in range(4):
        for t in range(0, nt, 2):
            both = [own[f * 8 : f * 8 + 8, (t + i) * TILE : (t + i + 1) * TILE] for i in range(2)]
            h = (f * nt + t) * 8
            pooln[h : h + 16, 0:TILE], pooln[h : h + 16, TILE : 2 * TILE] = split(
                jnp.concatenate(both, axis=0)
            )
        sa, ca, sb, cb, w = (own[f * 8 + i : f * 8 + i + 1, :] for i in range(5))
        for i, row in enumerate((w * ca * cb, w * ca * sb, -w * sa, -w * sb, w * cb)):
            coef[f, i : i + 1, :] = row
    gather(pooln, 8, recvn, None, 1)
    for f in range(1, 4):
        for j in range(lines):
            cols = slice(j * SUB, (j + 1) * SUB)
            at = slots[f : f + 1, cols]
            total = jnp.zeros((8, SUB), f32)
            for h in range(4 * lines):
                g, i = h // lines, h % lines
                x = lanes(own[g * 8 : g * 8 + 8, i * SUB : (i + 1) * SUB], at & (SUB - 1))
                total = jnp.where((at >> (SUB.bit_length() - 1)) == h, x, total)
            recvn[f, :, cols] = total
    weigh(slice(0, el))
    for t in range(nt):
        z = dot(jnp.concatenate([tracep[...]] * 2, axis=1), stacked(fpad[:, t * TILE : (t + 1) * TILE]))
        trs[t] = z
        fill(t, lambda r: z[r : r + FP])
    gather_direct(range(nt), None, ext)
    gather(pool, 2 * FP, ext, None, 4 - DIRECT)

    l2[...] = jnp.zeros_like(l2)
    hi, lo = split(lift[...])
    for i in range(4):
        l2[i * RP : i * RP + NP, :] = dot(lo if i % 2 else hi, lift_spread[i])
    @pl.when(coarse)
    def _():
        d3[...] = jnp.zeros_like(d3)
        for b in range(3):
            hi, lo = split(deriv[b])
            d3[b * RP : b * RP + NP, :] = dot(hi, spread[0]) + dot(lo, spread[1])
        db = d3[...].astype(bf16)
        for c in range(NC):
            x = fpad[c * RP : (c + 1) * RP, :]
            hi = x.astype(bf16).astype(f32)
            grads[c] = dot(db, jnp.concatenate([hi, x - hi, hi], axis=0).astype(bf16))

    def arrive(i):
        at = [recv0[i, c * FP : (c + 1) * FP, :] for c in range(NC)]
        rem[i] = project(at, [lnorm[r : r + 1, i * SUB : (i + 1) * SUB] for r in range(4)])
        remn[i] = recv0[i, NC * FP : MSG, :]

    rem[...] = jnp.zeros_like(rem)
    remn[...] = jnp.zeros_like(remn)

    @pl.when(has_prev)
    def _():
        first[0].wait_send()
        first[1].wait_recv()
        arrive(0)

    @pl.when(has_next)
    def _():
        first[1].wait_send()
        first[0].wait_recv()
        arrive(1)

    first[2].wait()
    arrive(2)

    def lifted(t, pq):
        cols = slice(t * TILE, (t + 1) * TILE)
        for pair in range(NC // 2):
            pieces = []
            for c in (2 * pair, 2 * pair + 1):
                rows = []
                k = c % 3
                for f in range(4):
                    p, q = pq[f][:FP], pq[f][FP:]
                    a, b = (p, q) if c < 3 else (q, -p)
                    row = coef[f, k : k + 1, cols] * a
                    if k < 2:
                        row = row + coef[f, 3 + k : 4 + k, cols] * b
                    rows.append(row)
                pieces.extend(split(jnp.concatenate(rows, axis=0)))
            y = dot(l2[...].astype(bf16), jnp.concatenate(pieces, axis=0))
            for i in range(2):
                at = 2 * i * RP
                yield 2 * pair + i, y[at : at + RP] + y[at + RP : at + 2 * RP]

    @pl.when(coarse)
    def _():
        for f in range(4):
            for j in range(lines):
                place_at(ext, rem, f, j, range(3))
        for t in range(nt):
            cols = slice(t * TILE, (t + 1) * TILE)

            def along(c, axis):
                return sum(
                    metric[3 * axis + b : 3 * axis + b + 1, cols]
                    * grads[c, b * RP : (b + 1) * RP, cols]
                    for b in range(3)
                )

            pq = []
            for f in range(4):
                at = [trs[t, (c * 4 + f) * FP : (c * 4 + f + 1) * FP, :] for c in range(NC)]
                n = [own[f * 8 + i : f * 8 + i + 1, cols] for i in range(4)]
                pq.append(project(at, n) - ext[f, :, cols])
            for c, s in lifted(t, pq):
                k, other = c % 3, 3 - 3 * (c // 3)
                one, two = (k + 1) % 3, (k + 2) % 3
                curl = along(other + two, one) - along(other + one, two)
                vol = curl if c < 3 else -curl
                value = fpad[c * RP : (c + 1) * RP, cols] + STEP * (vol + s)
                out[c, :, cols] = value[:NP]

    @pl.when(fine)
    def _():
        for f in range(4):
            for j in range(lines):
                edge = j < TILE // SUB
                place_at(ext, rem, f, j, range(3) if edge else (2,))
                if edge:
                    place_at(recvn, remn, f, j, range(2))
            base[f] = jnp.where(slots[f : f + 1, :] >= 4 * el, ext[f], 0.0)
        weigh(slice(0, TILE))

        def right_side(t):
            cols = slice(t * TILE, (t + 1) * TILE)
            terms = [
                fpad[c * RP : (c + 1) * RP, cols] - STEP * s
                for c, s in lifted(t, [ext[f, :, cols] for f in range(4)])
            ]
            rhs[t] = stacked(jnp.concatenate(terms, axis=0))

        def edge_blocks(weights, rows):
            z = dot(weights[0], rhs[0])
            for k in range(1, kinds):
                z = jnp.where(kindrow[:, 0:TILE] == k + 1, dot(weights[k], rhs[0]), z)
            zs[0, 0:rows, :] = z

        def inside(row, at, size):
            return jnp.clip(walk[row, at], 0, size - 1)

        def inner_blocks(weights, rows):
            lane = lax.broadcasted_iota(i32, (1, TILE), 1)
            for s in range(steps):
                y = dot(weights[inside(1, s, kinds)], rhs[inside(0, s, nt)])
                if s:
                    here = jnp.logical_and(lane >= walk[2, s], lane < walk[3, s])
                    y = jnp.where(here, y, zs[s, 0:rows, :])
                zs[1 + s, 0:rows, :] = y

        def sweep(no, carry):
            right_side(0)
            edge_blocks(wt, TR)
            for t in range(1, nt):
                right_side(t)
            fill(0, lambda r: zs[0, r : r + FP, :])
            for i in range(2):
                at = lsl[i : i + 1, :]
                v = jnp.zeros((2 * FP, SUB), f32)
                for h in range(4 * TILE // SUB):
                    f, j = h // (TILE // SUB), h % (TILE // SUB)
                    x = lanes(pqs[0, f, :, j * SUB : (j + 1) * SUB], at & (SUB - 1))
                    v = jnp.where((at >> (SUB.bit_length() - 1)) == h, x, v)
                sendk[no - 1, i] = v
            copies = later(no)

            @pl.when(fine_prev)
            def _():
                copies[0].start()

            @pl.when(fine_next)
            def _():
                copies[1].start()

            inner_blocks(wt, TR)
            for t in range(1, nt):
                end = inside(4, t, steps)
                fill(t, lambda r: zs[1 + end, r : r + FP, :])
            gather_direct(range(nt), base, ext)
            gather(pool, 2 * FP, ext, base, 4 - DIRECT)

            @pl.when(fine_prev)
            def _():
                copies[0].wait_send()
                copies[1].wait_recv()
                rem[0] = recvk[no - 1, 0]

            @pl.when(fine_next)
            def _():
                copies[1].wait_send()
                copies[0].wait_recv()
                rem[1] = recvk[no - 1, 1]

            for f in range(4):
                for j in range(TILE // SUB):
                    place_at(ext, rem, f, j, range(2))
            return carry

        lax.fori_loop(1, SWEEPS, sweep, 0)
        for t in range(nt):
            right_side(t)
        edge_blocks(wf, HB)
        inner_blocks(wf, HB)
        part = NC - SWAPPED
        for t in range(nt):
            at = 1 + inside(4, t, steps) if t else 0
            cols = slice(t * TILE, (t + 1) * TILE)
            z = zs[at, 0:HB, :]
            xs[0 : part * RP, cols], xs[HB : HB + part * RP, cols] = split(z[: part * RP])
            last[:, cols] = z[part * RP :]
        for j in range(lines):
            at = rank[:, j * SUB : (j + 1) * SUB]
            total = jnp.zeros((SWAPPED * RP, SUB), f32)
            for h in range(lines):
                x = lanes(last[:, h * SUB : (h + 1) * SUB], at & (SUB - 1))
                total = jnp.where((at >> (SUB.bit_length() - 1)) == h, x, total)
            for c in range(SWAPPED):
                out[part + c, :, j * SUB : (j + 1) * SUB] = total[c * RP : c * RP + NP]
        x = jnp.concatenate([xs[0 : part * RP, :], xs[HB : HB + part * RP, :]], axis=0)
        y = dot(x, pm[...])
        for c in range(part):
            at = c * RP
            out[c] = y[at : at + NP] + y[part * RP + at : part * RP + at + NP]


def shards(*args):
    (fields, metric, scale, angles, nb, send_dom, send_part, kind, deriv, lift, binv) = args
    el = fields.shape[2]
    kinds = binv.shape[0]
    nt, lines = el // TILE, el // SUB
    steps = nt - 1 + kinds - 1
    small, large = constants(el, kinds)
    near = [
        scale, angles, nb, send_dom, send_part.reshape(1, -1), kind.reshape(1, -1), deriv, lift,
        *small,
    ]
    far = [fields, metric, binv, *large]
    vmem, dma = pltpu.VMEM, pltpu.SemaphoreType.DMA
    return pl.pallas_call(
        functools.partial(kernel, el, kinds),
        out_shape=pltpu.VMEM(fields.shape, f32),
        in_specs=[pl.BlockSpec(memory_space=vmem)] * len(near)
        + [pl.BlockSpec(memory_space=pl.ANY)] * len(far),
        out_specs=pl.BlockSpec(memory_space=vmem),
        scratch_shapes=[
            *[vmem(a.shape, a.dtype) for a in far],
            vmem((HB, el), f32),
            vmem((32, el), f32),
            vmem((2 * HB + 64, el), bf16),
            vmem((8, 3 * SUB), f32),
            vmem((4, el), i32),
            vmem((4, el), f32),
            vmem((1, el), i32),
            vmem(((kinds + 1) * lines, SUB), i32),
            vmem((lines, SUB), i32),
            vmem((el, el), bf16),
            vmem((TILE, 4 * el), bf16),
            vmem((4 * nt * 8, 2 * TILE), bf16),
            vmem((4 * nt * 2 * FP, 2 * TILE), bf16),
            vmem((4, 8, el), f32),
            vmem((4, 16, el), f32),
            vmem((4, 8, el), f32),
            vmem((3 * RP, 3 * RP), f32),
            vmem((4 * RP, 16 * FP), f32),
            vmem((nt, TR, TILE), f32),
            vmem((4, 2 * FP, el), f32),
            vmem((4, 2 * FP, el), f32),
            vmem((3, 2 * FP, SUB), f32),
            vmem((3, 8, SUB), f32),
            vmem((kinds, TR, 2 * KB), bf16),
            vmem((kinds, HB, 2 * KB), bf16),
            vmem((nt, 2 * KB, TILE), bf16),
            vmem((1 + steps, TR, TILE), f32),
            vmem((nt, 4, 2 * FP, TILE), f32),
            vmem((1, el), i32),
            vmem((SWAPPED * RP, el), f32),
            vmem((NC, 3 * RP, el), f32),
            vmem((3, MSG, SUB), f32),
            vmem((3, MSG, SUB), f32),
            vmem((SWEEPS - 1, 2, 2 * FP, SUB), f32),
            vmem((SWEEPS - 1, 2, 2 * FP, SUB), f32),
            pltpu.SMEM((kinds + 1,), i32),
            pltpu.SMEM((5, max(steps, nt)), i32),
            dma((len(far),)), dma((3,)), dma((3,)), dma((SWEEPS - 1, 2)), dma((SWEEPS - 1, 2)),
        ],
        compiler_params=pltpu.CompilerParams(
            collective_id=0, has_side_effects=True, vmem_limit_bytes=56 * 2**20
        ),
    )(*near, *far)


def solution(mesh):
    both = ("group", "dom")
    in_specs = (
        P(None, None, both), P(None, both), P(None, both), P(None, None, both), P(None, both),
        P(None, both), P(both), P(both), P(), P(), P(),
    )
    return jax.shard_map(
        shards, mesh=mesh, in_specs=in_specs, out_specs=P(None, None, both), check_vma=False
    )
```

```python
import functools

import jax
import jax.numpy as jnp
import numpy as np
from jax import lax
from jax.experimental import pallas as pl
from jax.experimental.pallas import tpu as pltpu
from jax.sharding import PartitionSpec as P

SWEEPS = 4
STEP = 0.2
NC, NP, NFP = 6, 35, 15
RP = 40
HB = NC * RP
KB = 256
FP = 16
TR = NC * 4 * FP
TILE = 256
SUB = 128
DIRECT = 1
EXTRA = 3
SWAPPED = 2
MSG = NC * FP + 8
f32, bf16, i32 = jnp.float32, jnp.bfloat16, jnp.int32


def face_nodes():
    lattice = [(r, s, t) for r in range(5) for s in range(5 - r) for t in range(5 - r - s)]
    tests = [
        lambda p: p[2] == 0,
        lambda p: p[1] == 0,
        lambda p: p[0] == 0,
        lambda p: sum(p) == 4,
    ]
    return [[i for i, p in enumerate(lattice) if test(p)] for test in tests]


def constants(el, kinds):
    trace = np.zeros((4 * FP, NP), np.float32)
    for f, nodes in enumerate(face_nodes()):
        for n, node in enumerate(nodes):
            trace[f * FP + n, node] = 1
    eye6 = np.eye(NC, dtype=np.float32)
    pad = np.eye(RP, NP, dtype=np.float32)
    trace6 = np.kron(eye6, trace)
    rows6 = np.kron(eye6, pad)
    cols6 = np.zeros((NC * NP, KB), np.float32)
    cols6[:, :HB] = rows6.T
    tracep = trace6 @ cols6
    spread = np.zeros((2, NP, 3 * RP), np.float32)
    for i in range(NP):
        spread[0, i, i] = spread[0, i, RP + i] = spread[1, i, 2 * RP + i] = 1
    lift_spread = np.zeros((4, 4 * NFP, 16 * FP), np.float32)
    for f in range(4):
        for n in range(NFP):
            row, col = f * NFP + n, f * FP + n
            for i in range(2):
                lift_spread[2 * i, row, 8 * FP * i + col] = 1
                lift_spread[2 * i, row, 8 * FP * i + 4 * FP + col] = 1
                lift_spread[2 * i + 1, row, 8 * FP * i + col] = 1
    upper = np.concatenate([np.triu(np.ones((SUB, SUB)), 1), np.ones((SUB, SUB))], axis=1)
    lines = (kinds + 1) * (el // SUB)
    lower = np.tril(np.ones((lines, lines)), -1)
    small = [jnp.asarray(a, bf16) for a in (upper, lower, spread, lift_spread)]
    large = [jnp.asarray(a, bf16) for a in (tracep, rows6, cols6)]
    return small, large


def split(x):
    hi = x.astype(bf16)
    return hi, (x - hi.astype(f32)).astype(bf16)


def dot(a, b):
    return jnp.dot(a, b, preferred_element_type=f32)


def stacked(x):
    hi, lo = split(x)
    gap = jnp.zeros((KB - HB, x.shape[1]), bf16)
    return jnp.concatenate([hi, gap, lo, gap], axis=0)


def project(at, n):
    sa, ca, sb, cb = n
    e_t = ca * (cb * at[0] + sb * at[1]) - sa * at[2]
    e_p = cb * at[1] - sb * at[0]
    h_t = ca * (cb * at[3] + sb * at[4]) - sa * at[5]
    h_p = cb * at[4] - sb * at[3]
    return jnp.concatenate([h_p - e_t, -h_t - e_p], axis=0)


def lanes(x, index):
    return jnp.take_along_axis(x, jnp.broadcast_to(index, x.shape), axis=1)


def kernel(
    el, kinds, scale, angles, nb, send_dom, send_part, kind, deriv, lift,
    upper, lower, spread, lift_spread,
    fields_h, metric_h, binv_h, tracep_h, rows6_h, cols6_h,
    out,
    fraw, metric, binv, tracep, rows6, cols6,
    fpad, own, xs, lnorm, slots, sgn, kindrow, offs, lsl, pm, sel, pooln, pool, recvn, pc, coef,
    d3, l2, trs, ext, base, rem, remn, wt, wf, rhs, zs, pqs, rank, last, grads,
    send0, recv0, sendk, recvk, off, walk,
    in_sem, ssem0, rsem0, ssemk, rsemk,
):
    grp, dom = lax.axis_index("group"), lax.axis_index("dom")
    count = lax.axis_size("dom")
    half = count // 2
    fine = jnp.logical_and(grp == 1, dom >= half)
    coarse = jnp.logical_not(fine)
    nt = el // TILE
    shift = el.bit_length() - 1
    lines = el // SUB
    steps = nt - 1 + kinds - 1
    has_prev, has_next = dom > 0, dom < count - 1
    fine_prev = jnp.logical_and(fine, dom > half)
    fine_next = jnp.logical_and(fine, has_next)

    loads = [
        pltpu.make_async_copy(a, b, in_sem.at[i])
        for i, (a, b) in enumerate((
            (fields_h, fraw), (tracep_h, tracep), (cols6_h, cols6), (binv_h, binv),
            (rows6_h, rows6), (metric_h, metric),
        ))
    ]
    for load in loads:
        load.start()

    barrier = pltpu.get_barrier_semaphore()

    @pl.when(has_prev)
    def _():
        pl.semaphore_signal(barrier, inc=1, device_id={"dom": dom - 1})

    @pl.when(has_next)
    def _():
        pl.semaphore_signal(barrier, inc=1, device_id={"dom": dom + 1})

    pl.semaphore_signal(barrier, inc=1, device_id={"group": 1 - grp})

    targets = ({"dom": dom - 1}, {"dom": dom + 1}, {"group": 1 - grp})
    lands = (1, 0, 2)
    first = [
        pltpu.make_async_remote_copy(
            src_ref=send0.at[i], dst_ref=recv0.at[lands[i]],
            send_sem=ssem0.at[i], recv_sem=rsem0.at[lands[i]], device_id=targets[i],
        )
        for i in range(3)
    ]

    def later(no):
        return [
            pltpu.make_async_remote_copy(
                src_ref=sendk.at[no - 1, i], dst_ref=recvk.at[no - 1, lands[i]],
                send_sem=ssemk.at[no - 1, i], recv_sem=rsemk.at[no - 1, lands[i]],
                device_id=targets[i],
            )
            for i in range(2)
        ]

    polar, azimuth = angles[0], angles[1]
    parts = (jnp.sin(polar), jnp.cos(polar), jnp.sin(azimuth), jnp.cos(azimuth))
    own[...] = jnp.zeros_like(own)
    for f in range(4):
        for i in range(4):
            own[f * 8 + i : f * 8 + i + 1, :] = parts[i][f : f + 1, :]
        own[f * 8 + 4 : f * 8 + 5, :] = 0.5 * scale[f : f + 1, :]
    lists = jnp.concatenate([send_dom[0:1, :], send_dom[1:2, :], send_part[...]], axis=1)
    @pl.when(fine)
    def _():
        def square(row):
            return jnp.concatenate([row[:, i * SUB : (i + 1) * SUB] for i in range(lines)], axis=0)

        def line(sq):
            return jnp.concatenate([sq[i : i + 1] for i in range(lines)], axis=1)

        faces = [square(nb[f : f + 1, :]) for f in range(4)]
        which = square(kind[...])
        edge = functools.reduce(
            jnp.logical_or,
            [jnp.logical_and(n >= 4 * el, n < 4 * el + 2 * SUB) for n in faces],
        )
        group = jnp.where(edge, 0, which)
        masks = jnp.concatenate(
            [jnp.where(group == k, 1.0, 0.0) for k in range(kinds + 1)], axis=0
        )
        pre = dot(masks.astype(bf16), upper[...])
        before = dot(lower[...], pre[:, SUB:].astype(bf16))
        ranks = masks * (pre[:, :SUB] + before)
        pos = sum(ranks[k * lines : (k + 1) * lines] for k in range(kinds + 1))
        offs[...] = before.astype(i32)
        for k in range(kinds):
            off[k] = offs[(k + 1) * lines, 0]
        off[kinds] = jnp.int32(el)
        t, k = jnp.int32(1), jnp.int32(1)
        seen = [jnp.int32(-1)] * nt
        for s in range(steps):
            lo, hi = off[k - 1], off[k]
            walk[0, s] = t
            walk[1, s] = k - 1
            walk[2, s] = lo - t * TILE
            walk[3, s] = hi - t * TILE
            seen = [n + jnp.where(t <= i, 1, 0) for i, n in enumerate(seen)]
            stay = jnp.logical_and(hi <= (t + 1) * TILE, k < kinds)
            k, t = jnp.where(stay, k + 1, k), jnp.where(stay, t, jnp.minimum(t + 1, nt - 1))
        for i in range(nt):
            walk[4, i] = jnp.clip(seen[i], 0, steps - 1)

        def lookup(e):
            lane, row = e & (SUB - 1), e >> (SUB.bit_length() - 1)
            res = jnp.zeros((lines, SUB), f32)
            for r in range(lines):
                table = jnp.broadcast_to(pos[r : r + 1], (lines, SUB))
                res = jnp.where(row == r, jnp.take_along_axis(table, lane, axis=1), res)
            return res.astype(i32)

        place = pos.astype(i32)
        for f in range(4):
            n = faces[f]
            inner = (n >> shift) * el + lookup(n & (el - 1))
            m = jnp.where(n < 0, f * el + place, jnp.where(n >= 4 * el, n, inner))
            flag = 2 * which + jnp.where(n < 0, 1, 0)
            for i, v in enumerate((m >> 6, m & 63, flag)):
                own[f * 8 + 5 + i : f * 8 + 6 + i, :] = line(v.astype(f32))
        mine = jnp.concatenate([send_dom[...]] * (lines // 2), axis=0)
        lsl[...] = (mine >> shift) * TILE + lookup(mine & (el - 1))

        row = line(place)
        rank[...] = row
        for i in range(nt):
            down = lax.broadcasted_iota(i32, (TILE, el), 0) + i * TILE
            pm[i * TILE : (i + 1) * TILE, :] = jnp.where(down == row, 1.0, 0.0).astype(bf16)

    loads[0].wait()
    for c in range(NC):
        fpad[c * RP + 32 : (c + 1) * RP, :] = jnp.zeros((8, el), f32)
        fpad[c * RP : c * RP + NP, :] = fraw[c]
    for load in loads[1:]:
        load.wait()

    def listed(source):
        parts = []
        for i in range(3):
            at = lists[:, i * SUB : (i + 1) * SUB] & (el - 1)
            v = jnp.zeros((source.shape[0], SUB), f32)
            for h in range(lines):
                x = lanes(source[:, h * SUB : (h + 1) * SUB], at & (SUB - 1))
                v = jnp.where((at >> (SUB.bit_length() - 1)) == h, x, v)
            parts.append(v)
        return jnp.concatenate(parts, axis=1)

    at_list = listed(own)
    for k in range(kinds):
        b2 = dot(binv[k], cols6[...]).astype(bf16)
        b = dot(rows6[...], b2).astype(bf16)
        a = dot(tracep[:, 0:HB], b).astype(bf16)
        for i in range(2):
            wt[k, :, i * KB : (i + 1) * KB] = a
            wf[k, :, i * KB : (i + 1) * KB] = b
    face = lists >> shift
    mine = at_list[0:8]
    for f in range(1, 4):
        mine = jnp.where(face == f, at_list[f * 8 : (f + 1) * 8], mine)
    lnorm[...] = mine
    t = dot(jnp.concatenate([tracep[...]] * 2, axis=1), stacked(listed(fpad)))
    for c in range(NC):
        v = t[c * 4 * FP : c * 4 * FP + FP]
        for f in range(1, 4):
            v = jnp.where(face == f, t[(c * 4 + f) * FP : (c * 4 + f + 1) * FP], v)
        for i in range(3):
            send0[i, c * FP : (c + 1) * FP, :] = v[:, i * SUB : (i + 1) * SUB]
    for i in range(3):
        send0[i, NC * FP : MSG, :] = mine[:, i * SUB : (i + 1) * SUB]

    pl.semaphore_wait(barrier, 1 + has_prev.astype(i32) + has_next.astype(i32))

    @pl.when(has_prev)
    def _():
        first[0].start()

    @pl.when(has_next)
    def _():
        first[1].start()

    first[2].start()

    @pl.when(coarse)
    def _():
        for f in range(4):
            row = nb[f : f + 1, :]
            lane = lax.broadcasted_iota(i32, (1, el), 1)
            slots[f : f + 1, :] = jnp.where(row < 0, lane + f * el, row)
            sgn[f : f + 1, :] = jnp.where(row < 0, -1.0, 1.0)

    @pl.when(fine)
    def _():
        xs[0:HB, :], xs[HB : 2 * HB, :] = split(fpad[...])
        xs[2 * HB : 2 * HB + 32, :], xs[2 * HB + 32 : 2 * HB + 64, :] = split(own[...])
        y = lax.dot_general(
            xs[...], pm[...], (((1,), (1,)), ((), ())), preferred_element_type=f32
        )
        fpad[...] = y[0:HB] + y[HB : 2 * HB]
        own[...] = y[2 * HB : 2 * HB + 32] + y[2 * HB + 32 : 2 * HB + 64]
        for f in range(4):
            at = f * 8 + 5
            slots[f : f + 1, :] = (own[at : at + 1, :] * 64 + own[at + 1 : at + 2, :]).astype(i32)
            flag = own[at + 2 : at + 3, :].astype(i32)
            sgn[f : f + 1, :] = jnp.where((flag & 1) == 1, -1.0, 1.0)
            if f == 0:
                kindrow[...] = flag >> 1

    def pick(y, f, rows, total):
        which = slots[f : f + 1, 0 : total.shape[1]] >> (TILE.bit_length() - 1)
        for h in range(4 * nt):
            total = jnp.where(which == h, y[h * rows : (h + 1) * rows], total)
        return total

    def gather_direct(tiles, under, dest):
        for f in range(2, 4):
            for j in range(0 if f == 3 else lines - EXTRA, lines):
                cols = slice(j * SUB, (j + 1) * SUB)
                at = slots[f : f + 1, cols]
                total = jnp.zeros((2 * FP, SUB), f32) if under is None else under[f, :, cols]
                for t in tiles:
                    for g in range(4):
                        for i in range(TILE // SUB):
                            h = g * lines + t * (TILE // SUB) + i
                            x = lanes(pqs[t, g, :, i * SUB : (i + 1) * SUB], at & (SUB - 1))
                            total = jnp.where((at >> (SUB.bit_length() - 1)) == h, x, total)
                dest[f, :, cols] = total

    def gather(source, rows, dest, under=None, faces=4):
        for f in range(faces):
            n = el - EXTRA * SUB if f == 2 and faces < 4 else el
            s = sel[:, f * el : f * el + n]
            y = dot(source[...], jnp.concatenate([s, s], axis=0))
            total = jnp.zeros((rows, n), f32) if under is None else under[f, :, 0:n]
            dest[f, :, 0:n] = pick(y, f, rows, total)

    def place_at(dest, source, f, j, sources):
        s = slots[f : f + 1, j * SUB : (j + 1) * SUB]
        v = dest[f, :, j * SUB : (j + 1) * SUB]
        for i in sources:
            here = (s >> (SUB.bit_length() - 1)) == 4 * el // SUB + i
            v = jnp.where(here, lanes(source[i], s & (SUB - 1)), v)
        dest[f, :, j * SUB : (j + 1) * SUB] = v

    def weigh(cols):
        for f in range(4):
            sa, ca, sb, cb = (recvn[f, i : i + 1, cols] for i in range(4))
            sign = sgn[f : f + 1, cols]
            for i, row in enumerate((ca * cb, ca * sb, sa, cb, sb)):
                pc[f, i : i + 1, cols] = row
                pc[f, 8 + i : 9 + i, cols] = sign * row

    def fill(t, at_rows):
        cols = slice(t * TILE, (t + 1) * TILE)
        for f in range(4):
            at = [at_rows(c * 4 * FP + f * FP) for c in range(NC)]
            u, v, sa, cb, sb = (pc[f, i : i + 1, cols] for i in range(5))
            ue, ve, sae, cbe, sbe = (pc[f, 8 + i : 9 + i, cols] for i in range(5))
            p = cb * at[4] - sb * at[3] - ue * at[0] - ve * at[1] + sae * at[2]
            q = sa * at[5] - u * at[3] - v * at[4] - cbe * at[1] + sbe * at[0]
            pq = jnp.concatenate([p, q], axis=0)
            hi, lo = split(pq)
            h = f * nt + t
            pool[h * 2 * FP : (h + 1) * 2 * FP, 0:TILE] = hi
            pool[h * 2 * FP : (h + 1) * 2 * FP, TILE : 2 * TILE] = lo
            pqs[t, f] = pq

    down = lax.broadcasted_iota(i32, (TILE, el), 0)
    for f in range(4):
        low = slots[f : f + 1, :] & (TILE - 1)
        sel[:, f * el : (f + 1) * el] = jnp.where(down == low, 1.0, 0.0).astype(bf16)
    for f in range(4):
        for t in range(0, nt, 2):
            both = [own[f * 8 : f * 8 + 8, (t + i) * TILE : (t + i + 1) * TILE] for i in range(2)]
            h = (f * nt + t) * 8
            pooln[h : h + 16, 0:TILE], pooln[h : h + 16, TILE : 2 * TILE] = split(
                jnp.concatenate(both, axis=0)
            )
        sa, ca, sb, cb, w = (own[f * 8 + i : f * 8 + i + 1, :] for i in range(5))
        for i, row in enumerate((w * ca * cb, w * ca * sb, -w * sa, -w * sb, w * cb)):
            coef[f, i : i + 1, :] = row
    gather(pooln, 8, recvn, None, 1)
    for f in range(1, 4):
        for j in range(lines):
            cols = slice(j * SUB, (j + 1) * SUB)
            at = slots[f : f + 1, cols]
            total = jnp.zeros((8, SUB), f32)
            for h in range(4 * lines):
                g, i = h // lines, h % lines
                x = lanes(own[g * 8 : g * 8 + 8, i * SUB : (i + 1) * SUB], at & (SUB - 1))
                total = jnp.where((at >> (SUB.bit_length() - 1)) == h, x, total)
            recvn[f, :, cols] = total
    weigh(slice(0, el))
    for t in range(nt):
        z = dot(jnp.concatenate([tracep[...]] * 2, axis=1), stacked(fpad[:, t * TILE : (t + 1) * TILE]))
        trs[t] = z
        fill(t, lambda r: z[r : r + FP])
    gather(pool, 2 * FP, ext, None, 4 - DIRECT)
    gather_direct(range(nt), None, ext)

    l2[...] = jnp.zeros_like(l2)
    hi, lo = split(lift[...])
    for i in range(4):
        l2[i * RP : i * RP + NP, :] = dot(lo if i % 2 else hi, lift_spread[i])
    @pl.when(coarse)
    def _():
        d3[...] = jnp.zeros_like(d3)
        for b in range(3):
            hi, lo = split(deriv[b])
            d3[b * RP : b * RP + NP, :] = dot(hi, spread[0]) + dot(lo, spread[1])
        db = d3[...].astype(bf16)
        for c in range(NC):
            x = fpad[c * RP : (c + 1) * RP, :]
            hi = x.astype(bf16).astype(f32)
            grads[c] = dot(db, jnp.concatenate([hi, x - hi, hi], axis=0).astype(bf16))

    def arrive(i):
        at = [recv0[i, c * FP : (c + 1) * FP, :] for c in range(NC)]
        rem[i] = project(at, [lnorm[r : r + 1, i * SUB : (i + 1) * SUB] for r in range(4)])
        remn[i] = recv0[i, NC * FP : MSG, :]

    rem[...] = jnp.zeros_like(rem)
    remn[...] = jnp.zeros_like(remn)

    @pl.when(has_prev)
    def _():
        first[0].wait_send()
        first[1].wait_recv()
        arrive(0)

    @pl.when(has_next)
    def _():
        first[1].wait_send()
        first[0].wait_recv()
        arrive(1)

    first[2].wait()
    arrive(2)

    def lifted(t, pq):
        cols = slice(t * TILE, (t + 1) * TILE)
        for pair in range(NC // 2):
            pieces = []
            for c in (2 * pair, 2 * pair + 1):
                rows = []
                k = c % 3
                for f in range(4):
                    p, q = pq[f][:FP], pq[f][FP:]
                    a, b = (p, q) if c < 3 else (q, -p)
                    row = coef[f, k : k + 1, cols] * a
                    if k < 2:
                        row = row + coef[f, 3 + k : 4 + k, cols] * b
                    rows.append(row)
                pieces.extend(split(jnp.concatenate(rows, axis=0)))
            y = dot(l2[...].astype(bf16), jnp.concatenate(pieces, axis=0))
            for i in range(2):
                at = 2 * i * RP
                yield 2 * pair + i, y[at : at + RP] + y[at + RP : at + 2 * RP]

    @pl.when(coarse)
    def _():
        for f in range(4):
            for j in range(lines):
                place_at(ext, rem, f, j, range(3))
        for t in range(nt):
            cols = slice(t * TILE, (t + 1) * TILE)

            def along(c, axis):
                return sum(
                    metric[3 * axis + b : 3 * axis + b + 1, cols]
                    * grads[c, b * RP : (b + 1) * RP, cols]
                    for b in range(3)
                )

            pq = []
            for f in range(4):
                at = [trs[t, (c * 4 + f) * FP : (c * 4 + f + 1) * FP, :] for c in range(NC)]
                n = [own[f * 8 + i : f * 8 + i + 1, cols] for i in range(4)]
                pq.append(project(at, n) - ext[f, :, cols])
            for c, s in lifted(t, pq):
                k, other = c % 3, 3 - 3 * (c // 3)
                one, two = (k + 1) % 3, (k + 2) % 3
                curl = along(other + two, one) - along(other + one, two)
                vol = curl if c < 3 else -curl
                value = fpad[c * RP : (c + 1) * RP, cols] + STEP * (vol + s)
                out[c, :, cols] = value[:NP]

    @pl.when(fine)
    def _():
        for f in range(4):
            for j in range(lines):
                edge = j < TILE // SUB
                place_at(ext, rem, f, j, range(3) if edge else (2,))
                if edge:
                    place_at(recvn, remn, f, j, range(2))
            base[f] = jnp.where(slots[f : f + 1, :] >= 4 * el, ext[f], 0.0)
        weigh(slice(0, TILE))

        def right_side(t):
            cols = slice(t * TILE, (t + 1) * TILE)
            terms = [
                fpad[c * RP : (c + 1) * RP, cols] - STEP * s
                for c, s in lifted(t, [ext[f, :, cols] for f in range(4)])
            ]
            rhs[t] = stacked(jnp.concatenate(terms, axis=0))

        def edge_blocks(weights, rows):
            z = dot(weights[0], rhs[0])
            for k in range(1, kinds):
                z = jnp.where(kindrow[:, 0:TILE] == k + 1, dot(weights[k], rhs[0]), z)
            zs[0, 0:rows, :] = z

        def inside(row, at, size):
            return jnp.clip(walk[row, at], 0, size - 1)

        def inner_blocks(weights, rows):
            lane = lax.broadcasted_iota(i32, (1, TILE), 1)
            for s in range(steps):
                y = dot(weights[inside(1, s, kinds)], rhs[inside(0, s, nt)])
                if s:
                    here = jnp.logical_and(lane >= walk[2, s], lane < walk[3, s])
                    y = jnp.where(here, y, zs[s, 0:rows, :])
                zs[1 + s, 0:rows, :] = y

        def sweep(no, carry):
            right_side(0)
            edge_blocks(wt, TR)
            for t in range(1, nt):
                right_side(t)
            fill(0, lambda r: zs[0, r : r + FP, :])
            for i in range(2):
                at = lsl[i : i + 1, :]
                v = jnp.zeros((2 * FP, SUB), f32)
                for h in range(4 * TILE // SUB):
                    f, j = h // (TILE // SUB), h % (TILE // SUB)
                    x = lanes(pqs[0, f, :, j * SUB : (j + 1) * SUB], at & (SUB - 1))
                    v = jnp.where((at >> (SUB.bit_length() - 1)) == h, x, v)
                sendk[no - 1, i] = v
            copies = later(no)

            @pl.when(fine_prev)
            def _():
                copies[0].start()

            @pl.when(fine_next)
            def _():
                copies[1].start()

            inner_blocks(wt, TR)
            for t in range(1, nt):
                end = inside(4, t, steps)
                fill(t, lambda r: zs[1 + end, r : r + FP, :])
            gather(pool, 2 * FP, ext, base, 4 - DIRECT)
            gather_direct(range(nt), base, ext)

            @pl.when(fine_prev)
            def _():
                copies[0].wait_send()
                copies[1].wait_recv()
                rem[0] = recvk[no - 1, 0]

            @pl.when(fine_next)
            def _():
                copies[1].wait_send()
                copies[0].wait_recv()
                rem[1] = recvk[no - 1, 1]

            for f in range(4):
                for j in range(TILE // SUB):
                    place_at(ext, rem, f, j, range(2))
            return carry

        lax.fori_loop(1, SWEEPS, sweep, 0)
        for t in range(nt):
            right_side(t)
        edge_blocks(wf, HB)
        inner_blocks(wf, HB)
        part = NC - SWAPPED
        for t in range(nt):
            at = 1 + inside(4, t, steps) if t else 0
            cols = slice(t * TILE, (t + 1) * TILE)
            z = zs[at, 0:HB, :]
            xs[0 : part * RP, cols], xs[HB : HB + part * RP, cols] = split(z[: part * RP])
            last[:, cols] = z[part * RP :]
        for j in range(lines):
            at = rank[:, j * SUB : (j + 1) * SUB]
            total = jnp.zeros((SWAPPED * RP, SUB), f32)
            for h in range(lines):
                x = lanes(last[:, h * SUB : (h + 1) * SUB], at & (SUB - 1))
                total = jnp.where((at >> (SUB.bit_length() - 1)) == h, x, total)
            for c in range(SWAPPED):
                out[part + c, :, j * SUB : (j + 1) * SUB] = total[c * RP : c * RP + NP]
        x = jnp.concatenate([xs[0 : part * RP, :], xs[HB : HB + part * RP, :]], axis=0)
        y = dot(x, pm[...])
        for c in range(part):
            at = c * RP
            out[c] = y[at : at + NP] + y[part * RP + at : part * RP + at + NP]


def shards(*args):
    (fields, metric, scale, angles, nb, send_dom, send_part, kind, deriv, lift, binv) = args
    el = fields.shape[2]
    kinds = binv.shape[0]
    nt, lines = el // TILE, el // SUB
    steps = nt - 1 + kinds - 1
    small, large = constants(el, kinds)
    near = [
        scale, angles, nb, send_dom, send_part.reshape(1, -1), kind.reshape(1, -1), deriv, lift,
        *small,
    ]
    far = [fields, metric, binv, *large]
    vmem, dma = pltpu.VMEM, pltpu.SemaphoreType.DMA
    return pl.pallas_call(
        functools.partial(kernel, el, kinds),
        out_shape=pltpu.VMEM(fields.shape, f32),
        in_specs=[pl.BlockSpec(memory_space=vmem)] * len(near)
        + [pl.BlockSpec(memory_space=pl.ANY)] * len(far),
        out_specs=pl.BlockSpec(memory_space=vmem),
        scratch_shapes=[
            *[vmem(a.shape, a.dtype) for a in far],
            vmem((HB, el), f32),
            vmem((32, el), f32),
            vmem((2 * HB + 64, el), bf16),
            vmem((8, 3 * SUB), f32),
            vmem((4, el), i32),
            vmem((4, el), f32),
            vmem((1, el), i32),
            vmem(((kinds + 1) * lines, SUB), i32),
            vmem((lines, SUB), i32),
            vmem((el, el), bf16),
            vmem((TILE, 4 * el), bf16),
            vmem((4 * nt * 8, 2 * TILE), bf16),
            vmem((4 * nt * 2 * FP, 2 * TILE), bf16),
            vmem((4, 8, el), f32),
            vmem((4, 16, el), f32),
            vmem((4, 8, el), f32),
            vmem((3 * RP, 3 * RP), f32),
            vmem((4 * RP, 16 * FP), f32),
            vmem((nt, TR, TILE), f32),
            vmem((4, 2 * FP, el), f32),
            vmem((4, 2 * FP, el), f32),
            vmem((3, 2 * FP, SUB), f32),
            vmem((3, 8, SUB), f32),
            vmem((kinds, TR, 2 * KB), bf16),
            vmem((kinds, HB, 2 * KB), bf16),
            vmem((nt, 2 * KB, TILE), bf16),
            vmem((1 + steps, TR, TILE), f32),
            vmem((nt, 4, 2 * FP, TILE), f32),
            vmem((1, el), i32),
            vmem((SWAPPED * RP, el), f32),
            vmem((NC, 3 * RP, el), f32),
            vmem((3, MSG, SUB), f32),
            vmem((3, MSG, SUB), f32),
            vmem((SWEEPS - 1, 2, 2 * FP, SUB), f32),
            vmem((SWEEPS - 1, 2, 2 * FP, SUB), f32),
            pltpu.SMEM((kinds + 1,), i32),
            pltpu.SMEM((5, max(steps, nt)), i32),
            dma((len(far),)), dma((3,)), dma((3,)), dma((SWEEPS - 1, 2)), dma((SWEEPS - 1, 2)),
        ],
        compiler_params=pltpu.CompilerParams(
            collective_id=0, has_side_effects=True, vmem_limit_bytes=56 * 2**20
        ),
    )(*near, *far)


def solution(mesh):
    both = ("group", "dom")
    in_specs = (
        P(None, None, both), P(None, both), P(None, both), P(None, None, both), P(None, both),
        P(None, both), P(both), P(both), P(), P(), P(),
    )
    return jax.shard_map(
        shards, mesh=mesh, in_specs=in_specs, out_specs=P(None, None, both), check_vma=False
    )
```
